32 devices in a mesh: rows: 8 (over z, y), seq: 4 (over x, core).
Axes of the slice: x: 2, y: 2, z: 4, core: 2. Of those that a mesh axis runs over, the one named last changes fastest.
Arguments:
- molecules: bfloat16 [64, 512, 768], P('rows', 'seq'), may hold values from -6 to 6
- ln1_gain: float32 [768], replicated, may hold values from 0.5 to 1.5
- ln1_bias: float32 [768], replicated, may hold values from -3 to 3
- w_qkv: bfloat16 [768, 2304], replicated, may hold values from -0.21875 to 0.21875
- qkv_bias: float32 [2, 768], replicated, may hold values from -3 to 3
- w_out: bfloat16 [768, 768], replicated, may hold values from -3 to 3
- out_bias: float32 [768], replicated, may hold values from -3 to 3
- ln2_gain: float32 [768], replicated, may hold values from 0.5 to 1.5
- ln2_bias: float32 [768], replicated, may hold values from -3 to 3
- w_up: bfloat16 [768, 3072], replicated, may hold values from -0.21875 to 0.21875
- up_bias: float32 [3072], replicated, may hold values from -3 to 3
- w_down: bfloat16 [3072, 768], replicated, may hold values from -0.109375 to 0.109375
- down_bias: float32 [768], replicated, may hold values from -3 to 3
- out_cotangent: bfloat16 [64, 512, 768], P('rows', 'seq'), may hold values from -6 to 6
- bucket_ids: int32 [8, 64, 2048], P(None, 'rows', 'seq'), may hold values from 0 to 16383
Outputs:
- layer_out: bfloat16 [64, 512, 768], P('rows', 'seq')
- grad_molecules: float32 [64, 512, 768], P('rows', 'seq')
- grad_ln1_gain: float32 [768], replicated
- grad_ln1_bias: float32 [768], replicated
- grad_w_qkv: float32 [768, 2304], replicated
- grad_qkv_bias: float32 [2, 768], replicated
- grad_w_out: float32 [768, 768], replicated
- grad_out_bias: float32 [768], replicated
- grad_ln2_gain: float32 [768], replicated
- grad_ln2_bias: float32 [768], replicated
- grad_w_up: float32 [768, 3072], replicated
- grad_up_bias: float32 [3072], replicated
- grad_w_down: float32 [3072, 768], replicated
- grad_down_bias: float32 [768], replicated
- bucket_counts: int32 [8, 16384], replicated
The draws below stay inside these ranges and needn't reach their ends.
All inputs are finite; a program needn't handle non-finite values.
Results may differ from the reference program's by a relative error of at most 0.0085.
The reference program's roundings to bfloat16 on the way count: a program that leaves them out, or rounds other values in their place, can miss the bound.
Values may be sent and summed in bfloat16 or wider, within the bound.
A program may use at most 256 MiB of HBM per device.

```python
import math
import jax
import jax.numpy as jnp
import numpy as np
from jax import lax

D = 768
HEADS = 12
HEAD_DIM = 64
FF = 3072
HASHES = 8
BUCKETS = 16384
MOLS = 512
ROW_DEV = 8
ROWS = 64
CHARS = 2048


def place_ends(drawn, key, low, largest):
    longest = drawn.shape.index(max(drawn.shape))
    spots = []
    for shift in (0, 1):
        where = [jax.random.randint(jax.random.fold_in(key, axis), (), 0, length) for axis, length in enumerate(drawn.shape)]
        where[longest] = (where[longest] + shift) % drawn.shape[longest]
        spots.append(tuple(where))
    return drawn.at[spots[0]].set(low).at[spots[1]].set(largest)


def level_of(stream_key, shape, shards, least, largest):
    factor_of, own = 1.0, jax.random.fold_in(stream_key, 6)
    for dim, parts in shards:
        draws = jnp.exp(jax.random.uniform(jax.random.fold_in(own, dim), (parts,), jnp.float32, least / len(shards), largest / len(shards)))
        factor_of = factor_of * jnp.repeat(draws, shape[dim] // parts).reshape([-1 if axis == dim else 1 for axis in range(len(shape))])
    return factor_of


def rank_bounds(count, lean):
    portions = [(1 << 20) // math.isqrt(grade ** lean) + 1 for grade in range(1, count + 1)]
    scale = 1 + sum(portions) // (1 << 30)
    return np.cumsum(np.array([max(1, weight // scale) for weight in portions]))


def ranked_ids(stream_key, shape, number_of, skew):
    grid = rank_bounds(number_of, skew)
    ticket = jax.random.randint(jax.random.fold_in(stream_key, 1), shape, 0, int(grid[number_of - 1]))
    rank = jnp.searchsorted(jnp.asarray(grid, jnp.int32), ticket, side="right")
    return jax.random.permutation(jax.random.fold_in(stream_key, 2), number_of)[rank].astype(jnp.int32)


def gaussian(stream_key, dims, deviation, most, split=(), kind=jnp.bfloat16):
    array = deviation * jax.random.normal(stream_key, dims, jnp.float32)
    if split:
        array = array * level_of(stream_key, dims, split, -0.22, 0.18)
    return jnp.clip(array, -most, most).astype(kind)


def setup_inputs(seed: int = 0) -> dict:
    arg_keys = jax.random.split(jax.random.key(seed), 16)
    molecules = gaussian(arg_keys[0], (ROWS, MOLS, D), 1.0, 6.0, ((0, 8), (1, 4)))
    ln1_gain = jnp.clip(1.0 + 0.1 * jax.random.normal(arg_keys[1], (D,), jnp.float32), 0.5, 1.5)
    ln1_bias = gaussian(arg_keys[2], (D,), 0.3, 3.0, (), jnp.float32)
    w_qkv = gaussian(arg_keys[3], (D, 3 * D), D ** -0.5, 0.21875)
    qkv_bias = gaussian(arg_keys[4], (2, D), 0.3, 3.0, (), jnp.float32)
    w_out = gaussian(arg_keys[5], (D, D), (max(D // 192, 1)) ** -0.5, 3.0)
    out_bias = gaussian(arg_keys[6], (D,), 0.3, 3.0, (), jnp.float32)
    ln2_gain = jnp.clip(1.0 + 0.1 * jax.random.normal(arg_keys[7], (D,), jnp.float32), 0.5, 1.5)
    ln2_bias = gaussian(arg_keys[8], (D,), 0.3, 3.0, (), jnp.float32)
    w_up = gaussian(arg_keys[9], (D, FF), D ** -0.5, 0.21875)
    up_bias = gaussian(arg_keys[10], (FF,), 0.3, 3.0, (), jnp.float32)
    w_down = gaussian(arg_keys[11], (FF, D), FF ** -0.5, 0.109375)
    down_bias = gaussian(arg_keys[12], (D,), 0.3, 3.0, (), jnp.float32)
    out_cotangent = gaussian(arg_keys[13], (ROWS, MOLS, D), 1.0, 6.0, ((0, 8), (1, 4)))
    bucket_ids = place_ends(ranked_ids(arg_keys[14], (HASHES, ROWS, CHARS), BUCKETS, 2), jax.random.fold_in(arg_keys[14], 3), 0, BUCKETS - 1).astype(jnp.int32)
    return dict(molecules=molecules, ln1_gain=ln1_gain, ln1_bias=ln1_bias, w_qkv=w_qkv, qkv_bias=qkv_bias, w_out=w_out, out_bias=out_bias, ln2_gain=ln2_gain, ln2_bias=ln2_bias, w_up=w_up, up_bias=up_bias, w_down=w_down, down_bias=down_bias, out_cotangent=out_cotangent, bucket_ids=bucket_ids)


@jax.custom_vjp
def low(v):
    return lax.optimization_barrier(v.astype(jnp.bfloat16)).astype(jnp.float32)

@jax.custom_vjp
def low_back(v):
    return v

def low_keep(v):
    return (low(v), None)

def low_pass(kept, grad):
    return (grad,)

def back_keep(v):
    return (v, None)

def back_low(kept, grad):
    return (low(grad),)
low.defvjp(low_keep, low_pass)
low_back.defvjp(back_keep, back_low)
highest = lax.Precision.HIGHEST
norm_eps = 1e-05

def layer_norm(value, gain, shift):
    center = value - lax.optimization_barrier(jnp.mean(value, -1, keepdims=True))
    spread = lax.optimization_barrier(jnp.mean(center * center, -1, keepdims=True))
    return center * lax.rsqrt(spread + norm_eps) * gain + shift

def layer(inputs, params):
    g_one, b_one, w_proj, b_proj, w_back, b_back, g_two, b_two, w_wide, b_wide, w_narrow, b_narrow = params
    count, length, width = inputs.shape
    a_one = low(layer_norm(inputs, g_one, b_one))
    joined = jnp.dot(a_one, w_proj, precision=highest)
    query = low_back(low(joined[..., :width] + b_proj[0]))
    keys = low_back(low(joined[..., width:2 * width]))
    values = low_back(low(joined[..., 2 * width:] + b_proj[1]))
    query = query.reshape(count, length, HEADS, HEAD_DIM)
    keys = keys.reshape(count, length, HEADS, HEAD_DIM)
    values = values.reshape(count, length, HEADS, HEAD_DIM)
    scores = jnp.einsum('nqhd,nkhd->nhqk', query, keys, precision=highest) * HEAD_DIM ** (-0.5)
    scores = low_back(scores)
    peak = lax.optimization_barrier(jnp.max(scores, -1, keepdims=True))
    expo = jnp.exp(scores - peak)
    probs = expo / lax.optimization_barrier(jnp.sum(expo, -1, keepdims=True))
    context = jnp.einsum('nhqk,nkhd->nqhd', low(probs), values, precision=highest)
    context = low_back(low(context.reshape(count, length, width)))
    branch = low_back(jnp.dot(context, w_back, precision=highest) + b_back)
    mid = inputs + branch
    a_two = low(layer_norm(mid, g_two, b_two))
    upper = low_back(jnp.dot(a_two, w_wide, precision=highest) + b_wide)
    hidden = low(jax.nn.gelu(upper, approximate=False))
    return mid + jnp.dot(hidden, w_narrow, precision=highest) + b_narrow

def reference(molecules, ln1_gain, ln1_bias, w_qkv, qkv_bias, w_out, out_bias, ln2_gain, ln2_bias, w_up, up_bias, w_down, down_bias, out_cotangent, bucket_ids):
    params = tuple((item.astype(jnp.float32) for item in (ln1_gain, ln1_bias, w_qkv, qkv_bias, w_out, out_bias, ln2_gain, ln2_bias, w_up, up_bias, w_down, down_bias)))
    blocks = ROWS // ROW_DEV
    inputs = molecules.astype(jnp.float32).reshape(blocks, ROW_DEV, MOLS, D)
    cotan = out_cotangent.astype(jnp.float32).reshape(blocks, ROW_DEV, MOLS, D)

    def step(carry, pair):
        block_in, block_cot = pair
        result, pull = jax.vjp(layer, block_in, params)
        grad_in, grad_params = pull(block_cot)
        carry = jax.tree.map(lambda left, right: left + right, carry, grad_params)
        return (carry, (result, grad_in))
    start = jax.tree.map(jnp.zeros_like, params)
    totals, (results, grads) = lax.scan(step, start, (inputs, cotan))
    offsets = (jnp.arange(HASHES, dtype=jnp.int32) * BUCKETS)[:, None, None]
    flat_ids = (bucket_ids + offsets).reshape(-1)
    counts = jnp.zeros((HASHES * BUCKETS,), jnp.int32).at[flat_ids].add(1).reshape(HASHES, BUCKETS)
    return (results.reshape(ROWS, MOLS, D).astype(jnp.bfloat16), grads.reshape(ROWS, MOLS, D), totals[0], totals[1], totals[2], totals[3], totals[4], totals[5], totals[6], totals[7], totals[8], totals[9], totals[10], totals[11], counts)
```

```python
import functools
import jax
import jax.numpy as jnp
from jax import lax
from jax.experimental import pallas as pl
from jax.experimental.pallas import tpu as pltpu
from jax.sharding import PartitionSpec as P

MESH = pl.DeviceIdType.MESH
BF = jnp.bfloat16
F32 = jnp.float32
EPS = 1e-5
D = 768
HD = 64
NH = 12
FF = 3072
BUCKETS = 16384
LANE = 128
MIB = 1 << 20


def dot_nn(a, b):
    return lax.dot_general(a, b, (((1,), (0,)), ((), ())), preferred_element_type=F32)


def dot_nt(a, b):
    return lax.dot_general(a, b, (((1,), (1,)), ((), ())), preferred_element_type=F32)


def dot_tn(a, b):
    return lax.dot_general(a, b, (((0,), (0,)), ((), ())), preferred_element_type=F32)


def norm_parts(x):
    mean = jnp.mean(x, -1, keepdims=True)
    cen = x - mean
    var = jnp.mean(cen * cen, -1, keepdims=True)
    rstd = lax.rsqrt(var + EPS)
    return cen * rstd, rstd


def norm_back(xhat, rstd, gain, dy):
    dxh = dy * gain
    m1 = jnp.mean(dxh, -1, keepdims=True)
    m2 = jnp.mean(dxh * xhat, -1, keepdims=True)
    return rstd * (dxh - m1 - xhat * m2)


def lane_half(shape, half):
    lane = lax.broadcasted_iota(jnp.int32, shape, 1)
    return (lane < HD) if half == 0 else (lane >= HD)


def fwd_kernel(x_ref, g1_ref, b1_ref, wqkv_ref, qb_ref, wout_ref, ob_ref, qkv_ref, lse_ref, ctx_ref, mid_ref, lacc):
    length = x_ref.shape[0]
    x = x_ref[...].astype(F32)
    xhat, _ = norm_parts(x)
    a1 = (xhat * g1_ref[...] + b1_ref[...]).astype(BF)
    for j in range(3):
        c = slice(j * D, (j + 1) * D)
        qkv_ref[:, c] = (dot_nn(a1, wqkv_ref[:, c]) + qb_ref[:, c]).astype(BF)

    def pair(p, carry):
        at = pl.multiple_of(p * LANE, LANE)
        q = qkv_ref[:, pl.ds(at, LANE)] * BF(0.125)
        k = qkv_ref[:, pl.ds(pl.multiple_of(D + at, LANE), LANE)]
        v = qkv_ref[:, pl.ds(pl.multiple_of(2 * D + at, LANE), LANE)]
        outs = []
        lse = lacc[...]
        lane = lax.broadcasted_iota(jnp.int32, lse.shape, 1)
        for half in range(2):
            qm = jnp.where(lane_half(q.shape, half), q, BF(0))
            s = dot_nt(qm, k)
            m = jnp.max(s, -1, keepdims=True)
            e = jnp.exp(s - m)
            t = jnp.sum(e, -1, keepdims=True)
            pr = (e * (1.0 / t)).astype(BF)
            outs.append(dot_nn(pr, v))
            lse = jnp.where(lane == 2 * p + half, m + jnp.log(t), lse)
        lacc[...] = lse
        ctx_ref[:, pl.ds(at, LANE)] = jnp.where(lane_half(outs[0].shape, 0), outs[0], outs[1]).astype(BF)
        return carry

    lacc[...] = jnp.zeros_like(lacc)
    lax.fori_loop(0, NH // 2, pair, 0)
    lt = lacc[...].T
    for h in range(NH):
        lse_ref[h] = lt[h : h + 1, :]
    mid_ref[...] = x + (dot_nn(ctx_ref[...], wout_ref[...]) + ob_ref[...])


def forward(x, g1, b1, wqkv, qb, wout, ob, length):
    tokens = x.shape[0]
    rows = tokens // length
    whole = lambda a: pl.BlockSpec(a.shape, lambda i: (0,) * a.ndim)
    return pl.pallas_call(
        fwd_kernel,
        grid=(rows,),
        in_specs=[pl.BlockSpec((length, D), lambda i: (i, 0))] + [whole(a) for a in (g1, b1, wqkv, qb, wout, ob)],
        out_specs=[
            pl.BlockSpec((length, 3 * D), lambda i: (i, 0)),
            pl.BlockSpec((NH, 1, length), lambda i: (i, 0, 0)),
            pl.BlockSpec((length, D), lambda i: (i, 0)),
            pl.BlockSpec((length, D), lambda i: (i, 0)),
        ],
        out_shape=[
            jax.ShapeDtypeStruct((tokens, 3 * D), BF),
            jax.ShapeDtypeStruct((rows * NH, 1, length), F32),
            jax.ShapeDtypeStruct((tokens, D), BF),
            jax.ShapeDtypeStruct((tokens, D), F32),
        ],
        scratch_shapes=[pltpu.VMEM((length, LANE), F32)],
        compiler_params=pltpu.CompilerParams(vmem_limit_bytes=58 * MIB),
        name="attn_forward",
    )(x, g1, b1, wqkv, qb, wout, ob)


def mlp_kernel(nb, mid_ref, dy_ref, g2_ref, b2_ref, wup_ref, ub_ref, wdn_ref, db_ref,
               lo_ref, dx2_ref, gd_ref, gu_ref, vec_ref, gub_ref, a2_s, a2t_s, dyt_s, acc_s, da2_s):
    i = pl.program_id(0)

    @pl.when(i == 0)
    def _():
        xhat, _ = norm_parts(mid_ref[...])
        a2 = (xhat * g2_ref[...] + b2_ref[...]).astype(BF)
        a2_s[...] = a2
        a2t_s[...] = a2.T
        dyt_s[...] = dy_ref[...].T
        acc_s[...] = mid_ref[...] + db_ref[...]
        da2_s[...] = jnp.zeros_like(da2_s)

    u = dot_nn(a2_s[...], wup_ref[...]) + ub_ref[...]
    dh = dot_nt(dy_ref[...], wdn_ref[...])
    cdf = 0.5 + 0.5 * lax.erf(u * (2.0 ** -0.5))
    pdf = jnp.exp(u * u * -0.5) * 0.3989422804014327
    hid = (u * cdf).astype(BF)
    du32 = dh * (cdf + u * pdf)
    du = du32.astype(BF)
    gub_ref[...] = jnp.sum(du.astype(F32), 0, keepdims=True)
    acc_s[...] += dot_nn(hid, wdn_ref[...])
    da2_s[...] += dot_nt(du, wup_ref[...])
    gd = dot_nn(dyt_s[...], hid).astype(BF)
    gu = dot_nn(a2t_s[...], du).astype(BF)
    for j in range(nb):
        gd_ref[j] = gd[:, j * LANE : (j + 1) * LANE]
        gu_ref[j] = gu[:, j * LANE : (j + 1) * LANE]

    @pl.when(i == pl.num_programs(0) - 1)
    def _():
        lo_ref[...] = acc_s[...].astype(BF)
        dy = dy_ref[...].astype(F32)
        xhat, rstd = norm_parts(mid_ref[...])
        da2 = da2_s[...]
        dx2 = dy + norm_back(xhat, rstd, g2_ref[...], da2)
        dx2_ref[...] = dx2
        vec_ref[0:1, :] = jnp.sum(dy, 0, keepdims=True)
        vec_ref[1:2, :] = jnp.sum(da2 * xhat, 0, keepdims=True)
        vec_ref[2:3, :] = jnp.sum(da2, 0, keepdims=True)
        vec_ref[3:4, :] = jnp.sum(dx2.astype(BF).astype(F32), 0, keepdims=True)
        vec_ref[4:8, :] = jnp.zeros((4, D), F32)


def mlp(mid, dy, g2, b2, wup, ub, wdn, db, nb):
    tokens = mid.shape[0]
    fc = nb * LANE
    whole = lambda a: pl.BlockSpec(a.shape, lambda i: (0,) * a.ndim)
    tok = pl.BlockSpec((tokens, D), lambda i: (0, 0))
    return pl.pallas_call(
        functools.partial(mlp_kernel, nb),
        grid=(FF // fc,),
        in_specs=[tok, tok, whole(g2), whole(b2), pl.BlockSpec((D, fc), lambda i: (0, i)), pl.BlockSpec((1, fc), lambda i: (0, i)),
                  pl.BlockSpec((fc, D), lambda i: (i, 0)), whole(db)],
        out_specs=[tok, tok, pl.BlockSpec((nb, D, LANE), lambda i: (i, 0, 0)), pl.BlockSpec((nb, D, LANE), lambda i: (i, 0, 0)),
                   pl.BlockSpec((8, D), lambda i: (0, 0)), pl.BlockSpec((1, fc), lambda i: (0, i))],
        out_shape=[jax.ShapeDtypeStruct((tokens, D), BF), jax.ShapeDtypeStruct((tokens, D), F32),
                   jax.ShapeDtypeStruct((FF // LANE, D, LANE), BF), jax.ShapeDtypeStruct((FF // LANE, D, LANE), BF),
                   jax.ShapeDtypeStruct((8, D), F32), jax.ShapeDtypeStruct((1, FF), F32)],
        scratch_shapes=[pltpu.VMEM((tokens, D), BF), pltpu.VMEM((D, tokens), BF), pltpu.VMEM((D, tokens), BF),
                        pltpu.VMEM((tokens, D), F32), pltpu.VMEM((tokens, D), F32)],
        compiler_params=pltpu.CompilerParams(vmem_limit_bytes=60 * MIB),
        name="feed_forward",
    )(mid, dy, g2, b2, wup, ub, wdn, db)


def bwd_kernel(length, x_ref, qkv_ref, lse_ref, ctx_ref, dx2_ref, g1_ref, b1_ref, wqkv_ref, wout_ref,
               gm_ref, gr_ref, vec_ref, dctx_s, dqkv_s, do_s):
    tokens = x_ref.shape[0]
    rows = tokens // length
    do_s[...] = dx2_ref[...].astype(BF)
    dctx_s[...] = dot_nt(do_s[...], wout_ref[...]).astype(BF)
    gout = dot_tn(ctx_ref[...], do_s[...]).astype(BF)
    nq = 3 * D // LANE
    for j in range(D // LANE):
        gr_ref[nq + j] = gout[:, j * LANE : (j + 1) * LANE]

    def pair(i, carry):
        r = i // (NH // 2)
        p = i % (NH // 2)
        tok = pl.ds(pl.multiple_of(r * length, length), length)
        cq = pl.ds(pl.multiple_of(p * LANE, LANE), LANE)
        ck = pl.ds(pl.multiple_of(p * LANE + D, LANE), LANE)
        cv = pl.ds(pl.multiple_of(p * LANE + 2 * D, LANE), LANE)
        q = qkv_ref[tok, cq] * BF(0.125)
        k = qkv_ref[tok, ck]
        v = qkv_ref[tok, cv]
        dc = dctx_s[tok, cq]
        dqs, dks, dvs = [], [], []
        for half in range(2):
            keep = lane_half(k.shape, half)
            km = jnp.where(keep, k, BF(0))
            vm = jnp.where(keep, v, BF(0))
            lse = lse_ref[r * NH + 2 * p + half]
            st = dot_nt(km, q)
            pt = jnp.exp(st - lse)
            dpt = dot_nt(vm, dc)
            inner = jnp.sum(pt * dpt, 0, keepdims=True)
            dst = (pt * (dpt - inner)).astype(BF)
            dvs.append(dot_nn(pt.astype(BF), dc))
            dks.append(dot_nn(dst, q))
            dqs.append(dot_tn(dst, k))
        sel = lane_half(dqs[0].shape, 0)
        dqkv_s[tok, cq] = (jnp.where(sel, dqs[0], dqs[1]) * 0.125).astype(BF)
        dqkv_s[tok, ck] = jnp.where(sel, dks[0], dks[1]).astype(BF)
        dqkv_s[tok, cv] = jnp.where(sel, dvs[0], dvs[1]).astype(BF)
        return carry

    lax.fori_loop(0, rows * (NH // 2), pair, 0)
    xhat, rstd = norm_parts(x_ref[...].astype(F32))
    a1 = (xhat * g1_ref[...] + b1_ref[...]).astype(BF)
    a1t = a1.T
    for j in range(3):
        c = slice(j * D, (j + 1) * D)
        gq = dot_nn(a1t, dqkv_s[:, c]).astype(BF)
        for t in range(D // LANE):
            gr_ref[j * (D // LANE) + t] = gq[:, t * LANE : (t + 1) * LANE]
    da1 = dot_nt(dqkv_s[...], wqkv_ref[...])
    gm_ref[...] = (dx2_ref[...] + norm_back(xhat, rstd, g1_ref[...], da1)).astype(BF)
    vec_ref[0:1, :] = jnp.sum(da1 * xhat, 0, keepdims=True)
    vec_ref[1:2, :] = jnp.sum(da1, 0, keepdims=True)
    vec_ref[2:3, :] = jnp.sum(dqkv_s[:, 0:D].astype(F32), 0, keepdims=True)
    vec_ref[3:4, :] = jnp.sum(dqkv_s[:, 2 * D : 3 * D].astype(F32), 0, keepdims=True)
    vec_ref[4:8, :] = jnp.zeros((4, D), F32)


def backward(x, qkv, lse, ctx, dx2, g1, b1, wqkv, wout, length):
    tokens = x.shape[0]
    vm = pl.BlockSpec(memory_space=pltpu.VMEM)
    return pl.pallas_call(
        functools.partial(bwd_kernel, length),
        in_specs=[vm] * 9,
        out_specs=[vm] * 3,
        out_shape=[jax.ShapeDtypeStruct((tokens, D), BF), jax.ShapeDtypeStruct((4 * D // LANE, D, LANE), BF),
                   jax.ShapeDtypeStruct((8, D), F32)],
        scratch_shapes=[pltpu.VMEM((tokens, D), BF), pltpu.VMEM((tokens, 3 * D), BF), pltpu.VMEM((tokens, D), BF)],
        compiler_params=pltpu.CompilerParams(vmem_limit_bytes=60 * MIB),
        name="attn_backward",
    )(x, qkv, lse, ctx, dx2, g1, b1, wqkv, wout)


def count_kernel(ids_ref, out_ref):
    hashes, rows, chars = ids_ref.shape
    high = BUCKETS // LANE

    def one(h, carry):
        total = jnp.zeros((high, LANE), F32)
        for r in range(rows):
            ids = ids_ref[h, r : r + 1, :]
            row = lax.broadcasted_iota(jnp.int32, (high, chars), 0)
            hi = jnp.where(row == (ids >> 7), 1.0, 0.0).astype(BF)
            lo = jnp.where(row == (ids & (LANE - 1)), 1.0, 0.0).astype(BF)
            total = total + dot_nt(hi, lo)
        out_ref[h] = total.astype(jnp.int32)
        return carry

    lax.fori_loop(0, hashes, one, 0)


def count(ids):
    return pl.pallas_call(
        count_kernel,
        in_specs=[pl.BlockSpec(memory_space=pltpu.VMEM)],
        out_specs=pl.BlockSpec(memory_space=pltpu.VMEM),
        out_shape=jax.ShapeDtypeStruct((ids.shape[0], BUCKETS // LANE, LANE), jnp.int32),
        compiler_params=pltpu.CompilerParams(vmem_limit_bytes=32 * MIB),
        name="bucket_tally",
    )(ids)


def widen_kernel(src_ref, out_ref):
    for j in range(src_ref.shape[0]):
        out_ref[:, j * LANE : (j + 1) * LANE] = src_ref[j].astype(F32)


def widen(blocks, at, number, step):
    assert at % step == 0
    return pl.pallas_call(
        widen_kernel,
        grid=(number // step,),
        in_specs=[pl.BlockSpec((step, D, LANE), lambda i: (at // step + i, 0, 0))],
        out_specs=pl.BlockSpec((D, step * LANE), lambda i: (0, i)),
        out_shape=jax.ShapeDtypeStruct((D, number * LANE), F32),
        compiler_params=pltpu.CompilerParams(vmem_limit_bytes=32 * MIB),
        name="widen",
    )(blocks)


def widen_t_kernel(src_ref, out_ref):
    for j in range(src_ref.shape[0]):
        out_ref[j * LANE : (j + 1) * LANE, :] = src_ref[j].astype(F32).T


def widen_t(blocks, at, number, step):
    assert at % step == 0
    return pl.pallas_call(
        widen_t_kernel,
        grid=(number // step,),
        in_specs=[pl.BlockSpec((step, D, LANE), lambda i: (at // step + i, 0, 0))],
        out_specs=pl.BlockSpec((step * LANE, D), lambda i: (i, 0)),
        out_shape=jax.ShapeDtypeStruct((number * LANE, D), F32),
        compiler_params=pltpu.CompilerParams(vmem_limit_bytes=32 * MIB),
        name="widen_turned",
    )(blocks)


def on_device(shape, molecules, ln1_gain, ln1_bias, w_qkv, qkv_bias, w_out, out_bias, ln2_gain, ln2_bias, w_up, up_bias,
              w_down, down_bias, out_cotangent, bucket_ids):
    rows_here, local_len, width = molecules.shape
    seq = shape["seq"]
    length = local_len * seq
    row = lambda a: a.reshape(1, -1)
    tally = count(bucket_ids)
    counts = lax.psum(tally, ("rows", "seq")).reshape(bucket_ids.shape[0], BUCKETS)
    x = lax.all_to_all(molecules, "seq", split_axis=0, concat_axis=1, tiled=True).reshape(-1, width)
    dy = lax.all_to_all(out_cotangent, "seq", split_axis=0, concat_axis=1, tiled=True).reshape(-1, width)
    qb = jnp.concatenate([qkv_bias[0], jnp.zeros((width,), F32), qkv_bias[1]]).reshape(1, -1)
    qkv, lse, ctx, mid = forward(x, row(ln1_gain), row(ln1_bias), w_qkv, qb, w_out, row(out_bias), length)
    lo, dx2, gd, gu, vec2, gub = mlp(mid, dy, row(ln2_gain), row(ln2_bias), w_up, row(up_bias), w_down, row(down_bias), 4)
    gm, gr, vec1 = backward(x, qkv, lse, ctx, dx2, row(ln1_gain), row(ln1_bias), w_qkv, w_out, length)
    back = lambda a: lax.all_to_all(a.reshape(-1, length, width), "seq", split_axis=1, concat_axis=0, tiled=True)
    layer_out = back(lo)
    gmol = back(gm).astype(F32)
    gd, gu, gr = lax.psum((gd, gu, gr), ("rows", "seq"))
    small = lax.psum(jnp.concatenate([vec2.reshape(-1), vec1.reshape(-1), gub.reshape(-1)]), ("rows", "seq"))
    v2 = small[: 8 * D].reshape(8, D)
    v1 = small[8 * D : 16 * D].reshape(8, D)
    return (layer_out, gmol, v1[0], v1[1], widen(gr, 0, 18, 6), v1[2:4], widen(gr, 18, 6, 6), v2[3], v2[1], v2[2],
            widen(gu, 0, 24, 6), small[16 * D :], widen_t(gd, 0, 24, 6), v2[0], counts)


def solution(mesh):
    tok = P("rows", "seq", None)
    return jax.shard_map(
        functools.partial(on_device, dict(mesh.shape)),
        mesh=mesh,
        in_specs=(tok,) + (P(),) * 12 + (tok, P(None, "rows", "seq")),
        out_specs=(tok, tok) + (P(),) * 13,
        check_vma=False,
    )
```

```python
import functools
import jax
import jax.numpy as jnp
from jax import lax
from jax.experimental import pallas as pl
from jax.experimental.pallas import tpu as pltpu
from jax.sharding import PartitionSpec as P

MESH = pl.DeviceIdType.MESH
BF = jnp.bfloat16
F32 = jnp.float32
EPS = 1e-5
D = 768
HD = 64
NH = 12
FF = 3072
BUCKETS = 16384
LANE = 128
MIB = 1 << 20


def dot_nn(a, b):
    return lax.dot_general(a, b, (((1,), (0,)), ((), ())), preferred_element_type=F32)


def dot_nt(a, b):
    return lax.dot_general(a, b, (((1,), (1,)), ((), ())), preferred_element_type=F32)


def dot_tn(a, b):
    return lax.dot_general(a, b, (((0,), (0,)), ((), ())), preferred_element_type=F32)


def norm_parts(x):
    mean = jnp.mean(x, -1, keepdims=True)
    cen = x - mean
    var = jnp.mean(cen * cen, -1, keepdims=True)
    rstd = lax.rsqrt(var + EPS)
    return cen * rstd, rstd


def norm_back(xhat, rstd, gain, dy):
    dxh = dy * gain
    m1 = jnp.mean(dxh, -1, keepdims=True)
    m2 = jnp.mean(dxh * xhat, -1, keepdims=True)
    return rstd * (dxh - m1 - xhat * m2)


def lane_half(shape, half):
    lane = lax.broadcasted_iota(jnp.int32, shape, 1)
    return (lane < HD) if half == 0 else (lane >= HD)


def fwd_kernel(x_ref, g1_ref, b1_ref, wqkv_ref, qb_ref, wout_ref, ob_ref, qkv_ref, lse_ref, ctx_ref, mid_ref, lacc):
    length = x_ref.shape[0]
    x = x_ref[...].astype(F32)
    xhat, _ = norm_parts(x)
    a1 = (xhat * g1_ref[...] + b1_ref[...]).astype(BF)
    for j in range(3):
        c = slice(j * D, (j + 1) * D)
        qkv_ref[:, c] = (dot_nn(a1, wqkv_ref[:, c]) + qb_ref[:, c]).astype(BF)

    def pair(p, carry):
        at = pl.multiple_of(p * LANE, LANE)
        q = qkv_ref[:, pl.ds(at, LANE)] * BF(0.125)
        k = qkv_ref[:, pl.ds(pl.multiple_of(D + at, LANE), LANE)]
        v = qkv_ref[:, pl.ds(pl.multiple_of(2 * D + at, LANE), LANE)]
        outs = []
        lse = lacc[...]
        lane = lax.broadcasted_iota(jnp.int32, lse.shape, 1)
        for half in range(2):
            qm = jnp.where(lane_half(q.shape, half), q, BF(0))
            s = dot_nt(qm, k)
            m = jnp.max(s, -1, keepdims=True)
            e = jnp.exp(s - m)
            t = jnp.sum(e, -1, keepdims=True)
            pr = (e * (1.0 / t)).astype(BF)
            outs.append(dot_nn(pr, v))
            lse = jnp.where(lane == 2 * p + half, m + jnp.log(t), lse)
        lacc[...] = lse
        ctx_ref[:, pl.ds(at, LANE)] = jnp.where(lane_half(outs[0].shape, 0), outs[0], outs[1]).astype(BF)
        return carry

    lacc[...] = jnp.zeros_like(lacc)
    lax.fori_loop(0, NH // 2, pair, 0)
    lt = lacc[...].T
    for h in range(NH):
        lse_ref[h] = lt[h : h + 1, :]
    mid_ref[...] = x + (dot_nn(ctx_ref[...], wout_ref[...]) + ob_ref[...])


def forward(x, g1, b1, wqkv, qb, wout, ob, length):
    tokens = x.shape[0]
    rows = tokens // length
    whole = lambda a: pl.BlockSpec(a.shape, lambda i: (0,) * a.ndim)
    return pl.pallas_call(
        fwd_kernel,
        grid=(rows,),
        in_specs=[pl.BlockSpec((length, D), lambda i: (i, 0))] + [whole(a) for a in (g1, b1, wqkv, qb, wout, ob)],
        out_specs=[
            pl.BlockSpec((length, 3 * D), lambda i: (i, 0)),
            pl.BlockSpec((NH, 1, length), lambda i: (i, 0, 0)),
            pl.BlockSpec((length, D), lambda i: (i, 0)),
            pl.BlockSpec((length, D), lambda i: (i, 0)),
        ],
        out_shape=[
            jax.ShapeDtypeStruct((tokens, 3 * D), BF),
            jax.ShapeDtypeStruct((rows * NH, 1, length), F32),
            jax.ShapeDtypeStruct((tokens, D), BF),
            jax.ShapeDtypeStruct((tokens, D), F32),
        ],
        scratch_shapes=[pltpu.VMEM((length, LANE), F32)],
        compiler_params=pltpu.CompilerParams(vmem_limit_bytes=58 * MIB),
        name="attn_forward",
    )(x, g1, b1, wqkv, qb, wout, ob)


def count_kernel(ids_ref, out_ref):
    hashes, rows, chars = ids_ref.shape
    high = BUCKETS // LANE

    def one(h, carry):
        total = jnp.zeros((high, LANE), F32)
        for r in range(rows):
            ids = ids_ref[h, r : r + 1, :]
            row = lax.broadcasted_iota(jnp.int32, (high, chars), 0)
            hi = jnp.where(row == (ids >> 7), 1.0, 0.0).astype(BF)
            lo = jnp.where(row == (ids & (LANE - 1)), 1.0, 0.0).astype(BF)
            total = total + dot_nt(hi, lo)
        out_ref[h] = total.astype(jnp.int32)
        return carry

    lax.fori_loop(0, hashes, one, 0)


def count(ids):
    return pl.pallas_call(
        count_kernel,
        in_specs=[pl.BlockSpec(memory_space=pltpu.VMEM)],
        out_specs=pl.BlockSpec(memory_space=pltpu.VMEM),
        out_shape=jax.ShapeDtypeStruct((ids.shape[0], BUCKETS // LANE, LANE), jnp.int32),
        compiler_params=pltpu.CompilerParams(vmem_limit_bytes=32 * MIB),
        name="bucket_tally",
    )(ids)


NB = 4
NFF = FF // (NB * LANE)
NPAIR = NFF + 3


def spots():
    return lax.axis_index("rows"), lax.axis_index("seq")


def bit_of(step):
    axis, mask = step
    return (lax.axis_index(axis) // mask) % 2


def across(step):
    axis, mask = step
    rows, seq = spots()
    move = mask - 2 * mask * bit_of(step)
    return (rows + move, seq) if axis == "rows" else (rows, seq + move)


def orders(shape):
    seq = [("seq", 1 << b) for b in range(shape["seq"].bit_length() - 1)]
    row = [("rows", 1 << b) for b in range(shape["rows"].bit_length() - 1)]
    return [seq + row, seq[:1] + row[:1] + seq[1:] + row[1:]]


class Halving:
    def __init__(self, order, lead, rows, tile):
        self.order, self.tile = order, tile
        self.size, self.split, self.lead_at, self.row_at, self.own = [], [], [], [], []
        lead_at, row_at = 0, 0
        for i, step in enumerate(order):
            bit = bit_of(step)
            if lead > 1:
                lead //= 2
                how = 0
                if i == 0:
                    self.first = bit * lead
                else:
                    lead_at = lead_at + bit * lead
            elif rows % (2 * tile) == 0:
                rows //= 2
                how = 1
                row_at = row_at + bit * rows
            else:
                how = None
            self.own.append(bit)
            self.split.append(how)
            self.size.append((lead, rows))
            self.lead_at.append(lead_at)
            self.row_at.append(row_at)
        self.gathers = [i for i in reversed(range(len(order))) if self.split[i] is not None]

    def rows_of(self, at, size):
        return pl.ds(pl.multiple_of(at, self.tile), size)

    def send(self, i, mine, land, sems):
        step, (lead, rows) = self.order[i], self.size[i]
        if i == 0:
            src = mine.at[pl.ds(lead - self.first, lead)]
        else:
            la, ra = self.lead_at[i - 1], self.row_at[i - 1]
            if self.split[i] == 0:
                la = la + (1 - self.own[i]) * lead
            elif self.split[i] == 1:
                ra = ra + (1 - self.own[i]) * rows
            src = land[0].at[pl.ds(la, lead), self.rows_of(ra, rows)]
        return pltpu.make_async_remote_copy(src_ref=src, dst_ref=land[i], send_sem=sems[0].at[i], recv_sem=sems[1].at[i],
                                            device_id=across(step), device_id_type=MESH)

    def add(self, i, mine, land):
        lead, rows = self.size[i]
        part = rows if rows <= LANE else 96
        wide = F32 if land[0].dtype == BF else land[0].dtype

        def some(t, carry):
            at = t * part
            if i == 0:
                here = (slice(None), self.rows_of(at, part))
                left, right = land[0][here], mine[pl.ds(self.first, lead), self.rows_of(at, part)]
            else:
                here = (pl.ds(self.lead_at[i], lead), self.rows_of(self.row_at[i] + at, part))
                left, right = land[0][here], land[i][:, self.rows_of(at, part)]
            land[0][here] = (left.astype(wide) + right.astype(wide)).astype(land[0].dtype)
            return carry

        lax.fori_loop(0, rows // part, some, 0)

    def at_level(self, i):
        lead, rows = self.size[i]
        return pl.ds(self.lead_at[i], lead), self.rows_of(self.row_at[i], rows)

    def out_level(self, i):
        lead, rows = self.size[i]
        return pl.ds(self.first + self.lead_at[i], lead), self.rows_of(self.row_at[i], rows)

    def keep(self, land, out, sem):
        last = len(self.order) - 1
        return pltpu.make_async_copy(land[0].at[self.at_level(last)], out.at[self.out_level(last)], sem)

    def gather(self, m, land, out, sems):
        i = self.gathers[m]
        here = out.at[self.out_level(i)]
        src = land[0].at[self.at_level(len(self.order) - 1)] if m == 0 else here
        return pltpu.make_async_remote_copy(src_ref=src, dst_ref=here, send_sem=sems[0].at[m], recv_sem=sems[1].at[m],
                                            device_id=across(self.order[i]), device_id_type=MESH)

    def reduce_step(self, k, mine, land, sems):
        n = len(self.order)
        if k > 0:
            self.send(k - 1, mine, land, sems).wait()
            self.add(k - 1, mine, land)
        if k < n:
            self.send(k, mine, land, sems).start()

    def gather_step(self, m, land, out, sems, sem):
        if m == 0:
            self.keep(land, out, sem).start()
        else:
            if m == 1:
                self.keep(land, out, sem).wait()
            self.gather(m - 1, land, out, sems).wait()
        if m < len(self.gathers):
            self.gather(m, land, out, sems).start()


def land_shapes(count, lead, rows, tile, steps, dtype):
    shapes = []
    for _ in range(steps):
        if lead > 1:
            lead //= 2
        elif rows % (2 * tile) == 0:
            rows //= 2
        shapes.append(pltpu.VMEM(count + (lead, rows, LANE), dtype))
    return shapes


AG_AT = (8, 13, 18, 22, 23, 24, 25, 27, 28)


def rear_kernel(shape, length, mid_h, dy_h, x_h, qkv_h, ctx_h, wup_h, wdn_h, wqkv_h, wout_h, lse_ref, cnt_ref,
                g1_ref, b1_ref, g2_ref, b2_ref, ub_ref, db_ref,
                lo_out, gm_out, sum_out, cnt_out, vec_out,
                mid_s, dy_s, a2_s, a2t_s, dyt_s, acc_s, da2_s, wup_s, wdn_s, qkv_s, ctx_s, x_s, wqkv_s, wout_s,
                dqkv_s, gout_s, lo_s, vec_s, gub_s, part_s, fetch_sem, stage_s, vland_s, vacc_s,
                rs_send, rs_recv, ag_send, ag_recv, keep_sem, crs_send, crs_recv, cag_send, cag_recv, ckeep_sem,
                v_send, v_recv, t_send, t_recv, t_own, *lands):
    both = orders(shape)
    nd = len(both[0])
    nseq = shape["seq"]
    land = lands[:nd]
    cland = lands[nd:]
    rows_idx, me = spots()
    tokens = mid_s.shape[0]
    rows = tokens // length
    local = length // nseq
    fc = NB * LANE

    barrier = pltpu.get_barrier_semaphore()
    others = [across(step) for step in both[0]]
    for m in range(3, nseq):
        if m & (m - 1):
            others.append((rows_idx, sum(((me // (1 << b)) % 2 + ((m >> b) & 1) * (1 - 2 * ((me // (1 << b)) % 2))) * (1 << b)
                                         for b in range(nseq.bit_length() - 1))))
    for other in others:
        pl.semaphore_signal(barrier, inc=1, device_id=other, device_id_type=MESH)

    def fetch(t):
        return pltpu.make_async_copy((mid_h, dy_h, x_h, qkv_h, ctx_h, wqkv_h, wout_h)[t],
                                     (mid_s, dy_s, x_s, qkv_s, ctx_s, wqkv_s, wout_s)[t], fetch_sem.at[t])

    def weights(i, slot):
        return (pltpu.make_async_copy(wup_h.at[:, pl.ds(pl.multiple_of(i * fc, fc), fc)], wup_s.at[slot], fetch_sem.at[8 + slot]),
                pltpu.make_async_copy(wdn_h.at[pl.ds(pl.multiple_of(i * fc, fc), fc)], wdn_s.at[slot], fetch_sem.at[10 + slot]))

    fetch(0).start()
    fetch(1).start()
    for copy in weights(0, 0):
        copy.start()
    pl.semaphore_wait(barrier, len(others))

    plans = [Halving(order, NB, D, 16) for order in both]
    tally = Halving(both[1], cnt_ref.shape[0], cnt_ref.shape[1], 8)
    in_at = list(range(NFF)) + [NFF + 5, NFF + 10, NFF + 15]
    out_at = [max(a, b + nd) for a, b in zip(AG_AT, in_at)]
    last_tick = NFF + 16

    def tick(t):
        for k in reversed(range(nd + 1)):
            hit = sum(jnp.where(t == in_at[j] + k, 1, 0) for j in range(NPAIR))
            j = sum(jnp.where(t == in_at[j] + k, j, 0) for j in range(NPAIR))

            @pl.when(hit == 1)
            def _():
                for o, plan in enumerate(plans):
                    plan.reduce_step(k, stage_s.at[j % 2, o], [r.at[j, o] for r in land], (rs_send.at[j, o], rs_recv.at[j, o]))

        most = max(len(plan.gathers) for plan in plans)
        for m in reversed(range(most + 1)):
            hit = sum(jnp.where(t == out_at[j] + m, 1, 0) for j in range(NPAIR))
            j = sum(jnp.where(t == out_at[j] + m, j, 0) for j in range(NPAIR))

            @pl.when(hit == 1)
            def _():
                for o, plan in enumerate(plans):
                    plan.gather_step(m, [r.at[j, o] for r in land], sum_out.at[j, o], (ag_send.at[j, o], ag_recv.at[j, o]),
                                     keep_sem.at[j, o])

    def tick_counts(t):
        for k in range(nd + 1):

            @pl.when(t == k)
            def _():
                tally.reduce_step(k, cnt_ref, cland, (crs_send, crs_recv))

        for m in range(len(tally.gathers) + 1):

            @pl.when(t == nd + 1 + m)
            def _():
                tally.gather_step(m, cland, cnt_out, (cag_send, cag_recv), ckeep_sem)

    def give_back(which, out):
        copies = []
        for m in range(1, nseq):
            bits = [(me // (1 << b)) % 2 for b in range(nseq.bit_length() - 1)]
            to = sum((bit + ((m >> b) & 1) * (1 - 2 * bit)) * (1 << b) for b, bit in enumerate(bits))
            copies.append(pltpu.make_async_remote_copy(
                src_ref=lo_s.at[:, pl.ds(pl.multiple_of(to * local, local), local)], dst_ref=out.at[pl.ds(me * rows, rows)],
                send_sem=t_send.at[which, m], recv_sem=t_recv.at[which, m], device_id=(rows_idx, to), device_id_type=MESH))
        copies.append(pltpu.make_async_copy(lo_s.at[:, pl.ds(pl.multiple_of(me * local, local), local)],
                                            out.at[pl.ds(me * rows, rows)], t_own.at[which]))
        return copies

    step = 256
    pieces = tokens // step
    fetch(0).wait()
    fetch(1).wait()
    for t in (6, 4, 2, 3, 5):
        fetch(t).start()

    def open_piece(n, carry):
        at = pl.ds(pl.multiple_of(n * step, step), step)
        mid = mid_s[at]
        xhat, _ = norm_parts(mid)
        a2 = (xhat * g2_ref[...] + b2_ref[...]).astype(BF)
        a2_s[at] = a2
        a2t_s[:, at] = a2.T
        dyt_s[:, at] = dy_s[at].T
        acc_s[at] = mid + db_ref[...]
        da2_s[at] = jnp.zeros((step, D), F32)
        return carry

    lax.fori_loop(0, pieces, open_piece, 0)

    def ff(i, carry):
        slot = i % 2

        @pl.when(i + 1 < NFF)
        def _():
            for copy in weights(i + 1, 1 - slot):
                copy.start()

        for copy in weights(i, slot):
            copy.wait()
        cols = pl.ds(pl.multiple_of(i * fc, fc), fc)
        u = dot_nn(a2_s[...], wup_s[slot]) + ub_ref[:, cols]
        dh = dot_nt(dy_s[...], wdn_s[slot])
        cdf = 0.5 + 0.5 * lax.erf(u * (2.0 ** -0.5))
        pdf = jnp.exp(u * u * -0.5) * 0.3989422804014327
        hid = (u * cdf).astype(BF)
        du = (dh * (cdf + u * pdf)).astype(BF)
        gub_s[:, cols] = jnp.sum(du.astype(F32), 0, keepdims=True)
        acc_s[...] += dot_nn(hid, wdn_s[slot])
        da2_s[...] += dot_nt(du, wup_s[slot])
        gd = dot_nn(dyt_s[...], hid).astype(BF)
        gu = dot_nn(a2t_s[...], du).astype(BF)
        for b in range(NB):
            stage_s[slot, 0, b] = gd[:, b * LANE : (b + 1) * LANE]
            stage_s[slot, 1, b] = gu[:, b * LANE : (b + 1) * LANE]
        tick(i)
        tick_counts(i)
        return carry

    lax.fori_loop(0, NFF, ff, 0)

    part_s[...] = jnp.zeros_like(part_s)
    fetch(6).wait()

    def turn_piece(n, carry):
        at = pl.ds(pl.multiple_of(n * step, step), step)
        lo_s[n * step // length, pl.ds(pl.multiple_of((n * step) % length, step), step)] = acc_s[at].astype(BF)
        dy = dy_s[at].astype(F32)
        xhat, rstd = norm_parts(mid_s[at])
        da2 = da2_s[at]
        dx2 = dy + norm_back(xhat, rstd, g2_ref[...], da2)
        da2_s[at] = dx2
        do = dx2.astype(BF)
        a2_s[at] = do
        part_s[0:1] += jnp.sum(dy, 0, keepdims=True)
        part_s[1:2] += jnp.sum(da2 * xhat, 0, keepdims=True)
        part_s[2:3] += jnp.sum(da2, 0, keepdims=True)
        part_s[3:4] += jnp.sum(do.astype(F32), 0, keepdims=True)
        dy_s[at] = dot_nt(do, wout_s[...]).astype(BF)
        return carry

    lax.fori_loop(0, pieces, turn_piece, 0)
    dctx_s, do_s, dx2_s, da1_s, a1t_s = dy_s, a2_s, da2_s, acc_s, a2t_s
    for copy in give_back(0, lo_out):
        copy.start()
    fetch(4).wait()
    fetch(2).wait()
    gout = dot_tn(ctx_s[...], do_s[...]).astype(BF)
    for b in range(D // LANE):
        gout_s[b] = gout[:, b * LANE : (b + 1) * LANE]

    def first_norm(n, carry):
        at = pl.ds(pl.multiple_of(n * step, step), step)
        xhat, _ = norm_parts(x_s[at].astype(F32))
        a1t_s[:, at] = (xhat * g1_ref[...] + b1_ref[...]).astype(BF).T
        da1_s[at] = jnp.zeros((step, D), F32)
        return carry

    lax.fori_loop(0, pieces, first_norm, 0)
    fetch(3).wait()
    fetch(5).wait()
    tick(NFF)
    tick_counts(NFF)

    def group(g, carry):
        def unit(n, inner_carry):
            r = n // 2
            h = n % 2
            p = 2 * g + h
            tok = pl.ds(pl.multiple_of(r * length, length), length)
            cq = pl.ds(pl.multiple_of(p * LANE, LANE), LANE)
            q = qkv_s[tok, cq] * BF(0.125)
            k = qkv_s[tok, pl.ds(pl.multiple_of(p * LANE + D, LANE), LANE)]
            v = qkv_s[tok, pl.ds(pl.multiple_of(p * LANE + 2 * D, LANE), LANE)]
            dc = dctx_s[tok, cq]
            dqs, dks, dvs = [], [], []
            for half in range(2):
                keep = lane_half(k.shape, half)
                km = jnp.where(keep, k, BF(0))
                vm = jnp.where(keep, v, BF(0))
                lse = lse_ref[r * NH + 2 * p + half]
                st = dot_nt(km, q)
                pt = jnp.exp(st - lse)
                dpt = dot_nt(vm, dc)
                inner = jnp.sum(pt * dpt, 0, keepdims=True)
                dst = (pt * (dpt - inner)).astype(BF)
                dvs.append(dot_nn(pt.astype(BF), dc))
                dks.append(dot_nn(dst, q))
                dqs.append(dot_tn(dst, k))
            sel = lane_half(dqs[0].shape, 0)
            dqkv_s[tok, pl.ds(pl.multiple_of(h * LANE, LANE), LANE)] = (jnp.where(sel, dqs[0], dqs[1]) * 0.125).astype(BF)
            dqkv_s[tok, pl.ds(pl.multiple_of(h * LANE + 2 * LANE, LANE), LANE)] = jnp.where(sel, dks[0], dks[1]).astype(BF)
            dqkv_s[tok, pl.ds(pl.multiple_of(h * LANE + 4 * LANE, LANE), LANE)] = jnp.where(sel, dvs[0], dvs[1]).astype(BF)
            tick(NFF + 1 + 5 * g + n)
            tick_counts(NFF + 1 + 5 * g + n)
            return inner_carry

        lax.fori_loop(0, 4, unit, 0)
        slot = (NFF + g) % 2
        grads = dot_nn(a1t_s[...], dqkv_s[...]).astype(BF)
        for b in range(6):
            stage_s[slot, b // NB, b % NB] = grads[:, b * LANE : (b + 1) * LANE]
        for b in range(2):
            stage_s[slot, 1, 2 + b] = gout_s[2 * g + b]
        two = 2 * LANE
        for c in range(3):
            at = pl.ds(pl.multiple_of(c * D + g * two, two), two)
            da1_s[...] += dot_nt(dqkv_s[:, c * two : (c + 1) * two], wqkv_s[:, at])
        here = pl.ds(pl.multiple_of(g * two, two), two)
        part_s[6:7, here] = jnp.sum(dqkv_s[:, 0:two].astype(F32), 0, keepdims=True)
        part_s[7:8, here] = jnp.sum(dqkv_s[:, 2 * two : 3 * two].astype(F32), 0, keepdims=True)
        tick(NFF + 5 + 5 * g)
        tick_counts(NFF + 5 + 5 * g)
        return carry

    lax.fori_loop(0, 3, group, 0)

    for copy in give_back(0, lo_out):
        copy.wait()

    def last_piece(n, carry):
        at = pl.ds(pl.multiple_of(n * step, step), step)
        xhat, rstd = norm_parts(x_s[at].astype(F32))
        da1 = da1_s[at]
        part_s[4:5] += jnp.sum(da1 * xhat, 0, keepdims=True)
        part_s[5:6] += jnp.sum(da1, 0, keepdims=True)
        gm = dx2_s[at] + norm_back(xhat, rstd, g1_ref[...], da1)
        lo_s[n * step // length, pl.ds(pl.multiple_of((n * step) % length, step), step)] = gm.astype(BF)
        return carry

    lax.fori_loop(0, pieces, last_piece, 0)
    for copy in give_back(1, gm_out):
        copy.start()
    vacc_s[0, 0:8] = part_s[...]
    for b in range(FF // (2 * LANE)):
        vacc_s[0, 8 + b // 3 : 9 + b // 3, (b % 3) * 2 * LANE : (b % 3 + 1) * 2 * LANE] = gub_s[:, b * 2 * LANE : (b + 1) * 2 * LANE]
    vacc_s[0, 12:16] = jnp.zeros((4, D), F32)

    def swap(i):
        return pltpu.make_async_remote_copy(src_ref=vacc_s.at[i], dst_ref=vland_s.at[i], send_sem=v_send.at[i], recv_sem=v_recv.at[i],
                                            device_id=across(both[0][i]), device_id_type=MESH)

    def drain(t, carry):
        for i in range(nd + 1):

            @pl.when(t == last_tick + i)
            def _():
                if i > 0:
                    swap(i - 1).wait()
                    vacc_s[i] = vacc_s[i - 1] + vland_s[i - 1]
                if i < nd:
                    swap(i).start()

        tick(t)
        return carry

    end = max(max(out_at) + max(len(plan.gathers) for plan in plans), last_tick + nd) + 1
    lax.fori_loop(last_tick, end, drain, 0)
    vec_out[...] = vacc_s[nd]
    for copy in give_back(1, gm_out):
        copy.wait()


def rear(shape, length, mid, dy, x, qkv, ctx, wup, wdn, wqkv, wout, lse, cnt, g1, b1, g2, b2, ub, db):
    tokens = mid.shape[0]
    nseq = shape["seq"]
    rows = tokens // length
    nd = len(orders(shape)[0])
    vm, hb = pl.BlockSpec(memory_space=pltpu.VMEM), pl.BlockSpec(memory_space=pl.ANY)
    dma = pltpu.SemaphoreType.DMA
    V = pltpu.VMEM
    fc = NB * LANE
    scratch = [
        V((tokens, D), F32), V((tokens, D), BF), V((tokens, D), BF), V((D, tokens), BF), V((D, tokens), BF), V((tokens, D), F32),
        V((tokens, D), F32), V((2, D, fc), BF), V((2, fc, D), BF), V((tokens, 3 * D), BF), V((tokens, D), BF), V((tokens, D), BF),
        V((D, 3 * D), BF), V((D, D), BF), V((tokens, D), BF), V((D // LANE, D, LANE), BF), V((rows, length, D), BF), V((8, D), F32),
        V((1, FF), F32), V((8, D), F32), dma((12,)), V((2, 2, NB, D, LANE), BF), V((nd, 16, D), F32), V((nd + 1, 16, D), F32),
        dma((NPAIR, 2, nd)), dma((NPAIR, 2, nd)), dma((NPAIR, 2, nd)), dma((NPAIR, 2, nd)), dma((NPAIR, 2)),
        dma((nd,)), dma((nd,)), dma((nd,)), dma((nd,)), dma, dma((nd,)), dma((nd,)), dma((2, nseq)), dma((2, nseq)), dma((2,)),
    ]
    scratch += land_shapes((NPAIR, 2), NB, D, 16, nd, BF)
    scratch += land_shapes((), cnt.shape[0], cnt.shape[1], 8, nd, jnp.int32)
    local = length // nseq
    return pl.pallas_call(
        functools.partial(rear_kernel, shape, length),
        in_specs=[hb] * 9 + [vm] * 8,
        out_specs=[hb, hb, hb, hb, vm],
        out_shape=[jax.ShapeDtypeStruct((rows * nseq, local, D), BF), jax.ShapeDtypeStruct((rows * nseq, local, D), BF),
                   jax.ShapeDtypeStruct((NPAIR, 2, NB, D, LANE), BF), jax.ShapeDtypeStruct(cnt.shape, jnp.int32),
                   jax.ShapeDtypeStruct((16, D), F32)],
        scratch_shapes=scratch,
        compiler_params=pltpu.CompilerParams(vmem_limit_bytes=63 * MIB, collective_id=0, has_side_effects=True),
        name="rear",
    )(mid, dy, x, qkv, ctx, wup, wdn, wqkv, wout, lse, cnt, g1, b1, g2, b2, ub, db)


def widen_kernel(turned, src_ref, out_ref):
    for j in range(src_ref.shape[0]):
        at = slice(j * LANE, (j + 1) * LANE)
        if turned:
            out_ref[at, :] = src_ref[j].astype(F32).T
        else:
            out_ref[:, at] = src_ref[j].astype(F32)


def widen(blocks, number, group, where, turned=False):
    wide = group * LANE
    return pl.pallas_call(
        functools.partial(widen_kernel, turned),
        grid=(number,),
        in_specs=[pl.BlockSpec((group, D, LANE), lambda i: (where(i), 0, 0))],
        out_specs=pl.BlockSpec((wide, D), lambda i: (i, 0)) if turned else pl.BlockSpec((D, wide), lambda i: (0, i)),
        out_shape=jax.ShapeDtypeStruct((number * wide, D) if turned else (D, number * wide), F32),
        compiler_params=pltpu.CompilerParams(vmem_limit_bytes=32 * MIB),
        name="widen",
    )(blocks)


def on_device(shape, molecules, ln1_gain, ln1_bias, w_qkv, qkv_bias, w_out, out_bias, ln2_gain, ln2_bias, w_up, up_bias,
              w_down, down_bias, out_cotangent, bucket_ids):
    rows_here, local_len, width = molecules.shape
    length = local_len * shape["seq"]
    row = lambda a: a.reshape(1, -1)
    tally = count(bucket_ids)
    x = lax.all_to_all(molecules, "seq", split_axis=0, concat_axis=1, tiled=True).reshape(-1, width)
    dy = lax.all_to_all(out_cotangent, "seq", split_axis=0, concat_axis=1, tiled=True).reshape(-1, width)
    qb = jnp.concatenate([qkv_bias[0], jnp.zeros((width,), F32), qkv_bias[1]]).reshape(1, -1)
    qkv, lse, ctx, mid = forward(x, row(ln1_gain), row(ln1_bias), w_qkv, qb, w_out, row(out_bias), length)
    layer_out, gm, sums, counts, vec = rear(
        shape, length, mid, dy, x, qkv, ctx, w_up, w_down, w_qkv, w_out, lse, tally, row(ln1_gain), row(ln1_bias),
        row(ln2_gain), row(ln2_bias), row(up_bias), row(down_bias))
    blocks = sums.reshape(-1, D, LANE)
    g_qkv = widen(blocks, 9, 2, lambda i: (NFF + i % 3) * NB + i // 3)
    g_out = widen(blocks, 3, 2, lambda i: (NFF + i) * NB + 3)
    g_up = widen(blocks, NFF, NB, lambda i: 2 * i + 1)
    g_down = widen(blocks, NFF, NB, lambda i: 2 * i, True)
    return (layer_out, gm.astype(F32), vec[4], vec[5], g_qkv, vec[6:8], g_out, vec[3], vec[1], vec[2],
            g_up, vec[8:12].reshape(-1), g_down, vec[0], counts.reshape(bucket_ids.shape[0], BUCKETS))


def solution(mesh):
    tok = P("rows", "seq", None)
    return jax.shard_map(
        functools.partial(on_device, dict(mesh.shape)),
        mesh=mesh,
        in_specs=(tok,) + (P(),) * 12 + (tok, P(None, "rows", "seq")),
        out_specs=(tok, tok) + (P(),) * 13,
        check_vma=False,
    )
```

```python
import functools
import jax
import jax.numpy as jnp
from jax import lax
from jax.experimental import pallas as pl
from jax.experimental.pallas import tpu as pltpu
from jax.sharding import PartitionSpec as P

MESH = pl.DeviceIdType.MESH
BF = jnp.bfloat16
F32 = jnp.float32
EPS = 1e-5
D = 768
HD = 64
NH = 12
FF = 3072
BUCKETS = 16384
LANE = 128
MIB = 1 << 20


def dot_nn(a, b):
    return lax.dot_general(a, b, (((1,), (0,)), ((), ())), preferred_element_type=F32)


def dot_nt(a, b):
    return lax.dot_general(a, b, (((1,), (1,)), ((), ())), preferred_element_type=F32)


def dot_tn(a, b):
    return lax.dot_general(a, b, (((0,), (0,)), ((), ())), preferred_element_type=F32)


def norm_parts(x):
    mean = jnp.mean(x, -1, keepdims=True)
    cen = x - mean
    var = jnp.mean(cen * cen, -1, keepdims=True)
    rstd = lax.rsqrt(var + EPS)
    return cen * rstd, rstd


def norm_back(xhat, rstd, gain, dy):
    dxh = dy * gain
    m1 = jnp.mean(dxh, -1, keepdims=True)
    m2 = jnp.mean(dxh * xhat, -1, keepdims=True)
    return rstd * (dxh - m1 - xhat * m2)


def lane_half(shape, half):
    lane = lax.broadcasted_iota(jnp.int32, shape, 1)
    return (lane < HD) if half == 0 else (lane >= HD)


NB = 4
NFF = FF // (NB * LANE)
NPAIR = NFF + 3


def spots():
    return lax.axis_index("rows"), lax.axis_index("seq")


def bit_of(step):
    axis, mask = step
    return (lax.axis_index(axis) // mask) % 2


def across(step):
    axis, mask = step
    rows, seq = spots()
    move = mask - 2 * mask * bit_of(step)
    return (rows + move, seq) if axis == "rows" else (rows, seq + move)


def orders(shape):
    seq = [("seq", 1 << b) for b in range(shape["seq"].bit_length() - 1)]
    row = [("rows", 1 << b) for b in range(shape["rows"].bit_length() - 1)]
    first, rest, near, far = seq[:1], seq[1:], row[:1], row[1:]
    return first + near + far + rest, first + rest + near + far


class Halving:
    def __init__(self, order, lead, rows, tile):
        self.order, self.tile = order, tile
        self.size, self.split, self.lead_at, self.row_at, self.own = [], [], [], [], []
        lead_at, row_at = 0, 0
        for i, step in enumerate(order):
            bit = bit_of(step)
            if lead > 1:
                lead //= 2
                how = 0
                if i == 0:
                    self.first = bit * lead
                else:
                    lead_at = lead_at + bit * lead
            elif rows % (2 * tile) == 0:
                rows //= 2
                how = 1
                row_at = row_at + bit * rows
            else:
                how = None
            self.own.append(bit)
            self.split.append(how)
            self.size.append((lead, rows))
            self.lead_at.append(lead_at)
            self.row_at.append(row_at)
        self.gathers = [i for i in reversed(range(len(order))) if self.split[i] is not None]

    def partner(self, i):
        return across(self.order[i])

    def rows_of(self, at, size):
        return pl.ds(pl.multiple_of(at, self.tile), size)

    def send(self, i, mine, land, sems):
        lead, rows = self.size[i]
        if i == 0:
            src = mine.at[pl.ds(lead - self.first, lead)]
        else:
            la, ra = self.lead_at[i - 1], self.row_at[i - 1]
            if self.split[i] == 0:
                la = la + (1 - self.own[i]) * lead
            elif self.split[i] == 1:
                ra = ra + (1 - self.own[i]) * rows
            src = land[0].at[pl.ds(la, lead), self.rows_of(ra, rows)]
        return pltpu.make_async_remote_copy(src_ref=src, dst_ref=land[i], send_sem=sems[0].at[i], recv_sem=sems[1].at[i],
                                            device_id=self.partner(i), device_id_type=MESH)

    def add(self, i, mine, land):
        lead, rows = self.size[i]
        part = rows if rows <= LANE else 96
        wide = F32 if land[0].dtype == BF else land[0].dtype

        def some(t, carry):
            at = t * part
            if i == 0:
                here = (slice(None), self.rows_of(at, part))
                left, right = land[0][here], mine[pl.ds(self.first, lead), self.rows_of(at, part)]
            else:
                here = (pl.ds(self.lead_at[i], lead), self.rows_of(self.row_at[i] + at, part))
                left, right = land[0][here], land[i][:, self.rows_of(at, part)]
            land[0][here] = (left.astype(wide) + right.astype(wide)).astype(land[0].dtype)
            return carry

        lax.fori_loop(0, rows // part, some, 0)

    def at_level(self, i):
        lead, rows = self.size[i]
        return pl.ds(self.lead_at[i], lead), self.rows_of(self.row_at[i], rows)

    def out_level(self, i):
        lead, rows = self.size[i]
        return pl.ds(self.first + self.lead_at[i], lead), self.rows_of(self.row_at[i], rows)

    def keep(self, land, out, sem):
        last = len(self.order) - 1
        return pltpu.make_async_copy(land[0].at[self.at_level(last)], out.at[self.out_level(last)], sem)

    def gather(self, m, land, out, sems):
        i = self.gathers[m]
        here = out.at[self.out_level(i)]
        src = land[0].at[self.at_level(len(self.order) - 1)] if m == 0 else here
        return pltpu.make_async_remote_copy(src_ref=src, dst_ref=here, send_sem=sems[0].at[m], recv_sem=sems[1].at[m],
                                            device_id=self.partner(i), device_id_type=MESH)

    def reduce_step(self, k, mine, land, sems):
        n = len(self.order)
        if k > 0:
            self.send(k - 1, mine, land, sems).wait()
            self.add(k - 1, mine, land)
        if k < n:
            self.send(k, mine, land, sems).start()

    def gather_step(self, m, land, out, sems, sem):
        if m == 0:
            self.keep(land, out, sem).start()
        else:
            if m == 1:
                self.keep(land, out, sem).wait()
            self.gather(m - 1, land, out, sems).wait()
        if m < len(self.gathers):
            self.gather(m, land, out, sems).start()


def land_shapes(count, lead, rows, tile, steps, dtype):
    shapes = []
    for _ in range(steps):
        if lead > 1:
            lead //= 2
        elif rows % (2 * tile) == 0:
            rows //= 2
        shapes.append(pltpu.VMEM(count + (lead, rows, LANE), dtype))
    return shapes


def peers(nseq):
    me = lax.axis_index("seq")
    found = []
    for m in sorted(range(1, nseq), key=lambda m: -(m >> 1)):
        to = 0
        for b in range(nseq.bit_length() - 1):
            bit = (me // (1 << b)) % 2
            to = to + (bit + ((m >> b) & 1) * (1 - 2 * bit)) * (1 << b)
        found.append((m, to))
    return found


def front_kernel(shape, mol_h, cot_h, wqkv_h, wout_h, ids_ref, g1_ref, b1_ref, qb_ref, ob_ref,
                 x_out, dy_out, qkv_out, ctx_out, mid_out, lse_ref, cnt_ref,
                 xs, qkv_s, ctx_s, mid_s, wqkv_s, wout_s, lacc,
                 w_sem, m_send, m_recv, m_own, c_send, c_recv, c_own, o_sem):
    nseq = shape["seq"]
    rows, length = xs.shape[0], xs.shape[1]
    local = length // nseq
    rows_idx, me = spots()
    near = peers(nseq)

    barrier = pltpu.get_barrier_semaphore()
    for _, to in near:
        pl.semaphore_signal(barrier, inc=1, device_id=(rows_idx, to), device_id_type=MESH)
    fetch = [pltpu.make_async_copy(wqkv_h, wqkv_s, w_sem.at[0]), pltpu.make_async_copy(wout_h, wout_s, w_sem.at[1])]
    here = pl.ds(pl.multiple_of(me * local, local), local)

    def own(r):
        return pltpu.make_async_copy(mol_h.at[me * rows + r], xs.at[r, here], m_own.at[r])

    def mol(r, n):
        m, to = near[n]
        return pltpu.make_async_remote_copy(src_ref=mol_h.at[to * rows + r], dst_ref=xs.at[r, here], send_sem=m_send.at[r, m],
                                            recv_sem=m_recv.at[r, m], device_id=(rows_idx, to), device_id_type=MESH)

    def cot(n):
        m, to = near[n]
        return pltpu.make_async_remote_copy(src_ref=cot_h.at[pl.ds(to * rows, rows)], dst_ref=dy_out.at[:, here],
                                            send_sem=c_send.at[m], recv_sem=c_recv.at[m], device_id=(rows_idx, to),
                                            device_id_type=MESH)

    cot_own = pltpu.make_async_copy(cot_h.at[pl.ds(me * rows, rows)], dy_out.at[:, here], c_own)

    for r in range(rows):
        own(r).start()
    fetch[0].start()
    pl.semaphore_wait(barrier, len(near))
    for r in range(rows):
        for n in range(len(near)):
            mol(r, n).start()
    fetch[1].start()
    cot_own.start()

    half = 2 * local

    def project(r, at):
        src = pl.ds(pl.multiple_of(at, half), half)
        dst = pl.ds(pl.multiple_of(r * length + at, half), half)
        xhat, _ = norm_parts(xs[r, src].astype(F32))
        a1 = (xhat * g1_ref[...] + b1_ref[...]).astype(BF)
        for c in range(3):
            cols = slice(c * D, (c + 1) * D)
            qkv_s[dst, cols] = (dot_nn(a1, wqkv_s[:, cols]) + qb_ref[:, cols]).astype(BF)

    for r in range(rows):
        own(r).wait()
        mol(r, len(near) - 1).wait()
    fetch[0].wait()
    mine = (me // 2) * half

    def early(r, carry):
        project(r, mine)
        return carry

    lax.fori_loop(0, rows, early, 0)

    hashes, id_rows, chars = ids_ref.shape
    high = BUCKETS // LANE

    def tally(h, carry):
        total = jnp.zeros((high, LANE), F32)
        for r in range(id_rows):
            ids = ids_ref[h, r : r + 1, :]
            row = lax.broadcasted_iota(jnp.int32, (high, chars), 0)
            hi = jnp.where(row == (ids >> 7), 1.0, 0.0).astype(BF)
            lo = jnp.where(row == (ids & (LANE - 1)), 1.0, 0.0).astype(BF)
            total = total + dot_nt(hi, lo)
        cnt_ref[h] = total.astype(jnp.int32)
        return carry

    lax.fori_loop(0, hashes, tally, 0)
    fetch[1].wait()

    def outs(r):
        at = pl.ds(r * length, length)
        return [pltpu.make_async_copy(xs.at[r], x_out.at[r], o_sem.at[r, 0]),
                pltpu.make_async_copy(qkv_s.at[at], qkv_out.at[at], o_sem.at[r, 1]),
                pltpu.make_async_copy(ctx_s.at[at], ctx_out.at[at], o_sem.at[r, 2]),
                pltpu.make_async_copy(mid_s.at[at], mid_out.at[at], o_sem.at[r, 3])]

    for r in range(rows):
        for n in range(len(near) - 1):
            mol(r, n).wait()
        for other in range(1, nseq // 2):
            project(r, ((me // 2 + other) % (nseq // 2)) * half)
        ready = outs(r)
        ready[0].start()
        ready[1].start()
        tok = slice(r * length, (r + 1) * length)

        def pair(p, carry):
            at = pl.multiple_of(p * LANE, LANE)
            q = qkv_s[tok, pl.ds(at, LANE)] * BF(0.125)
            k = qkv_s[tok, pl.ds(pl.multiple_of(D + at, LANE), LANE)]
            v = qkv_s[tok, pl.ds(pl.multiple_of(2 * D + at, LANE), LANE)]
            ctx = []
            lse = lacc[...]
            lane = lax.broadcasted_iota(jnp.int32, lse.shape, 1)
            for half_of in range(2):
                qm = jnp.where(lane_half(q.shape, half_of), q, BF(0))
                s = dot_nt(qm, k)
                m = jnp.max(s, -1, keepdims=True)
                e = jnp.exp(s - m)
                t = jnp.sum(e, -1, keepdims=True)
                pr = (e * (1.0 / t)).astype(BF)
                ctx.append(dot_nn(pr, v))
                lse = jnp.where(lane == 2 * p + half_of, m + jnp.log(t), lse)
            lacc[...] = lse
            ctx_s[tok, pl.ds(at, LANE)] = jnp.where(lane_half(ctx[0].shape, 0), ctx[0], ctx[1]).astype(BF)
            if r == 0:

                @pl.when(p == 3)
                def _():
                    for n in range(len(near)):
                        cot(n).start()

            return carry

        lacc[...] = jnp.zeros_like(lacc)
        lax.fori_loop(0, NH // 2, pair, 0)
        ready[2].start()
        lt = lacc[...].T
        for h in range(NH):
            lse_ref[r * NH + h] = lt[h : h + 1, :]
        mid_s[tok] = xs[r].astype(F32) + (dot_nn(ctx_s[tok], wout_s[...]) + ob_ref[...])
        ready[3].start()
    for r in range(rows):
        for copy in outs(r):
            copy.wait()
    cot_own.wait()
    for n in range(len(near)):
        cot(n).wait()


def front(shape, mol, cot, wqkv, wout, ids, g1, b1, qb, ob):
    nseq = shape["seq"]
    rows, length = mol.shape[0] // nseq, mol.shape[1] * nseq
    tokens = rows * length
    vm, hb = pl.BlockSpec(memory_space=pltpu.VMEM), pl.BlockSpec(memory_space=pl.ANY)
    dma = pltpu.SemaphoreType.DMA
    sds = jax.ShapeDtypeStruct
    return pl.pallas_call(
        functools.partial(front_kernel, shape),
        in_specs=[hb] * 4 + [vm] * 5,
        out_specs=[hb] * 5 + [vm] * 2,
        out_shape=[sds((rows, length, D), BF), sds((rows, length, D), BF), sds((tokens, 3 * D), BF), sds((tokens, D), BF),
                   sds((tokens, D), F32), sds((rows * NH, 1, length), F32), sds((ids.shape[0], BUCKETS // LANE, LANE), jnp.int32)],
        scratch_shapes=[pltpu.VMEM((rows, length, D), BF), pltpu.VMEM((tokens, 3 * D), BF), pltpu.VMEM((tokens, D), BF),
                        pltpu.VMEM((tokens, D), F32), pltpu.VMEM((D, 3 * D), BF), pltpu.VMEM((D, D), BF),
                        pltpu.VMEM((length, LANE), F32), dma((2,)), dma((rows, nseq)), dma((rows, nseq)), dma((rows,)),
                        dma((nseq,)), dma((nseq,)), dma, dma((rows, 4))],
        compiler_params=pltpu.CompilerParams(vmem_limit_bytes=60 * MIB, collective_id=1, has_side_effects=True),
        name="front",
    )(mol, cot, wqkv, wout, ids, g1, b1, qb, ob)


GAP_IN, GAP_OUT, GAP = 3, 3, 2
IN_AT = tuple(2 * j + 1 for j in range(NFF)) + (2 * NFF + 6, 2 * NFF + 11, 2 * NFF + 16)
AG_AT = (16, 18, 22, 24, 26, 28, 33, 38, 43)
DRAIN = 2 * NFF + 17


def rear_kernel(shape, length, mid_h, dy_h, x_h, qkv_h, ctx_h, wup_h, wdn_h, wqkv_h, wout_h, lse_ref, cnt_ref,
                g1_ref, b1_ref, g2_ref, b2_ref, ub_ref, db_ref,
                lo_out, gm_out, sum_out, cnt_out, vec_out,
                mid_s, dy_s, a2_s, a2t_s, dyt_s, acc_s, da2_s, wup_s, wdn_s, qkv_s, ctx_s, x_s, wqkv_s, wout_s,
                dqkv_s, gout_s, lo_s, vec_s, gub_s, part_s, fetch_sem, stage_s, vland_s, vacc_s,
                rs_send, rs_recv, ag_send, ag_recv, keep_sem, crs_send, crs_recv, cag_send, cag_recv, ckeep_sem,
                v_send, v_recv, t_send, t_recv, t_own, *lands):
    both = orders(shape)
    nd = len(both[0])
    nseq = shape["seq"]
    land = lands[:nd]
    cland = lands[nd:]
    rows_idx, me = spots()
    tokens = mid_s.shape[0]
    rows = tokens // length
    local = length // nseq
    fc = NB * LANE

    barrier = pltpu.get_barrier_semaphore()
    others = [across(step) for step in both[0]]
    for m in range(3, nseq):
        if m & (m - 1):
            others.append((rows_idx, sum(((me // (1 << b)) % 2 + ((m >> b) & 1) * (1 - 2 * ((me // (1 << b)) % 2))) * (1 << b)
                                         for b in range(nseq.bit_length() - 1))))
    for other in others:
        pl.semaphore_signal(barrier, inc=1, device_id=other, device_id_type=MESH)

    def fetch(t):
        return pltpu.make_async_copy((mid_h, dy_h, x_h, qkv_h, ctx_h, wqkv_h, wout_h)[t],
                                     (mid_s, dy_s, x_s, qkv_s, ctx_s, wqkv_s, wout_s)[t], fetch_sem.at[t])

    def weights(i, slot):
        return (pltpu.make_async_copy(wup_h.at[:, pl.ds(pl.multiple_of(i * fc, fc), fc)], wup_s.at[slot], fetch_sem.at[8 + slot]),
                pltpu.make_async_copy(wdn_h.at[pl.ds(pl.multiple_of(i * fc, fc), fc)], wdn_s.at[slot], fetch_sem.at[10 + slot]))

    fetch(0).start()
    fetch(1).start()
    for copy in weights(0, 0):
        copy.start()
    pl.semaphore_wait(barrier, len(others))

    def plans(j):
        return [Halving(order, NB, D, 16) for order in both]

    tally = Halving(both[0], cnt_ref.shape[0], cnt_ref.shape[1], 8)
    most = len(Halving(both[0], NB, D, 16).gathers)
    out_at = []
    for a, b in zip(AG_AT, IN_AT):
        out_at.append(max(a, b + GAP_IN * nd, out_at[-1] + 1 if out_at else 0))

    def tick(t):
        for k in reversed(range(nd + 1)):
            hit = sum(jnp.where(t == IN_AT[j] + GAP_IN * k, 1, 0) for j in range(NPAIR))
            j = sum(jnp.where(t == IN_AT[j] + GAP_IN * k, j, 0) for j in range(NPAIR))

            @pl.when(hit == 1)
            def _():
                for o, plan in enumerate(plans(j)):
                    plan.reduce_step(k, stage_s.at[j % 2, o], [r.at[j, o] for r in land], (rs_send.at[j, o], rs_recv.at[j, o]))

        for m in reversed(range(most + 1)):
            hit = sum(jnp.where(t == out_at[j] + GAP_OUT * m, 1, 0) for j in range(NPAIR))
            j = sum(jnp.where(t == out_at[j] + GAP_OUT * m, j, 0) for j in range(NPAIR))

            @pl.when(hit == 1)
            def _():
                for o, plan in enumerate(plans(j)):
                    plan.gather_step(m, [r.at[j, o] for r in land], sum_out.at[j, o], (ag_send.at[j, o], ag_recv.at[j, o]),
                                     keep_sem.at[j, o])

    def tick_counts(t):
        for k in range(nd + 1):

            @pl.when(t == GAP * k)
            def _():
                tally.reduce_step(k, cnt_ref, cland, (crs_send, crs_recv))

        for m in range(len(tally.gathers) + 1):

            @pl.when(t == GAP * (nd + 1 + m))
            def _():
                tally.gather_step(m, cland, cnt_out, (cag_send, cag_recv), ckeep_sem)

    def give_back(which, out):
        copies = []
        for m in range(1, nseq):
            bits = [(me // (1 << b)) % 2 for b in range(nseq.bit_length() - 1)]
            to = sum((bit + ((m >> b) & 1) * (1 - 2 * bit)) * (1 << b) for b, bit in enumerate(bits))
            copies.append(pltpu.make_async_remote_copy(
                src_ref=lo_s.at[:, pl.ds(pl.multiple_of(to * local, local), local)], dst_ref=out.at[pl.ds(me * rows, rows)],
                send_sem=t_send.at[which, m], recv_sem=t_recv.at[which, m], device_id=(rows_idx, to), device_id_type=MESH))
        copies.append(pltpu.make_async_copy(lo_s.at[:, pl.ds(pl.multiple_of(me * local, local), local)],
                                            out.at[pl.ds(me * rows, rows)], t_own.at[which]))
        return copies

    step = 256
    pieces = tokens // step
    fetch(0).wait()
    fetch(1).wait()
    for t in (6, 4, 2, 3, 5):
        fetch(t).start()

    def open_piece(n, carry):
        at = pl.ds(pl.multiple_of(n * step, step), step)
        mid = mid_s[at]
        xhat, _ = norm_parts(mid)
        a2 = (xhat * g2_ref[...] + b2_ref[...]).astype(BF)
        a2_s[at] = a2
        a2t_s[:, at] = a2.T
        dyt_s[:, at] = dy_s[at].T
        acc_s[at] = mid + db_ref[...]
        da2_s[at] = jnp.zeros((step, D), F32)
        return carry

    lax.fori_loop(0, pieces, open_piece, 0)

    def ff(i, carry):
        slot = i % 2

        @pl.when(i + 1 < NFF)
        def _():
            for copy in weights(i + 1, 1 - slot):
                copy.start()

        for copy in weights(i, slot):
            copy.wait()
        cols = pl.ds(pl.multiple_of(i * fc, fc), fc)
        u = dot_nn(a2_s[...], wup_s[slot]) + ub_ref[:, cols]
        dh = dot_nt(dy_s[...], wdn_s[slot])
        cdf = 0.5 + 0.5 * lax.erf(u * (2.0 ** -0.5))
        pdf = jnp.exp(u * u * -0.5) * 0.3989422804014327
        hid = (u * cdf).astype(BF)
        du = (dh * (cdf + u * pdf)).astype(BF)
        gub_s[:, cols] = jnp.sum(du.astype(F32), 0, keepdims=True)
        tick(2 * i)
        tick_counts(2 * i)
        acc_s[...] += dot_nn(hid, wdn_s[slot])
        da2_s[...] += dot_nt(du, wup_s[slot])
        gd = dot_nn(dyt_s[...], hid).astype(BF)
        gu = dot_nn(a2t_s[...], du).astype(BF)
        for b in range(NB):
            stage_s[slot, 0, b] = gd[:, b * LANE : (b + 1) * LANE]
            stage_s[slot, 1, b] = gu[:, b * LANE : (b + 1) * LANE]
        tick(2 * i + 1)
        tick_counts(2 * i + 1)
        return carry

    lax.fori_loop(0, NFF, ff, 0)

    part_s[...] = jnp.zeros_like(part_s)
    fetch(6).wait()

    def turn_piece(n, carry):
        at = pl.ds(pl.multiple_of(n * step, step), step)
        lo_s[n * step // length, pl.ds(pl.multiple_of((n * step) % length, step), step)] = acc_s[at].astype(BF)
        dy = dy_s[at].astype(F32)
        xhat, rstd = norm_parts(mid_s[at])
        da2 = da2_s[at]
        dx2 = dy + norm_back(xhat, rstd, g2_ref[...], da2)
        da2_s[at] = dx2
        do = dx2.astype(BF)
        a2_s[at] = do
        part_s[0:1] += jnp.sum(dy, 0, keepdims=True)
        part_s[1:2] += jnp.sum(da2 * xhat, 0, keepdims=True)
        part_s[2:3] += jnp.sum(da2, 0, keepdims=True)
        part_s[3:4] += jnp.sum(do.astype(F32), 0, keepdims=True)
        dy_s[at] = dot_nt(do, wout_s[...]).astype(BF)
        return carry

    lax.fori_loop(0, pieces, turn_piece, 0)
    dctx_s, do_s, dx2_s, da1_s, a1t_s = dy_s, a2_s, da2_s, acc_s, a2t_s
    for copy in give_back(0, lo_out):
        copy.start()
    tick(2 * NFF)
    tick_counts(2 * NFF)
    fetch(4).wait()
    fetch(2).wait()
    gout = dot_tn(ctx_s[...], do_s[...]).astype(BF)
    for b in range(D // LANE):
        gout_s[b] = gout[:, b * LANE : (b + 1) * LANE]

    def first_norm(n, carry):
        at = pl.ds(pl.multiple_of(n * step, step), step)
        xhat, _ = norm_parts(x_s[at].astype(F32))
        a1t_s[:, at] = (xhat * g1_ref[...] + b1_ref[...]).astype(BF).T
        da1_s[at] = jnp.zeros((step, D), F32)
        return carry

    lax.fori_loop(0, pieces, first_norm, 0)
    fetch(3).wait()
    fetch(5).wait()
    tick(2 * NFF + 1)
    tick_counts(2 * NFF + 1)

    def group(g, carry):
        def unit(n, inner_carry):
            r = n // 2
            h = n % 2
            p = 2 * g + h
            tok = pl.ds(pl.multiple_of(r * length, length), length)
            cq = pl.ds(pl.multiple_of(p * LANE, LANE), LANE)
            q = qkv_s[tok, cq] * BF(0.125)
            k = qkv_s[tok, pl.ds(pl.multiple_of(p * LANE + D, LANE), LANE)]
            v = qkv_s[tok, pl.ds(pl.multiple_of(p * LANE + 2 * D, LANE), LANE)]
            dc = dctx_s[tok, cq]
            dqs, dks, dvs = [], [], []
            for half in range(2):
                keep = lane_half(k.shape, half)
                km = jnp.where(keep, k, BF(0))
                vm = jnp.where(keep, v, BF(0))
                lse = lse_ref[r * NH + 2 * p + half]
                st = dot_nt(km, q)
                pt = jnp.exp(st - lse)
                dpt = dot_nt(vm, dc)
                inner = jnp.sum(pt * dpt, 0, keepdims=True)
                dst = (pt * (dpt - inner)).astype(BF)
                dvs.append(dot_nn(pt.astype(BF), dc))
                dks.append(dot_nn(dst, q))
                dqs.append(dot_tn(dst, k))
            sel = lane_half(dqs[0].shape, 0)
            dqkv_s[tok, pl.ds(pl.multiple_of(h * LANE, LANE), LANE)] = (jnp.where(sel, dqs[0], dqs[1]) * 0.125).astype(BF)
            dqkv_s[tok, pl.ds(pl.multiple_of(h * LANE + 2 * LANE, LANE), LANE)] = jnp.where(sel, dks[0], dks[1]).astype(BF)
            dqkv_s[tok, pl.ds(pl.multiple_of(h * LANE + 4 * LANE, LANE), LANE)] = jnp.where(sel, dvs[0], dvs[1]).astype(BF)
            tick(2 * NFF + 2 + 5 * g + n)
            tick_counts(2 * NFF + 2 + 5 * g + n)
            return inner_carry

        lax.fori_loop(0, 4, unit, 0)
        slot = (NFF + g) % 2
        grads = dot_nn(a1t_s[...], dqkv_s[...]).astype(BF)
        for b in range(6):
            stage_s[slot, b // NB, b % NB] = grads[:, b * LANE : (b + 1) * LANE]
        for b in range(2):
            stage_s[slot, 1, 2 + b] = gout_s[2 * g + b]
        two = 2 * LANE
        for c in range(3):
            at = pl.ds(pl.multiple_of(c * D + g * two, two), two)
            da1_s[...] += dot_nt(dqkv_s[:, c * two : (c + 1) * two], wqkv_s[:, at])
        here = pl.ds(pl.multiple_of(g * two, two), two)
        part_s[6:7, here] = jnp.sum(dqkv_s[:, 0:two].astype(F32), 0, keepdims=True)
        part_s[7:8, here] = jnp.sum(dqkv_s[:, 2 * two : 3 * two].astype(F32), 0, keepdims=True)
        tick(2 * NFF + 6 + 5 * g)
        tick_counts(2 * NFF + 6 + 5 * g)
        return carry

    lax.fori_loop(0, 3, group, 0)

    for copy in give_back(0, lo_out):
        copy.wait()

    def last_piece(n, carry):
        at = pl.ds(pl.multiple_of(n * step, step), step)
        xhat, rstd = norm_parts(x_s[at].astype(F32))
        da1 = da1_s[at]
        part_s[4:5] += jnp.sum(da1 * xhat, 0, keepdims=True)
        part_s[5:6] += jnp.sum(da1, 0, keepdims=True)
        gm = dx2_s[at] + norm_back(xhat, rstd, g1_ref[...], da1)
        lo_s[n * step // length, pl.ds(pl.multiple_of((n * step) % length, step), step)] = gm.astype(BF)
        return carry

    lax.fori_loop(0, pieces, last_piece, 0)
    for copy in give_back(1, gm_out):
        copy.start()
    vacc_s[0, 0:8] = part_s[...]
    for b in range(FF // (2 * LANE)):
        vacc_s[0, 8 + b // 3 : 9 + b // 3, (b % 3) * 2 * LANE : (b % 3 + 1) * 2 * LANE] = gub_s[:, b * 2 * LANE : (b + 1) * 2 * LANE]
    vacc_s[0, 12:16] = jnp.zeros((4, D), F32)

    def swap(i):
        return pltpu.make_async_remote_copy(src_ref=vacc_s.at[i], dst_ref=vland_s.at[i], send_sem=v_send.at[i], recv_sem=v_recv.at[i],
                                            device_id=across(both[0][i]), device_id_type=MESH)

    def drain(t, carry):
        for i in range(nd + 1):

            @pl.when(t == DRAIN + GAP * i)
            def _():
                if i > 0:
                    swap(i - 1).wait()
                    vacc_s[i] = vacc_s[i - 1] + vland_s[i - 1]
                if i < nd:
                    swap(i).start()

        tick(t)
        return carry

    end = max(max(out_at) + GAP_OUT * most, DRAIN + GAP * nd) + 1
    lax.fori_loop(DRAIN, end, drain, 0)
    vec_out[...] = vacc_s[nd]
    for copy in give_back(1, gm_out):
        copy.wait()


def rear(shape, length, mid, dy, x, qkv, ctx, wup, wdn, wqkv, wout, lse, cnt, g1, b1, g2, b2, ub, db):
    tokens = mid.shape[0]
    nseq = shape["seq"]
    rows = tokens // length
    nd = len(orders(shape)[0])
    vm, hb = pl.BlockSpec(memory_space=pltpu.VMEM), pl.BlockSpec(memory_space=pl.ANY)
    dma = pltpu.SemaphoreType.DMA
    V = pltpu.VMEM
    fc = NB * LANE
    scratch = [
        V((tokens, D), F32), V((tokens, D), BF), V((tokens, D), BF), V((D, tokens), BF), V((D, tokens), BF), V((tokens, D), F32),
        V((tokens, D), F32), V((2, D, fc), BF), V((2, fc, D), BF), V((tokens, 3 * D), BF), V((tokens, D), BF), V((tokens, D), BF),
        V((D, 3 * D), BF), V((D, D), BF), V((tokens, D), BF), V((D // LANE, D, LANE), BF), V((rows, length, D), BF), V((8, D), F32),
        V((1, FF), F32), V((8, D), F32), dma((12,)), V((2, 2, NB, D, LANE), BF), V((nd, 16, D), F32), V((nd + 1, 16, D), F32),
        dma((NPAIR, 2, nd)), dma((NPAIR, 2, nd)), dma((NPAIR, 2, nd)), dma((NPAIR, 2, nd)), dma((NPAIR, 2)),
        dma((nd,)), dma((nd,)), dma((nd,)), dma((nd,)), dma, dma((nd,)), dma((nd,)), dma((2, nseq)), dma((2, nseq)), dma((2,)),
    ]
    scratch += land_shapes((NPAIR, 2), NB, D, 16, nd, BF)
    scratch += land_shapes((), cnt.shape[0], cnt.shape[1], 8, nd, jnp.int32)
    local = length // nseq
    return pl.pallas_call(
        functools.partial(rear_kernel, shape, length),
        in_specs=[hb] * 9 + [vm] * 8,
        out_specs=[hb, hb, hb, hb, vm],
        out_shape=[jax.ShapeDtypeStruct((rows * nseq, local, D), BF), jax.ShapeDtypeStruct((rows * nseq, local, D), BF),
                   jax.ShapeDtypeStruct((NPAIR, 2, NB, D, LANE), BF), jax.ShapeDtypeStruct(cnt.shape, jnp.int32),
                   jax.ShapeDtypeStruct((16, D), F32)],
        scratch_shapes=scratch,
        compiler_params=pltpu.CompilerParams(vmem_limit_bytes=63 * MIB, collective_id=0, has_side_effects=True),
        name="rear",
    )(mid, dy, x, qkv, ctx, wup, wdn, wqkv, wout, lse, cnt, g1, b1, g2, b2, ub, db)


def widen_kernel(src_ref, gm_ref, gmol_ref, qkv_out, out_out, up_out, down_out, wide_s, tall_s, sem):
    j = pl.program_id(0)
    slot = j % 2
    fc = NB * LANE
    two = 2 * LANE

    def first(i, s):
        at = pl.ds(pl.multiple_of(i * fc, fc), fc)
        return [pltpu.make_async_copy(tall_s.at[s], down_out.at[at], sem.at[s, 0]),
                pltpu.make_async_copy(wide_s.at[s, 0], up_out.at[:, at], sem.at[s, 1])]

    def later(i, s):
        g = i - NFF
        to = lambda c: pl.ds(pl.multiple_of(c * D + g * two, two), two)
        return [pltpu.make_async_copy(wide_s.at[s, 0, :, 0:two], qkv_out.at[:, to(0)], sem.at[s, 0]),
                pltpu.make_async_copy(wide_s.at[s, 0, :, two : 2 * two], qkv_out.at[:, to(1)], sem.at[s, 1]),
                pltpu.make_async_copy(wide_s.at[s, 1, :, 0:two], qkv_out.at[:, to(2)], sem.at[s, 2]),
                pltpu.make_async_copy(wide_s.at[s, 1, :, two : 2 * two], out_out.at[:, to(0)], sem.at[s, 3])]

    def finish(i, s):
        @pl.when(i < NFF)
        def _():
            for copy in first(i, s):
                copy.wait()

        @pl.when(i >= NFF)
        def _():
            for copy in later(i, s):
                copy.wait()

    @pl.when(j >= 2)
    def _():
        finish(j - 2, slot)

    gmol_ref[...] = gm_ref[...].astype(F32)

    @pl.when(j < NFF)
    def _():
        for b in range(NB):
            at = slice(b * LANE, (b + 1) * LANE)
            tall_s[slot, at, :] = src_ref[0, 0, b].astype(F32).T
            wide_s[slot, 0, :, at] = src_ref[0, 1, b].astype(F32)
        for copy in first(j, slot):
            copy.start()

    @pl.when(j >= NFF)
    def _():
        for o in range(2):
            for b in range(NB):
                wide_s[slot, o, :, b * LANE : (b + 1) * LANE] = src_ref[0, o, b].astype(F32)
        for copy in later(j, slot):
            copy.start()

    @pl.when(j == NPAIR - 1)
    def _():
        finish(j - 1, 1 - slot)
        finish(j, slot)


def widen(sums, gm):
    hb = pl.BlockSpec(memory_space=pl.ANY)
    sds = jax.ShapeDtypeStruct
    rows = gm.shape[0]
    some = pl.BlockSpec((1,) + gm.shape[1:], lambda j: (jnp.minimum(j, rows - 1), 0, 0))
    return pl.pallas_call(
        widen_kernel,
        grid=(NPAIR,),
        in_specs=[pl.BlockSpec((1, 2, NB, D, LANE), lambda j: (j, 0, 0, 0, 0)), some],
        out_specs=[some, hb, hb, hb, hb],
        out_shape=[sds(gm.shape, F32), sds((D, 3 * D), F32), sds((D, D), F32), sds((D, FF), F32), sds((FF, D), F32)],
        scratch_shapes=[pltpu.VMEM((2, 2, D, NB * LANE), F32), pltpu.VMEM((2, NB * LANE, D), F32), pltpu.SemaphoreType.DMA((2, 4))],
        compiler_params=pltpu.CompilerParams(vmem_limit_bytes=60 * MIB),
        name="widen",
    )(sums, gm)


def on_device(shape, molecules, ln1_gain, ln1_bias, w_qkv, qkv_bias, w_out, out_bias, ln2_gain, ln2_bias, w_up, up_bias,
              w_down, down_bias, out_cotangent, bucket_ids):
    width = molecules.shape[2]
    length = molecules.shape[1] * shape["seq"]
    row = lambda a: a.reshape(1, -1)
    qb = jnp.concatenate([qkv_bias[0], jnp.zeros((width,), F32), qkv_bias[1]]).reshape(1, -1)
    x, dy, qkv, ctx, mid, lse, tally = front(shape, molecules, out_cotangent, w_qkv, w_out, bucket_ids, row(ln1_gain),
                                             row(ln1_bias), qb, row(out_bias))
    layer_out, gm, sums, counts, vec = rear(
        shape, length, mid, dy.reshape(-1, width), x.reshape(-1, width), qkv, ctx, w_up, w_down, w_qkv, w_out, lse, tally,
        row(ln1_gain), row(ln1_bias), row(ln2_gain), row(ln2_bias), row(up_bias), row(down_bias))
    g_mol, g_qkv, g_out, g_up, g_down = widen(sums, gm)
    return (layer_out, g_mol, vec[4], vec[5], g_qkv, vec[6:8], g_out, vec[3], vec[1], vec[2],
            g_up, vec[8:12].reshape(-1), g_down, vec[0], counts.reshape(bucket_ids.shape[0], BUCKETS))


def solution(mesh):
    tok = P("rows", "seq", None)
    return jax.shard_map(
        functools.partial(on_device, dict(mesh.shape)),
        mesh=mesh,
        in_specs=(tok,) + (P(),) * 12 + (tok, P(None, "rows", "seq")),
        out_specs=(tok, tok) + (P(),) * 13,
        check_vma=False,
    )
```

```python
import functools
import jax
import jax.numpy as jnp
from jax import lax
from jax.experimental import pallas as pl
from jax.experimental.pallas import tpu as pltpu
from jax.sharding import PartitionSpec as P

MESH = pl.DeviceIdType.MESH
BF = jnp.bfloat16
F32 = jnp.float32
EPS = 1e-5
D = 768
HD = 64
NH = 12
FF = 3072
BUCKETS = 16384
LANE = 128
MIB = 1 << 20


def dot_nn(a, b):
    return lax.dot_general(a, b, (((1,), (0,)), ((), ())), preferred_element_type=F32)


def dot_nt(a, b):
    return lax.dot_general(a, b, (((1,), (1,)), ((), ())), preferred_element_type=F32)


def dot_tn(a, b):
    return lax.dot_general(a, b, (((0,), (0,)), ((), ())), preferred_element_type=F32)


def norm_parts(x):
    mean = jnp.mean(x, -1, keepdims=True)
    cen = x - mean
    var = jnp.mean(cen * cen, -1, keepdims=True)
    rstd = lax.rsqrt(var + EPS)
    return cen * rstd, rstd


def norm_back(xhat, rstd, gain, dy):
    dxh = dy * gain
    m1 = jnp.mean(dxh, -1, keepdims=True)
    m2 = jnp.mean(dxh * xhat, -1, keepdims=True)
    return rstd * (dxh - m1 - xhat * m2)


def lane_half(shape, half):
    lane = lax.broadcasted_iota(jnp.int32, shape, 1)
    return (lane < HD) if half == 0 else (lane >= HD)


NB = 4
NFF = FF // (NB * LANE)
NPAIR = NFF + 3


def spots():
    return lax.axis_index("rows"), lax.axis_index("seq")


def bit_of(step):
    axis, mask = step
    return (lax.axis_index(axis) // mask) % 2


def across(step):
    axis, mask = step
    rows, seq = spots()
    move = mask - 2 * mask * bit_of(step)
    return (rows + move, seq) if axis == "rows" else (rows, seq + move)


def orders(shape):
    seq = [("seq", 1 << b) for b in range(shape["seq"].bit_length() - 1)]
    row = [("rows", 1 << b) for b in range(shape["rows"].bit_length() - 1)]
    first, rest, near, far = seq[:1], seq[1:], row[:1], row[1:]
    named = {"W": near + far + rest, "X": rest + near + far, "Y": near + rest + far, "Z": far + near + rest,
             "V": rest + far + near, "U": far + rest + near}
    return {name: first + then for name, then in named.items()}


class Halving:
    def __init__(self, order, lead, rows, tile):
        self.order, self.tile = order, tile
        self.size, self.split, self.lead_at, self.row_at, self.own = [], [], [], [], []
        lead_at, row_at = 0, 0
        for i, step in enumerate(order):
            bit = bit_of(step)
            if lead > 1:
                lead //= 2
                how = 0
                if i == 0:
                    self.first = bit * lead
                else:
                    lead_at = lead_at + bit * lead
            elif rows % (2 * tile) == 0:
                rows //= 2
                how = 1
                row_at = row_at + bit * rows
            else:
                how = None
            self.own.append(bit)
            self.split.append(how)
            self.size.append((lead, rows))
            self.lead_at.append(lead_at)
            self.row_at.append(row_at)
        self.gathers = [i for i in reversed(range(len(order))) if self.split[i] is not None]

    def partner(self, i):
        return across(self.order[i])

    def rows_of(self, at, size):
        return pl.ds(pl.multiple_of(at, self.tile), size)

    def send(self, i, mine, land, sems):
        lead, rows = self.size[i]
        if i == 0:
            src = mine.at[pl.ds(lead - self.first, lead)]
        else:
            la, ra = self.lead_at[i - 1], self.row_at[i - 1]
            if self.split[i] == 0:
                la = la + (1 - self.own[i]) * lead
            elif self.split[i] == 1:
                ra = ra + (1 - self.own[i]) * rows
            src = land[0].at[pl.ds(la, lead), self.rows_of(ra, rows)]
        return pltpu.make_async_remote_copy(src_ref=src, dst_ref=land[i], send_sem=sems[0].at[i], recv_sem=sems[1].at[i],
                                            device_id=self.partner(i), device_id_type=MESH)

    def add(self, i, mine, land):
        lead, rows = self.size[i]
        part = rows if rows <= LANE else 96
        wide = F32 if land[0].dtype == BF else land[0].dtype

        def some(t, carry):
            at = t * part
            if i == 0:
                here = (slice(None), self.rows_of(at, part))
                left, right = land[0][here], mine[pl.ds(self.first, lead), self.rows_of(at, part)]
            else:
                here = (pl.ds(self.lead_at[i], lead), self.rows_of(self.row_at[i] + at, part))
                left, right = land[0][here], land[i][:, self.rows_of(at, part)]
            land[0][here] = (left.astype(wide) + right.astype(wide)).astype(land[0].dtype)
            return carry

        lax.fori_loop(0, rows // part, some, 0)

    def at_level(self, i):
        lead, rows = self.size[i]
        return pl.ds(self.lead_at[i], lead), self.rows_of(self.row_at[i], rows)

    def out_level(self, i):
        lead, rows = self.size[i]
        return pl.ds(self.first + self.lead_at[i], lead), self.rows_of(self.row_at[i], rows)

    def keep(self, land, out, sem):
        last = len(self.order) - 1
        return pltpu.make_async_copy(land[0].at[self.at_level(last)], out.at[self.out_level(last)], sem)

    def gather(self, m, land, out, sems):
        i = self.gathers[m]
        here = out.at[self.out_level(i)]
        src = land[0].at[self.at_level(len(self.order) - 1)] if m == 0 else here
        return pltpu.make_async_remote_copy(src_ref=src, dst_ref=here, send_sem=sems[0].at[m], recv_sem=sems[1].at[m],
                                            device_id=self.partner(i), device_id_type=MESH)

    def reduce_step(self, k, mine, land, sems):
        n = len(self.order)
        if k > 0:
            self.send(k - 1, mine, land, sems).wait()
            self.add(k - 1, mine, land)
        if k < n:
            self.send(k, mine, land, sems).start()

    def gather_step(self, m, land, out, sems, sem):
        if m == 0:
            self.keep(land, out, sem).start()
        else:
            if m == 1:
                self.keep(land, out, sem).wait()
            self.gather(m - 1, land, out, sems).wait()
        if m < len(self.gathers):
            self.gather(m, land, out, sems).start()


def land_shapes(count, lead, rows, tile, steps, dtype):
    shapes = []
    for _ in range(steps):
        if lead > 1:
            lead //= 2
        elif rows % (2 * tile) == 0:
            rows //= 2
        shapes.append(pltpu.VMEM(count + (lead, rows, LANE), dtype))
    return shapes


def peers(nseq):
    me = lax.axis_index("seq")
    found = []
    for m in sorted(range(1, nseq), key=lambda m: -(m >> 1)):
        to = 0
        for b in range(nseq.bit_length() - 1):
            bit = (me // (1 << b)) % 2
            to = to + (bit + ((m >> b) & 1) * (1 - 2 * bit)) * (1 << b)
        found.append((m, to))
    return found


def front_kernel(shape, mol_h, cot_h, wqkv_h, wout_h, ids_ref, g1_in, b1_in, qb_ref, ob_in,
                 x_out, dy_out, qkv_out, ctx_out, mid_out, lse_ref, cnt_ref,
                 xs, qkv_s, ctx_s, mid_s, wqkv_s, wout_s, lacc,
                 w_sem, m_send, m_recv, m_own, c_send, c_recv, c_own, o_sem):
    nseq = shape["seq"]
    rows, length = xs.shape[0], xs.shape[1]
    local = length // nseq
    rows_idx, me = spots()
    near = peers(nseq)

    barrier = pltpu.get_barrier_semaphore()
    for _, to in near:
        pl.semaphore_signal(barrier, inc=1, device_id=(rows_idx, to), device_id_type=MESH)
    fetch = [pltpu.make_async_copy(wqkv_h, wqkv_s, w_sem.at[0]), pltpu.make_async_copy(wout_h, wout_s, w_sem.at[1])]
    here = pl.ds(pl.multiple_of(me * local, local), local)

    def own(r):
        return pltpu.make_async_copy(mol_h.at[me * rows + r], xs.at[r, here], m_own.at[r])

    def mol(r, n):
        m, to = near[n]
        return pltpu.make_async_remote_copy(src_ref=mol_h.at[to * rows + r], dst_ref=xs.at[r, here], send_sem=m_send.at[r, m],
                                            recv_sem=m_recv.at[r, m], device_id=(rows_idx, to), device_id_type=MESH)

    def cot(n):
        m, to = near[n]
        return pltpu.make_async_remote_copy(src_ref=cot_h.at[pl.ds(to * rows, rows)], dst_ref=dy_out.at[:, here],
                                            send_sem=c_send.at[m], recv_sem=c_recv.at[m], device_id=(rows_idx, to),
                                            device_id_type=MESH)

    cot_own = pltpu.make_async_copy(cot_h.at[pl.ds(me * rows, rows)], dy_out.at[:, here], c_own)

    for r in range(rows):
        own(r).start()
    fetch[0].start()
    pl.semaphore_wait(barrier, len(near))
    for r in range(rows):
        for n in range(len(near)):
            mol(r, n).start()
    fetch[1].start()
    cot_own.start()

    half = 2 * local

    def project(r, at):
        src = pl.ds(pl.multiple_of(at, half), half)
        dst = pl.ds(pl.multiple_of(r * length + at, half), half)
        xhat, _ = norm_parts(xs[r, src].astype(F32))
        a1 = (xhat * g1 + b1).astype(BF)
        for c in range(3):
            cols = slice(c * D, (c + 1) * D)
            part = dot_nn(a1, wqkv_s[:, cols])
            qkv_s[dst, cols] = (part if c == 1 else part + qb_ref[c // 2 : c // 2 + 1]).astype(BF)

    g1, b1, ob = (ref[...].reshape(1, D) for ref in (g1_in, b1_in, ob_in))

    for r in range(rows):
        own(r).wait()
        mol(r, len(near) - 1).wait()
    fetch[0].wait()
    mine = (me // 2) * half

    def early(r, carry):
        project(r, mine)
        return carry

    lax.fori_loop(0, rows, early, 0)

    hashes, id_rows, chars = ids_ref.shape
    high = BUCKETS // LANE

    def tally(h, carry):
        total = jnp.zeros((high, LANE), F32)
        for r in range(id_rows):
            ids = ids_ref[h, r : r + 1, :]
            row = lax.broadcasted_iota(jnp.int32, (high, chars), 0)
            hi = jnp.where(row == (ids >> 7), 1.0, 0.0).astype(BF)
            lo = jnp.where(row == (ids & (LANE - 1)), 1.0, 0.0).astype(BF)
            total = total + dot_nt(hi, lo)
        cnt_ref[:, pl.ds(h, 1), :] = total.astype(jnp.int32).reshape(high, 1, LANE)
        return carry

    lax.fori_loop(0, hashes, tally, 0)
    fetch[1].wait()

    def outs(r):
        at = pl.ds(r * length, length)
        return [pltpu.make_async_copy(xs.at[r], x_out.at[r], o_sem.at[r, 0]),
                pltpu.make_async_copy(qkv_s.at[at], qkv_out.at[at], o_sem.at[r, 1]),
                pltpu.make_async_copy(ctx_s.at[at], ctx_out.at[at], o_sem.at[r, 2]),
                pltpu.make_async_copy(mid_s.at[at], mid_out.at[at], o_sem.at[r, 3])]

    for r in range(rows):
        for n in range(len(near) - 1):
            mol(r, n).wait()
        for other in range(1, nseq // 2):
            project(r, ((me // 2 + other) % (nseq // 2)) * half)
        ready = outs(r)
        ready[0].start()
        ready[1].start()
        tok = slice(r * length, (r + 1) * length)

        def pair(p, carry):
            at = pl.multiple_of(p * LANE, LANE)
            q = qkv_s[tok, pl.ds(at, LANE)] * BF(0.125)
            k = qkv_s[tok, pl.ds(pl.multiple_of(D + at, LANE), LANE)]
            v = qkv_s[tok, pl.ds(pl.multiple_of(2 * D + at, LANE), LANE)]
            ctx = []
            lse = lacc[...]
            lane = lax.broadcasted_iota(jnp.int32, lse.shape, 1)
            for half_of in range(2):
                qm = jnp.where(lane_half(q.shape, half_of), q, BF(0))
                s = dot_nt(qm, k)
                m = jnp.max(s, -1, keepdims=True)
                e = jnp.exp(s - m)
                t = jnp.sum(e, -1, keepdims=True)
                pr = (e * (1.0 / t)).astype(BF)
                ctx.append(dot_nn(pr, v))
                lse = jnp.where(lane == 2 * p + half_of, m + jnp.log(t), lse)
            lacc[...] = lse
            ctx_s[tok, pl.ds(at, LANE)] = jnp.where(lane_half(ctx[0].shape, 0), ctx[0], ctx[1]).astype(BF)
            if r == 0:

                @pl.when(p == 3)
                def _():
                    for n in range(len(near)):
                        cot(n).start()

            return carry

        lacc[...] = jnp.zeros_like(lacc)
        lax.fori_loop(0, NH // 2, pair, 0)
        ready[2].start()
        lt = lacc[...].T
        for h in range(NH):
            lse_ref[r * NH + h] = lt[h : h + 1, :]
        mid_s[tok] = xs[r].astype(F32) + (dot_nn(ctx_s[tok], wout_s[...]) + ob)
        ready[3].start()
    for r in range(rows):
        for copy in outs(r):
            copy.wait()
    cot_own.wait()
    for n in range(len(near)):
        cot(n).wait()


def front(shape, mol, cot, wqkv, wout, ids, g1, b1, qb, ob):
    nseq = shape["seq"]
    rows, length = mol.shape[0] // nseq, mol.shape[1] * nseq
    tokens = rows * length
    vm, hb = pl.BlockSpec(memory_space=pltpu.VMEM), pl.BlockSpec(memory_space=pl.ANY)
    dma = pltpu.SemaphoreType.DMA
    sds = jax.ShapeDtypeStruct
    return pl.pallas_call(
        functools.partial(front_kernel, shape),
        in_specs=[hb] * 4 + [vm] * 5,
        out_specs=[hb] * 5 + [vm] * 2,
        out_shape=[sds((rows, length, D), BF), sds((rows, length, D), BF), sds((tokens, 3 * D), BF), sds((tokens, D), BF),
                   sds((tokens, D), F32), sds((rows * NH, 1, length), F32), sds((BUCKETS // LANE, ids.shape[0], LANE), jnp.int32)],
        scratch_shapes=[pltpu.VMEM((rows, length, D), BF), pltpu.VMEM((tokens, 3 * D), BF), pltpu.VMEM((tokens, D), BF),
                        pltpu.VMEM((tokens, D), F32), pltpu.VMEM((D, 3 * D), BF), pltpu.VMEM((D, D), BF),
                        pltpu.VMEM((length, LANE), F32), dma((2,)), dma((rows, nseq)), dma((rows, nseq)), dma((rows,)),
                        dma((nseq,)), dma((nseq,)), dma, dma((rows, 4))],
        compiler_params=pltpu.CompilerParams(vmem_limit_bytes=60 * MIB, collective_id=1, has_side_effects=True),
        name="front",
    )(mol, cot, wqkv, wout, ids, g1, b1, qb, ob)


SPLIT = 2
MID = SPLIT * NFF
DRAIN = MID + 17
IN_AT = tuple(SPLIT * (j + 1) - 1 for j in range(NFF)) + (MID + 6, MID + 11, MID + 16)
EARLY_WAYS, LATE_WAYS, COUNT_WAY = ('X', 'W'), ('W', 'Y'), 'Z'
REDUCE_AT = (
    ((1, 2, 4, 5, 6, 7), (1, 2, 4, 5, 7, 8)),
    ((3, 4, 6, 7, 8, 9), (3, 4, 7, 9, 11, 12)),
    ((5, 6, 8, 9, 11, 12), (5, 6, 9, 11, 13, 17)),
    ((7, 8, 10, 12, 13, 15), (7, 8, 11, 13, 16, 18)),
    ((9, 10, 12, 13, 16, 19), (9, 10, 13, 17, 20, 25)),
    ((11, 12, 15, 19, 22, 24), (11, 12, 15, 18, 21, 26)),
    ((18, 19, 22, 25, 28, 99), (18, 20, 24, 28, 99, 99)),
    ((23, 24, 28, 99, 99, 99), (23, 24, 99, 99, 99, 99)),
    ((28, 99, 99, 99, 99, 99), (28, 99, 99, 99, 99, 99)),
)
GATHER_AT = (
    ((7, 8, 9, 11, 13, 14), (8, 9, 12, 14, 18, 20)),
    ((9, 10, 12, 16, 19, 20), (12, 13, 17, 20, 26, 28)),
    ((12, 13, 17, 19, 25, 26), (17, 21, 24, 28, 99, 99)),
    ((15, 18, 21, 27, 99, 99), (18, 23, 27, 99, 99, 99)),
    ((27, 28, 99, 99, 99, 99), (27, 99, 99, 99, 99, 99)),
    ((28, 99, 99, 99, 99, 99), (28, 99, 99, 99, 99, 99)),
    ((99, 99, 99, 99, 99, 99), (99, 99, 99, 99, 99, 99)),
    ((99, 99, 99, 99, 99, 99), (99, 99, 99, 99, 99, 99)),
    ((99, 99, 99, 99, 99, 99), (99, 99, 99, 99, 99, 99)),
)
COUNT_AT = (0, 1, 3, 5, 7, 8, 15, 17, 20, 23, 26, 27)
BACK_AT = (17, 24, 13, 18)
LATE = (
    (3, 0, 0, 0), (1, 3, 1, 3), (1, 3, 0, 4), (0, 7, 1, 2), (0, 8, 0, 1), (1, 4, 1, 1), (0, 6, 0, 5), (0, 6, 1, 4), (0, 8, 1, 1),
    (3, 0, 0, 1), (1, 5, 1, 1), (1, 3, 0, 5), (0, 7, 0, 3), (1, 4, 0, 2), (1, 2, 1, 4), (1, 5, 0, 1), (1, 2, 1, 5), (1, 4, 1, 2),
    (0, 6, 1, 5), (1, 3, 1, 4), (1, 6, 0, 0), (1, 6, 1, 0), (1, 5, 1, 2), (1, 3, 1, 5), (1, 5, 0, 2), (0, 7, 0, 4), (0, 8, 0, 2),
    (1, 4, 1, 3), (1, 6, 1, 1), (0, 8, 1, 2), (1, 5, 1, 3), (1, 4, 0, 3), (0, 8, 0, 3), (0, 7, 1, 3), (1, 6, 1, 2), (3, 0, 0, 2),
    (1, 5, 0, 3), (1, 6, 0, 1), (0, 7, 0, 5), (1, 7, 0, 0), (0, 7, 1, 4), (0, 8, 0, 4), (0, 8, 1, 3), (1, 4, 1, 4), (1, 6, 0, 2),
    (0, 7, 1, 5), (1, 7, 1, 0), (0, 8, 1, 4), (1, 4, 1, 5), (1, 4, 0, 4), (1, 6, 0, 3), (1, 5, 1, 4), (1, 4, 0, 5), (1, 7, 1, 1),
    (1, 6, 1, 3), (3, 0, 0, 3), (1, 5, 1, 5), (0, 8, 1, 5), (1, 8, 1, 0), (1, 7, 1, 2), (3, 0, 0, 4), (1, 5, 0, 4), (1, 8, 1, 1),
    (1, 6, 0, 4), (1, 7, 0, 1), (0, 8, 0, 5), (1, 8, 0, 0), (1, 5, 0, 5), (1, 6, 0, 5), (1, 7, 1, 3), (3, 0, 0, 5), (1, 8, 1, 2),
    (1, 8, 0, 1), (1, 6, 1, 4), (1, 7, 0, 2), (1, 6, 1, 5), (1, 8, 1, 3), (1, 8, 0, 2), (1, 7, 1, 4), (1, 7, 0, 3), (1, 7, 1, 5),
    (1, 8, 0, 3), (1, 8, 1, 4), (1, 8, 1, 5), (1, 7, 0, 4), (1, 7, 0, 5), (1, 8, 0, 4), (1, 8, 0, 5),
)


def timetable(nd, gathers, tally_gathers):
    if nd == len(REDUCE_AT[0][0]) - 1:
        ticks = {}
        for j in range(NPAIR):
            for o in range(2):
                ticks |= {(0, j, o, k): t for k, t in enumerate(REDUCE_AT[j][o])}
                ticks |= {(1, j, o, m): t for m, t in enumerate(GATHER_AT[j][o])}
        ticks |= {(2, 0, 0, k): t for k, t in enumerate(COUNT_AT)}
        return {key: t for key, t in ticks.items() if t < DRAIN}, BACK_AT, list(LATE)
    ticks = {}
    for j, t in enumerate(IN_AT):
        for o in range(2):
            ticks |= {(0, j, o, k): t + 3 * k for k in range(nd + 1)}
            ticks |= {(1, j, o, m): max(t + 3 * nd, 20 + 2 * j) + 3 * m for m in range(gathers + 1)}
    ticks |= {(2, 0, 0, k): 2 * k for k in range(nd + 2 + tally_gathers)}
    late = sorted((t, key) for key, t in ticks.items() if t >= DRAIN)
    return {key: t for key, t in ticks.items() if t < DRAIN}, (MID + 1,) * 4, [(3, 0, 0, k) for k in range(nd + 1)] + [key for _, key in late]


def rear_kernel(shape, length, mid_h, dy_h, x_h, qkv_h, ctx_h, wup_h, wdn_h, wqkv_h, wout_h, lse_ref, cnt_ref,
                g1_in, b1_in, g2_in, b2_in, ub_in, db_in,
                lo_out, gm_out, sum_out, cnt_out, vec_out,
                mid_s, dy_s, a2_s, a2t_s, dyt_s, acc_s, da2_s, wup_s, wdn_s, qkv_s, ctx_s, x_s, wqkv_s, wout_s,
                dqkv_s, gout_s, lo_s, vec_s, gub_s, part_s, fetch_sem, stage_s, vland_s, vacc_s, five_s, ub_s,
                rs_send, rs_recv, ag_send, ag_recv, keep_sem, crs_send, crs_recv, cag_send, cag_recv, ckeep_sem,
                v_send, v_recv, t_send, t_recv, t_own, *lands):
    ways = orders(shape)
    nd = len(ways["X"])
    nseq = shape["seq"]
    land = lands[:nd]
    cland = lands[nd:]
    rows_idx, me = spots()
    tokens = mid_s.shape[0]
    rows = tokens // length
    local = length // nseq
    fc = NB * LANE

    barrier = pltpu.get_barrier_semaphore()
    others = [across(step) for step in ways["X"]]
    others += [(rows_idx, to) for m, to in peers(nseq) if m & (m - 1)]
    for other in others:
        pl.semaphore_signal(barrier, inc=1, device_id=other, device_id_type=MESH)

    def fetch(t):
        return pltpu.make_async_copy((mid_h, dy_h, x_h, qkv_h, ctx_h, wqkv_h, wout_h)[t],
                                     (mid_s, dy_s, x_s, qkv_s, ctx_s, wqkv_s, wout_s)[t], fetch_sem.at[t])

    def weights(i, slot):
        return (pltpu.make_async_copy(wup_h.at[:, pl.ds(pl.multiple_of(i * fc, fc), fc)], wup_s.at[slot], fetch_sem.at[8 + slot]),
                pltpu.make_async_copy(wdn_h.at[pl.ds(pl.multiple_of(i * fc, fc), fc)], wdn_s.at[slot], fetch_sem.at[10 + slot]))

    for n, ref in enumerate((g1_in, b1_in, g2_in, b2_in, db_in)):
        five_s[n : n + 1] = ref[...].reshape(1, D)
    ub_s[...] = ub_in[...].reshape(1, FF)
    g1_ref, b1_ref, g2_ref, b2_ref, db_ref = (five_s.at[n : n + 1] for n in range(5))
    ub_ref = ub_s
    fetch(0).start()
    fetch(1).start()
    for copy in weights(0, 0):
        copy.start()
    pl.semaphore_wait(barrier, len(others))

    near = peers(nseq)

    def give_back(which, out, r, n):
        m, to = near[n]
        return pltpu.make_async_remote_copy(
            src_ref=lo_s.at[r, pl.ds(pl.multiple_of(to * local, local), local)], dst_ref=out.at[me * rows + r],
            send_sem=t_send.at[which, r, m], recv_sem=t_recv.at[which, r, m], device_id=(rows_idx, to), device_id_type=MESH)

    def give_self(which, out):
        return pltpu.make_async_copy(lo_s.at[:, pl.ds(pl.multiple_of(me * local, local), local)],
                                     out.at[pl.ds(me * rows, rows)], t_own.at[which])

    def give_wait(which, out):
        give_self(which, out).wait()
        for r in range(rows):
            for n in range(len(near)):
                give_back(which, out, r, n).wait()

    back = [(r, n) for r in range(rows) for n in range(len(near) - 1)]

    tally = Halving(ways[COUNT_WAY], cnt_ref.shape[0], cnt_ref.shape[1], 8)
    gathers = len(Halving(ways["X"], NB, D, 16).gathers)
    ticks, back_at, late = timetable(nd, gathers, len(tally.gathers))

    def act(kind, j, o, k, which):
        plan = Halving(ways[which], NB, D, 16)
        here = [r.at[j, o] for r in land]
        if kind == 0:
            plan.reduce_step(k, stage_s.at[j % 2, o], here, (rs_send.at[j, o], rs_recv.at[j, o]))
        else:
            plan.gather_step(k, here, sum_out.at[j, o], (ag_send.at[j, o], ag_recv.at[j, o]), keep_sem.at[j, o])

    def act_counts(k):
        if k <= nd:
            tally.reduce_step(k, cnt_ref, cland, (crs_send, crs_recv))
        else:
            tally.gather_step(k - nd - 1, cland, cnt_out, (cag_send, cag_recv), ckeep_sem)

    def tick(t, low, high):
        for kind, most in ((0, nd), (1, gathers)):
            for k in reversed(range(most + 1)):
                for o in range(2):
                    for named, pairs in ((EARLY_WAYS[o], range(NFF)), (LATE_WAYS[o], range(NFF, NPAIR))):
                        found = [(ticks.get((kind, j, o, k), -1), j) for j in pairs]
                        found = [(at, j) for at, j in found if low <= at <= high]
                        assert len({at for at, _ in found}) == len(found)
                        if not found:
                            continue
                        hit = sum(jnp.where(t == at, 1, 0) for at, _ in found)
                        j = sum(jnp.where(t == at, j, 0) for at, j in found)

                        @pl.when(hit == 1)
                        def _():
                            act(kind, j, o, k, named)

        for k in range(nd + 2 + len(tally.gathers)):
            at = ticks.get((2, 0, 0, k), -1)
            if low <= at <= high:

                @pl.when(t == at)
                def _():
                    act_counts(k)

        for n, at in enumerate(back_at):
            if low <= at <= high:

                @pl.when(t == at)
                def _():
                    give_back(0, lo_out, *back[n]).start()

    step = 256
    pieces = tokens // step
    fetch(0).wait()
    fetch(1).wait()
    for t in (6, 4, 2, 3, 5):
        fetch(t).start()

    def open_piece(n, carry):
        at = pl.ds(pl.multiple_of(n * step, step), step)
        mid = mid_s[at]
        xhat, _ = norm_parts(mid)
        a2 = (xhat * g2_ref[...] + b2_ref[...]).astype(BF)
        a2_s[at] = a2
        a2t_s[:, at] = a2.T
        dyt_s[:, at] = dy_s[at].T
        acc_s[at] = mid + db_ref[...]
        da2_s[at] = jnp.zeros((step, D), F32)
        return carry

    lax.fori_loop(0, pieces, open_piece, 0)

    def ff(i, carry):
        slot = i % 2

        @pl.when(i + 1 < NFF)
        def _():
            for copy in weights(i + 1, 1 - slot):
                copy.start()

        for copy in weights(i, slot):
            copy.wait()
        cols = pl.ds(pl.multiple_of(i * fc, fc), fc)
        u = dot_nn(a2_s[...], wup_s[slot]) + ub_ref[:, cols]
        dh = dot_nt(dy_s[...], wdn_s[slot])
        cdf = 0.5 + 0.5 * lax.erf(u * (2.0 ** -0.5))
        pdf = jnp.exp(u * u * -0.5) * 0.3989422804014327
        hid = (u * cdf).astype(BF)
        du = (dh * (cdf + u * pdf)).astype(BF)
        gub_s[:, cols] = jnp.sum(du.astype(F32), 0, keepdims=True)
        tick(SPLIT * i, 0, MID - 1)
        acc_s[...] += dot_nn(hid, wdn_s[slot])
        da2_s[...] += dot_nt(du, wup_s[slot])
        gd = dot_nn(dyt_s[...], hid).astype(BF)
        gu = dot_nn(a2t_s[...], du).astype(BF)
        for b in range(NB):
            stage_s[slot, 0, b] = gd[:, b * LANE : (b + 1) * LANE]
            stage_s[slot, 1, b] = gu[:, b * LANE : (b + 1) * LANE]
        tick(SPLIT * i + SPLIT - 1, 0, MID - 1)
        return carry

    lax.fori_loop(0, NFF, ff, 0)

    part_s[...] = jnp.zeros_like(part_s)
    fetch(6).wait()

    def turn_piece(n, carry):
        at = pl.ds(pl.multiple_of(n * step, step), step)
        lo_s[n * step // length, pl.ds(pl.multiple_of((n * step) % length, step), step)] = acc_s[at].astype(BF)
        dy = dy_s[at].astype(F32)
        xhat, rstd = norm_parts(mid_s[at])
        da2 = da2_s[at]
        dx2 = dy + norm_back(xhat, rstd, g2_ref[...], da2)
        da2_s[at] = dx2
        do = dx2.astype(BF)
        a2_s[at] = do
        part_s[0:1] += jnp.sum(dy, 0, keepdims=True)
        part_s[1:2] += jnp.sum(da2 * xhat, 0, keepdims=True)
        part_s[2:3] += jnp.sum(da2, 0, keepdims=True)
        part_s[3:4] += jnp.sum(do.astype(F32), 0, keepdims=True)
        dy_s[at] = dot_nt(do, wout_s[...]).astype(BF)
        return carry

    lax.fori_loop(0, pieces, turn_piece, 0)
    dctx_s, do_s, dx2_s, da1_s, a1t_s = dy_s, a2_s, da2_s, acc_s, a2t_s
    give_self(0, lo_out).start()
    for r in range(rows):
        give_back(0, lo_out, r, len(near) - 1).start()
    tick(MID, MID, MID)
    fetch(4).wait()
    fetch(2).wait()
    gout = dot_tn(ctx_s[...], do_s[...]).astype(BF)
    for b in range(D // LANE):
        gout_s[b] = gout[:, b * LANE : (b + 1) * LANE]

    def first_norm(n, carry):
        at = pl.ds(pl.multiple_of(n * step, step), step)
        xhat, _ = norm_parts(x_s[at].astype(F32))
        a1t_s[:, at] = (xhat * g1_ref[...] + b1_ref[...]).astype(BF).T
        da1_s[at] = jnp.zeros((step, D), F32)
        return carry

    lax.fori_loop(0, pieces, first_norm, 0)
    fetch(3).wait()
    fetch(5).wait()
    tick(MID + 1, MID + 1, MID + 1)

    def group(g, carry):
        def unit(n, inner_carry):
            r = n // 2
            h = n % 2
            p = 2 * g + h
            tok = pl.ds(pl.multiple_of(r * length, length), length)
            cq = pl.ds(pl.multiple_of(p * LANE, LANE), LANE)
            q = qkv_s[tok, cq] * BF(0.125)
            k = qkv_s[tok, pl.ds(pl.multiple_of(p * LANE + D, LANE), LANE)]
            v = qkv_s[tok, pl.ds(pl.multiple_of(p * LANE + 2 * D, LANE), LANE)]
            dc = dctx_s[tok, cq]
            dqs, dks, dvs = [], [], []
            for half in range(2):
                keep = lane_half(k.shape, half)
                km = jnp.where(keep, k, BF(0))
                vm = jnp.where(keep, v, BF(0))
                lse = lse_ref[r * NH + 2 * p + half]
                st = dot_nt(km, q)
                pt = jnp.exp(st - lse)
                dpt = dot_nt(vm, dc)
                inner = jnp.sum(pt * dpt, 0, keepdims=True)
                dst = (pt * (dpt - inner)).astype(BF)
                dvs.append(dot_nn(pt.astype(BF), dc))
                dks.append(dot_nn(dst, q))
                dqs.append(dot_tn(dst, k))
            sel = lane_half(dqs[0].shape, 0)
            dqkv_s[tok, pl.ds(pl.multiple_of(h * LANE, LANE), LANE)] = (jnp.where(sel, dqs[0], dqs[1]) * 0.125).astype(BF)
            dqkv_s[tok, pl.ds(pl.multiple_of(h * LANE + 2 * LANE, LANE), LANE)] = jnp.where(sel, dks[0], dks[1]).astype(BF)
            dqkv_s[tok, pl.ds(pl.multiple_of(h * LANE + 4 * LANE, LANE), LANE)] = jnp.where(sel, dvs[0], dvs[1]).astype(BF)
            tick(MID + 2 + 5 * g + n, MID + 2, DRAIN - 1)
            return inner_carry

        lax.fori_loop(0, 4, unit, 0)
        slot = (NFF + g) % 2
        grads = dot_nn(a1t_s[...], dqkv_s[...]).astype(BF)
        for b in range(6):
            stage_s[slot, b // NB, b % NB] = grads[:, b * LANE : (b + 1) * LANE]
        for b in range(2):
            stage_s[slot, 1, 2 + b] = gout_s[2 * g + b]
        two = 2 * LANE
        for c in range(3):
            at = pl.ds(pl.multiple_of(c * D + g * two, two), two)
            da1_s[...] += dot_nt(dqkv_s[:, c * two : (c + 1) * two], wqkv_s[:, at])
        here = pl.ds(pl.multiple_of(g * two, two), two)
        part_s[6:7, here] = jnp.sum(dqkv_s[:, 0:two].astype(F32), 0, keepdims=True)
        part_s[7:8, here] = jnp.sum(dqkv_s[:, 2 * two : 3 * two].astype(F32), 0, keepdims=True)
        tick(MID + 6 + 5 * g, MID + 2, DRAIN - 1)
        return carry

    lax.fori_loop(0, 3, group, 0)

    give_wait(0, lo_out)

    def last_piece(n, carry):
        at = pl.ds(pl.multiple_of(n * step, step), step)
        xhat, rstd = norm_parts(x_s[at].astype(F32))
        da1 = da1_s[at]
        part_s[4:5] += jnp.sum(da1 * xhat, 0, keepdims=True)
        part_s[5:6] += jnp.sum(da1, 0, keepdims=True)
        gm = dx2_s[at] + norm_back(xhat, rstd, g1_ref[...], da1)
        lo_s[n * step // length, pl.ds(pl.multiple_of((n * step) % length, step), step)] = gm.astype(BF)
        return carry

    lax.fori_loop(0, pieces, last_piece, 0)
    give_self(1, gm_out).start()
    for r in range(rows):
        for n in range(len(near)):
            give_back(1, gm_out, r, n).start()
    vacc_s[0, 0:8] = part_s[...]
    for b in range(FF // (2 * LANE)):
        vacc_s[0, 8 + b // 3 : 9 + b // 3, (b % 3) * 2 * LANE : (b % 3 + 1) * 2 * LANE] = gub_s[:, b * 2 * LANE : (b + 1) * 2 * LANE]
    vacc_s[0, 12:16] = jnp.zeros((4, D), F32)

    def swap(i):
        return pltpu.make_async_remote_copy(src_ref=vacc_s.at[i], dst_ref=vland_s.at[i], send_sem=v_send.at[i], recv_sem=v_recv.at[i],
                                            device_id=across(ways["X"][i]), device_id_type=MESH)

    for kind, j, o, k in late:
        if kind < 2:
            act(kind, j, o, k, (EARLY_WAYS if j < NFF else LATE_WAYS)[o])
        elif kind == 2:
            act_counts(k)
        else:
            if k > 0:
                swap(k - 1).wait()
                vacc_s[k] = vacc_s[k - 1] + vland_s[k - 1]
            if k < nd:
                swap(k).start()
    vec_out[...] = vacc_s[nd]
    give_wait(1, gm_out)


def rear(shape, length, mid, dy, x, qkv, ctx, wup, wdn, wqkv, wout, lse, cnt, g1, b1, g2, b2, ub, db):
    tokens = mid.shape[0]
    nseq = shape["seq"]
    rows = tokens // length
    nd = len(orders(shape)["X"])
    vm, hb = pl.BlockSpec(memory_space=pltpu.VMEM), pl.BlockSpec(memory_space=pl.ANY)
    dma = pltpu.SemaphoreType.DMA
    V = pltpu.VMEM
    fc = NB * LANE
    scratch = [
        V((tokens, D), F32), V((tokens, D), BF), V((tokens, D), BF), V((D, tokens), BF), V((D, tokens), BF), V((tokens, D), F32),
        V((tokens, D), F32), V((2, D, fc), BF), V((2, fc, D), BF), V((tokens, 3 * D), BF), V((tokens, D), BF), V((tokens, D), BF),
        V((D, 3 * D), BF), V((D, D), BF), V((tokens, D), BF), V((D // LANE, D, LANE), BF), V((rows, length, D), BF), V((8, D), F32),
        V((1, FF), F32), V((8, D), F32), dma((12,)), V((2, 2, NB, D, LANE), BF), V((nd, 16, D), F32), V((nd + 1, 16, D), F32), V((8, D), F32), V((1, FF), F32),
        dma((NPAIR, 2, nd)), dma((NPAIR, 2, nd)), dma((NPAIR, 2, nd)), dma((NPAIR, 2, nd)), dma((NPAIR, 2)),
        dma((nd,)), dma((nd,)), dma((nd,)), dma((nd,)), dma, dma((nd,)), dma((nd,)), dma((2, rows, nseq)), dma((2, rows, nseq)), dma((2,)),
    ]
    scratch += land_shapes((NPAIR, 2), NB, D, 16, nd, BF)
    scratch += land_shapes((), cnt.shape[0], cnt.shape[1], 8, nd, jnp.int32)
    local = length // nseq
    return pl.pallas_call(
        functools.partial(rear_kernel, shape, length),
        in_specs=[hb] * 9 + [vm] * 8,
        out_specs=[hb, hb, hb, hb, vm],
        out_shape=[jax.ShapeDtypeStruct((rows * nseq, local, D), BF), jax.ShapeDtypeStruct((rows * nseq, local, D), BF),
                   jax.ShapeDtypeStruct((NPAIR, 2, NB, D, LANE), BF), jax.ShapeDtypeStruct(cnt.shape, jnp.int32),
                   jax.ShapeDtypeStruct((16, D), F32)],
        scratch_shapes=scratch,
        compiler_params=pltpu.CompilerParams(vmem_limit_bytes=63 * MIB, collective_id=0, has_side_effects=True),
        name="rear",
    )(mid, dy, x, qkv, ctx, wup, wdn, wqkv, wout, lse, cnt, g1, b1, g2, b2, ub, db)


def widen_kernel(src_ref, gm_ref, lo_ref, vec_ref, cnt_ref, gmol_ref, lout_ref, counts_ref, g1_ref, b1_ref, qb_ref, ob_ref, g2_ref,
                 b2_ref, ub_ref, db_ref, qkv_out, out_out, up_out, down_out, wide_s, tall_s, sem):
    j = pl.program_id(0)
    slot = j % 2
    fc = NB * LANE
    two = 2 * LANE

    def first(i, s):
        at = pl.ds(pl.multiple_of(i * fc, fc), fc)
        return [pltpu.make_async_copy(tall_s.at[s], down_out.at[at], sem.at[s, 0]),
                pltpu.make_async_copy(wide_s.at[s, 0], up_out.at[:, at], sem.at[s, 1])]

    def later(i, s):
        g = i - NFF
        to = lambda c: pl.ds(pl.multiple_of(c * D + g * two, two), two)
        return [pltpu.make_async_copy(wide_s.at[s, 0, :, 0:two], qkv_out.at[:, to(0)], sem.at[s, 0]),
                pltpu.make_async_copy(wide_s.at[s, 0, :, two : 2 * two], qkv_out.at[:, to(1)], sem.at[s, 1]),
                pltpu.make_async_copy(wide_s.at[s, 1, :, 0:two], qkv_out.at[:, to(2)], sem.at[s, 2]),
                pltpu.make_async_copy(wide_s.at[s, 1, :, two : 2 * two], out_out.at[:, to(0)], sem.at[s, 3])]

    def finish(i, s):
        @pl.when(i < NFF)
        def _():
            for copy in first(i, s):
                copy.wait()

        @pl.when(i >= NFF)
        def _():
            for copy in later(i, s):
                copy.wait()

    @pl.when(j >= 2)
    def _():
        finish(j - 2, slot)

    gmol_ref[...] = gm_ref[...].astype(F32)
    lout_ref[...] = lo_ref[...]

    @pl.when(j == 0)
    def _():
        for n, ref in ((0, db_ref), (1, g2_ref), (2, b2_ref), (3, ob_ref), (4, g1_ref), (5, b1_ref)):
            ref[...] = vec_ref[n : n + 1].reshape(D)
        qb_ref[...] = vec_ref[6:8]
        ub_ref[...] = jnp.concatenate([vec_ref[n : n + 1] for n in range(8, 12)], 1).reshape(FF)
        for n in range(cnt_ref.shape[0]):
            counts_ref[:, n * LANE : (n + 1) * LANE] = cnt_ref[n]

    @pl.when(j < NFF)
    def _():
        for b in range(NB):
            at = slice(b * LANE, (b + 1) * LANE)
            tall_s[slot, at, :] = src_ref[0, 0, b].astype(F32).T
            wide_s[slot, 0, :, at] = src_ref[0, 1, b].astype(F32)
        for copy in first(j, slot):
            copy.start()

    @pl.when(j >= NFF)
    def _():
        for o in range(2):
            for b in range(NB):
                wide_s[slot, o, :, b * LANE : (b + 1) * LANE] = src_ref[0, o, b].astype(F32)
        for copy in later(j, slot):
            copy.start()

    @pl.when(j == NPAIR - 1)
    def _():
        finish(j - 1, 1 - slot)
        finish(j, slot)


def widen(sums, gm, lo, vec, cnt):
    hb = pl.BlockSpec(memory_space=pl.ANY)
    vm = pl.BlockSpec(memory_space=pltpu.VMEM)
    sds = jax.ShapeDtypeStruct
    one = sds((D,), F32)
    rows = gm.shape[0]
    some = pl.BlockSpec((1,) + gm.shape[1:], lambda j: (jnp.minimum(j, rows - 1), 0, 0))
    return pl.pallas_call(
        widen_kernel,
        grid=(NPAIR,),
        in_specs=[pl.BlockSpec((1, 2, NB, D, LANE), lambda j: (j, 0, 0, 0, 0)), some, some, vm, vm],
        out_specs=[some, some] + [vm] * 9 + [hb] * 4,
        out_shape=[sds(gm.shape, F32), sds(lo.shape, BF), sds((cnt.shape[1], BUCKETS), jnp.int32), one, one, sds((2, D), F32), one, one,
                   one, sds((FF,), F32), one, sds((D, 3 * D), F32), sds((D, D), F32), sds((D, FF), F32), sds((FF, D), F32)],
        scratch_shapes=[pltpu.VMEM((2, 2, D, NB * LANE), F32), pltpu.VMEM((2, NB * LANE, D), F32), pltpu.SemaphoreType.DMA((2, 4))],
        compiler_params=pltpu.CompilerParams(vmem_limit_bytes=60 * MIB),
        name="widen",
    )(sums, gm, lo, vec, cnt)


def on_device(shape, molecules, ln1_gain, ln1_bias, w_qkv, qkv_bias, w_out, out_bias, ln2_gain, ln2_bias, w_up, up_bias,
              w_down, down_bias, out_cotangent, bucket_ids):
    width = molecules.shape[2]
    length = molecules.shape[1] * shape["seq"]
    x, dy, qkv, ctx, mid, lse, tally = front(shape, molecules, out_cotangent, w_qkv, w_out, bucket_ids, ln1_gain, ln1_bias,
                                             qkv_bias, out_bias)
    layer_out, gm, sums, counts, vec = rear(
        shape, length, mid, dy.reshape(-1, width), x.reshape(-1, width), qkv, ctx, w_up, w_down, w_qkv, w_out, lse, tally,
        ln1_gain, ln1_bias, ln2_gain, ln2_bias, up_bias, down_bias)
    (g_mol, layer_out, counts, g_g1, g_b1, g_qb, g_ob, g_g2, g_b2, g_ub, g_db, g_qkv, g_out, g_up,
     g_down) = widen(sums, gm, layer_out, vec, counts)
    return (layer_out, g_mol, g_g1, g_b1, g_qkv, g_qb, g_out, g_ob, g_g2, g_b2, g_up, g_ub, g_down, g_db, counts)


def solution(mesh):
    tok = P("rows", "seq", None)
    return jax.shard_map(
        functools.partial(on_device, dict(mesh.shape)),
        mesh=mesh,
        in_specs=(tok,) + (P(),) * 12 + (tok, P(None, "rows", "seq")),
        out_specs=(tok, tok) + (P(),) * 13,
        check_vma=False,
    )
```

```python
import functools
import jax
import jax.numpy as jnp
from jax import lax
from jax.experimental import pallas as pl
from jax.experimental.pallas import tpu as pltpu
from jax.sharding import PartitionSpec as P

MESH = pl.DeviceIdType.MESH
BF = jnp.bfloat16
F32 = jnp.float32
EPS = 1e-5
D = 768
HD = 64
NH = 12
FF = 3072
BUCKETS = 16384
LANE = 128
MIB = 1 << 20


def dot_nn(a, b):
    return lax.dot_general(a, b, (((1,), (0,)), ((), ())), preferred_element_type=F32)


def dot_nt(a, b):
    return lax.dot_general(a, b, (((1,), (1,)), ((), ())), preferred_element_type=F32)


def dot_tn(a, b):
    return lax.dot_general(a, b, (((0,), (0,)), ((), ())), preferred_element_type=F32)


def norm_parts(x):
    mean = jnp.mean(x, -1, keepdims=True)
    cen = x - mean
    var = jnp.mean(cen * cen, -1, keepdims=True)
    rstd = lax.rsqrt(var + EPS)
    return cen * rstd, rstd


def norm_back(xhat, rstd, gain, dy):
    dxh = dy * gain
    m1 = jnp.mean(dxh, -1, keepdims=True)
    m2 = jnp.mean(dxh * xhat, -1, keepdims=True)
    return rstd * (dxh - m1 - xhat * m2)


def lane_half(shape, half):
    lane = lax.broadcasted_iota(jnp.int32, shape, 1)
    return (lane < HD) if half == 0 else (lane >= HD)


NB = 4
NFF = FF // (NB * LANE)
NPAIR = NFF + 3


def spots():
    return lax.axis_index("rows"), lax.axis_index("seq")


def bit_of(step):
    axis, mask = step
    return (lax.axis_index(axis) // mask) % 2


def across(step):
    axis, mask = step
    rows, seq = spots()
    move = mask - 2 * mask * bit_of(step)
    return (rows + move, seq) if axis == "rows" else (rows, seq + move)


def orders(shape):
    seq = [("seq", 1 << b) for b in range(shape["seq"].bit_length() - 1)]
    row = [("rows", 1 << b) for b in range(shape["rows"].bit_length() - 1)]
    first, rest, near, far = seq[:1], seq[1:], row[:1], row[1:]
    named = {"W": near + far + rest, "X": rest + near + far, "Y": near + rest + far, "Z": far + near + rest,
             "V": rest + far + near, "U": far + rest + near}
    return {name: first + then for name, then in named.items()}


class Halving:
    def __init__(self, order, lead, rows, tile):
        self.order, self.tile = order, tile
        self.size, self.split, self.lead_at, self.row_at, self.own = [], [], [], [], []
        lead_at, row_at = 0, 0
        for i, step in enumerate(order):
            bit = bit_of(step)
            if lead > 1:
                lead //= 2
                how = 0
                if i == 0:
                    self.first = bit * lead
                else:
                    lead_at = lead_at + bit * lead
            elif rows % (2 * tile) == 0:
                rows //= 2
                how = 1
                row_at = row_at + bit * rows
            else:
                how = None
            self.own.append(bit)
            self.split.append(how)
            self.size.append((lead, rows))
            self.lead_at.append(lead_at)
            self.row_at.append(row_at)
        self.gathers = [i for i in reversed(range(len(order))) if self.split[i] is not None]

    def partner(self, i):
        return across(self.order[i])

    def rows_of(self, at, size):
        return pl.ds(pl.multiple_of(at, self.tile), size)

    def send(self, i, mine, land, sems):
        lead, rows = self.size[i]
        if i == 0:
            src = mine.at[pl.ds(lead - self.first, lead)]
        else:
            la, ra = self.lead_at[i - 1], self.row_at[i - 1]
            if self.split[i] == 0:
                la = la + (1 - self.own[i]) * lead
            elif self.split[i] == 1:
                ra = ra + (1 - self.own[i]) * rows
            src = land[0].at[pl.ds(la, lead), self.rows_of(ra, rows)]
        return pltpu.make_async_remote_copy(src_ref=src, dst_ref=land[i], send_sem=sems[0].at[i], recv_sem=sems[1].at[i],
                                            device_id=self.partner(i), device_id_type=MESH)

    def add(self, i, mine, land):
        lead, rows = self.size[i]
        part = rows if rows <= LANE else 96
        wide = F32 if land[0].dtype == BF else land[0].dtype

        def some(t, carry):
            at = t * part
            if i == 0:
                here = (slice(None), self.rows_of(at, part))
                left, right = land[0][here], mine[pl.ds(self.first, lead), self.rows_of(at, part)]
            else:
                here = (pl.ds(self.lead_at[i], lead), self.rows_of(self.row_at[i] + at, part))
                left, right = land[0][here], land[i][:, self.rows_of(at, part)]
            land[0][here] = (left.astype(wide) + right.astype(wide)).astype(land[0].dtype)
            return carry

        lax.fori_loop(0, rows // part, some, 0)

    def at_level(self, i):
        lead, rows = self.size[i]
        return pl.ds(self.lead_at[i], lead), self.rows_of(self.row_at[i], rows)

    def out_level(self, i):
        lead, rows = self.size[i]
        return pl.ds(self.first + self.lead_at[i], lead), self.rows_of(self.row_at[i], rows)

    def keep(self, land, out, sem):
        last = len(self.order) - 1
        return pltpu.make_async_copy(land[0].at[self.at_level(last)], out.at[self.out_level(last)], sem)

    def gather(self, m, land, out, sems):
        i = self.gathers[m]
        here = out.at[self.out_level(i)]
        src = land[0].at[self.at_level(len(self.order) - 1)] if m == 0 else here
        return pltpu.make_async_remote_copy(src_ref=src, dst_ref=here, send_sem=sems[0].at[m], recv_sem=sems[1].at[m],
                                            device_id=self.partner(i), device_id_type=MESH)

    def reduce_step(self, k, mine, land, sems):
        n = len(self.order)
        if k > 0:
            self.send(k - 1, mine, land, sems).wait()
            self.add(k - 1, mine, land)
        if k < n:
            self.send(k, mine, land, sems).start()

    def gather_step(self, m, land, out, sems, sem):
        if m == 0:
            self.keep(land, out, sem).start()
        else:
            if m == 1:
                self.keep(land, out, sem).wait()
            self.gather(m - 1, land, out, sems).wait()
        if m < len(self.gathers):
            self.gather(m, land, out, sems).start()


def land_shapes(count, lead, rows, tile, steps, dtype):
    shapes = []
    for _ in range(steps):
        if lead > 1:
            lead //= 2
        elif rows % (2 * tile) == 0:
            rows //= 2
        shapes.append(pltpu.VMEM(count + (lead, rows, LANE), dtype))
    return shapes


def peers(nseq):
    me = lax.axis_index("seq")
    found = []
    for m in sorted(range(1, nseq), key=lambda m: -(m >> 1)):
        to = 0
        for b in range(nseq.bit_length() - 1):
            bit = (me // (1 << b)) % 2
            to = to + (bit + ((m >> b) & 1) * (1 - 2 * bit)) * (1 << b)
        found.append((m, to))
    return found


SPLIT = 2
TOGETHER = 2
MID = SPLIT * NFF
DRAIN = MID + 17
IN_AT = tuple(SPLIT * (j + 1) - 1 for j in range(NFF)) + (MID + 6, MID + 11, MID + 16)
COUNT_WAY = 'Y'
WAYS = (
    ('Y', 'W'), ('W', 'Y'), ('W', 'W'), ('X', 'Y'), ('Y', 'X'), ('X', 'W'), ('X', 'W'), ('X', 'W'), ('W', 'Z'),
)
REDUCE_AT = (
    ((1, 2, 4, 5, 6, 7), (1, 2, 5, 7, 9, 11)),
    ((3, 4, 7, 9, 11, 13), (3, 4, 8, 9, 11, 12)),
    ((5, 6, 9, 11, 13, 18), (5, 6, 10, 12, 14, 18)),
    ((7, 8, 11, 13, 14, 16), (7, 8, 11, 13, 14, 16)),
    ((9, 10, 12, 14, 16, 19), (9, 10, 12, 14, 18, 21)),
    ((11, 12, 16, 19, 21, 24), (11, 12, 16, 20, 24, 26)),
    ((18, 19, 24, 26, 28, 99), (18, 19, 23, 28, 99, 99)),
    ((23, 24, 28, 99, 99, 99), (23, 24, 28, 99, 99, 99)),
    ((28, 99, 99, 99, 99, 99), (28, 99, 99, 99, 99, 99)),
)
GATHER_AT = (
    ((7, 8, 9, 11, 14, 16), (11, 12, 14, 18, 21, 23)),
    ((13, 18, 21, 24, 99, 99), (12, 13, 16, 19, 24, 26)),
    ((18, 21, 26, 28, 99, 99), (18, 21, 26, 99, 99, 99)),
    ((16, 19, 22, 26, 99, 99), (16, 19, 23, 26, 99, 99)),
    ((99, 99, 99, 99, 99, 99), (99, 99, 99, 99, 99, 99)),
    ((24, 28, 99, 99, 99, 99), (26, 99, 99, 99, 99, 99)),
    ((99, 99, 99, 99, 99, 99), (99, 99, 99, 99, 99, 99)),
    ((99, 99, 99, 99, 99, 99), (99, 99, 99, 99, 99, 99)),
    ((99, 99, 99, 99, 99, 99), (99, 99, 99, 99, 99, 99)),
)
COUNT_AT = (0, 1, 3, 4, 5, 6, 21, 26, 99, 99, 99, 99)
BACK_AT = (13, 18, 19, 25)
LATE = (
    (3, 0, 0, 0), (1, 5, 1, 1), (1, 2, 1, 3), (1, 1, 0, 4), (2, 0, 0, 8), (0, 8, 0, 1), (0, 6, 0, 5), (0, 8, 1, 1), (3, 0, 0, 1),
    (1, 1, 0, 5), (0, 6, 1, 4), (1, 3, 0, 4), (1, 3, 1, 4), (0, 7, 1, 3), (1, 3, 0, 5), (1, 5, 0, 2), (1, 3, 1, 5), (0, 7, 0, 3),
    (1, 5, 1, 2), (1, 2, 0, 4), (0, 8, 1, 2), (1, 6, 0, 0), (1, 2, 0, 5), (0, 7, 0, 4), (0, 7, 1, 4), (1, 2, 1, 4), (1, 5, 1, 3),
    (1, 2, 1, 5), (0, 8, 0, 2), (0, 8, 1, 3), (1, 6, 0, 1), (1, 5, 0, 3), (1, 4, 0, 0), (1, 4, 1, 0), (0, 7, 0, 5), (2, 0, 0, 9),
    (3, 0, 0, 2), (0, 8, 0, 3), (0, 6, 1, 5), (1, 6, 1, 0), (0, 7, 1, 5), (1, 6, 0, 2), (1, 4, 0, 1), (1, 5, 1, 4), (1, 4, 1, 1),
    (0, 8, 1, 4), (1, 5, 1, 5), (1, 7, 0, 0), (1, 7, 1, 0), (1, 5, 0, 4), (0, 8, 0, 4), (1, 4, 0, 2), (1, 6, 1, 1), (0, 8, 1, 5),
    (1, 8, 1, 0), (2, 0, 0, 10), (1, 4, 1, 2), (1, 7, 1, 1), (1, 5, 0, 5), (3, 0, 0, 3), (1, 7, 0, 1), (0, 8, 0, 5), (1, 8, 0, 0),
    (2, 0, 0, 11), (1, 6, 0, 3), (1, 6, 1, 2), (1, 4, 0, 3), (1, 8, 1, 1), (1, 8, 0, 1), (1, 4, 1, 3), (3, 0, 0, 4), (1, 7, 1, 2),
    (1, 7, 0, 2), (1, 6, 1, 3), (1, 6, 0, 4), (1, 4, 0, 4), (1, 8, 1, 2), (1, 8, 0, 2), (1, 6, 0, 5), (1, 4, 0, 5), (1, 7, 0, 3),
    (3, 0, 0, 5), (1, 4, 1, 4), (1, 7, 1, 3), (1, 4, 1, 5), (1, 6, 1, 4), (1, 8, 0, 3), (1, 8, 1, 3), (1, 7, 0, 4), (1, 6, 1, 5),
    (1, 7, 0, 5), (1, 7, 1, 4), (1, 7, 1, 5), (1, 8, 1, 4), (1, 8, 0, 4), (1, 8, 1, 5), (1, 8, 0, 5),
)


def timetable(nd, gathers, tally_gathers):
    if nd == len(REDUCE_AT[0][0]) - 1:
        ticks = {}
        for j in range(NPAIR):
            for o in range(2):
                ticks |= {(0, j, o, k): t for k, t in enumerate(REDUCE_AT[j][o])}
                ticks |= {(1, j, o, m): t for m, t in enumerate(GATHER_AT[j][o])}
        ticks |= {(2, 0, 0, k): t for k, t in enumerate(COUNT_AT)}
        return {key: t for key, t in ticks.items() if t < DRAIN}, BACK_AT, list(LATE)
    ticks = {}
    for j, t in enumerate(IN_AT):
        for o in range(2):
            ticks |= {(0, j, o, k): t + 3 * k for k in range(nd + 1)}
            ticks |= {(1, j, o, m): max(t + 3 * nd, 20 + 2 * j) + 3 * m for m in range(gathers + 1)}
    ticks |= {(2, 0, 0, k): 2 * k for k in range(nd + 2 + tally_gathers)}
    late = sorted((t, key) for key, t in ticks.items() if t >= DRAIN)
    return {key: t for key, t in ticks.items() if t < DRAIN}, (MID + 1,) * 4, [(3, 0, 0, k) for k in range(nd + 1)] + [key for _, key in late]


def layer_kernel(shape, mol_h, cot_h, wup_h, wdn_h, wqkv_h, wout_h, ids_ref,
                 g1_in, b1_in, qb_ref, ob_in, g2_in, b2_in, ub_in, db_in,
                 lo_out, gm_out, sum_out, cnt_out, vec_out,
                 mid_s, dy_s, a2_s, a2t_s, dyt_s, acc_s, da2_s, wup_s, wdn_s, qkv_s, ctx_s, x_s, wqkv_s, wout_s,
                 dqkv_s, lo_s, gub_s, part_s, fetch_sem, stage_s, vland_s, vacc_s, six_s, ub_s, lacc, lse_s, cnt_s,
                 rs_send, rs_recv, ag_send, ag_recv, keep_sem, crs_send, crs_recv, cag_send, cag_recv, ckeep_sem,
                 v_send, v_recv, t_send, t_recv, t_own, m_send, m_recv, m_own, c_send, c_recv, c_own, *lands):
    ways = orders(shape)
    nd = len(ways["X"])
    nseq = shape["seq"]
    land = lands[:nd]
    cland = lands[nd:]
    rows_idx, me = spots()
    rows, length = x_s.shape[0], x_s.shape[1]
    tokens = rows * length
    local = length // nseq
    near = peers(nseq)
    fc = NB * LANE

    barrier = pltpu.get_barrier_semaphore()
    others = [across(step) for step in ways["X"]]
    others += [(rows_idx, to) for m, to in near if m & (m - 1)]
    for other in others:
        pl.semaphore_signal(barrier, inc=1, device_id=other, device_id_type=MESH)

    here = pl.ds(pl.multiple_of(me * local, local), local)

    def weights(i, slot):
        return (pltpu.make_async_copy(wup_h.at[:, pl.ds(pl.multiple_of(i * fc, fc), fc)], wup_s.at[slot], fetch_sem.at[slot]),
                pltpu.make_async_copy(wdn_h.at[pl.ds(pl.multiple_of(i * fc, fc), fc)], wdn_s.at[slot], fetch_sem.at[2 + slot]))

    fetch = [pltpu.make_async_copy(wqkv_h, wqkv_s, fetch_sem.at[4]), pltpu.make_async_copy(wout_h, wout_s, fetch_sem.at[5])]

    def own(r):
        return pltpu.make_async_copy(mol_h.at[me * rows + r], x_s.at[r, here], m_own.at[r])

    def mol(r, n):
        m, to = near[n]
        return pltpu.make_async_remote_copy(src_ref=mol_h.at[to * rows + r], dst_ref=x_s.at[r, here], send_sem=m_send.at[r, m],
                                            recv_sem=m_recv.at[r, m], device_id=(rows_idx, to), device_id_type=MESH)

    def cot(n):
        m, to = near[n]
        return pltpu.make_async_remote_copy(src_ref=cot_h.at[pl.ds(to * rows, rows)], dst_ref=dy_s.at[:, here],
                                            send_sem=c_send.at[m], recv_sem=c_recv.at[m], device_id=(rows_idx, to),
                                            device_id_type=MESH)

    cot_own = pltpu.make_async_copy(cot_h.at[pl.ds(me * rows, rows)], dy_s.at[:, here], c_own)
    for r in range(rows):
        own(r).start()
    fetch[0].start()
    for n, ref in enumerate((g1_in, b1_in, g2_in, b2_in, db_in, ob_in)):
        six_s[n : n + 1] = ref[...].reshape(1, D)
    ub_s[...] = ub_in[...].reshape(1, FF)
    g1_ref, b1_ref, g2_ref, b2_ref, db_ref, ob_ref = (six_s.at[n : n + 1] for n in range(6))
    ub_ref = ub_s
    pl.semaphore_wait(barrier, len(others))
    for r in range(rows):
        for n in range(len(near)):
            mol(r, n).start()
    fetch[1].start()
    cot_own.start()
    for copy in weights(0, 0):
        copy.start()


    def give_back(which, out, r, n):
        m, to = near[n]
        return pltpu.make_async_remote_copy(
            src_ref=lo_s.at[r, pl.ds(pl.multiple_of(to * local, local), local)], dst_ref=out.at[me * rows + r],
            send_sem=t_send.at[which, r, m], recv_sem=t_recv.at[which, r, m], device_id=(rows_idx, to), device_id_type=MESH)

    def give_self(which, out):
        return pltpu.make_async_copy(lo_s.at[:, pl.ds(pl.multiple_of(me * local, local), local)],
                                     out.at[pl.ds(me * rows, rows)], t_own.at[which])

    def give_wait(which, out):
        give_self(which, out).wait()
        for r in range(rows):
            for n in range(len(near)):
                give_back(which, out, r, n).wait()

    back = [(r, n) for r in range(rows) for n in range(len(near) - 1)]

    tally = Halving(ways[COUNT_WAY], cnt_s.shape[0], cnt_s.shape[1], 8)
    gathers = len(Halving(ways["X"], NB, D, 16).gathers)
    ticks, back_at, late = timetable(nd, gathers, len(tally.gathers))

    def act(kind, j, o, k, which):
        plan = Halving(ways[which], NB, D, 16)
        here = [r.at[j, o] for r in land]
        if kind == 0:
            plan.reduce_step(k, stage_s.at[j % 2, o], here, (rs_send.at[j, o], rs_recv.at[j, o]))
        else:
            plan.gather_step(k, here, sum_out.at[j, o], (ag_send.at[j, o], ag_recv.at[j, o]), keep_sem.at[j, o])

    def act_counts(k):
        if k <= nd:
            tally.reduce_step(k, cnt_s, cland, (crs_send, crs_recv))
        else:
            tally.gather_step(k - nd - 1, cland, cnt_out, (cag_send, cag_recv), ckeep_sem)

    def tick(t, low, high):
        for kind, most in ((0, nd), (1, gathers)):
            for k in reversed(range(most + 1)):
                for o in range(2):
                    for named in sorted(set(way[o] for way in WAYS)):
                        found = [(ticks.get((kind, j, o, k), -1), j) for j in range(NPAIR) if WAYS[j][o] == named]
                        found = [(at, j) for at, j in found if low <= at <= high]
                        assert len({at for at, _ in found}) == len(found)
                        if not found:
                            continue
                        hit = sum(jnp.where(t == at, 1, 0) for at, _ in found)
                        j = sum(jnp.where(t == at, j, 0) for at, j in found)

                        @pl.when(hit == 1)
                        def _():
                            act(kind, j, o, k, named)

        for k in range(nd + 2 + len(tally.gathers)):
            at = ticks.get((2, 0, 0, k), -1)
            if low <= at <= high:

                @pl.when(t == at)
                def _():
                    act_counts(k)

        for n, at in enumerate(back_at):
            if low <= at <= high:

                @pl.when(t == at)
                def _():
                    give_back(0, lo_out, *back[n]).start()

    half = 2 * local

    def project(r, at):
        src = pl.ds(pl.multiple_of(at, half), half)
        dst = pl.ds(pl.multiple_of(r * length + at, half), half)
        xhat, _ = norm_parts(x_s[r, src].astype(F32))
        a1 = (xhat * g1_ref[...] + b1_ref[...]).astype(BF)
        for c in range(3):
            cols = slice(c * D, (c + 1) * D)
            part = dot_nn(a1, wqkv_s[:, cols])
            qkv_s[dst, cols] = (part if c == 1 else part + qb_ref[c // 2 : c // 2 + 1]).astype(BF)

    for r in range(rows):
        own(r).wait()
        mol(r, len(near) - 1).wait()
    fetch[0].wait()
    mine = (me // 2) * half

    def early(r, carry):
        project(r, mine)
        return carry

    lax.fori_loop(0, rows, early, 0)

    hashes, id_rows, chars = ids_ref.shape
    high = BUCKETS // LANE

    def bucket(h, carry):
        total = jnp.zeros((high, LANE), F32)
        for r in range(id_rows):
            ids = ids_ref[h, r : r + 1, :]
            row = lax.broadcasted_iota(jnp.int32, (high, chars), 0)
            hi = jnp.where(row == (ids >> 7), 1.0, 0.0).astype(BF)
            lo = jnp.where(row == (ids & (LANE - 1)), 1.0, 0.0).astype(BF)
            total = total + dot_nt(hi, lo)
        cnt_s[:, pl.ds(h, 1), :] = total.astype(jnp.int32).reshape(high, 1, LANE)
        return carry

    lax.fori_loop(0, hashes, bucket, 0)
    fetch[1].wait()
    early_counts = [k for k, t in enumerate(COUNT_AT) if t < 0] if nd == len(COUNT_AT) // 2 - 1 else []

    for r in range(rows):
        for n in range(len(near) - 1):
            mol(r, n).wait()
        for other in range(1, nseq // 2):
            project(r, ((me // 2 + other) % (nseq // 2)) * half)
        tok = slice(r * length, (r + 1) * length)

        def pair(p):
            at = pl.multiple_of(p * LANE, LANE)
            q = qkv_s[tok, pl.ds(at, LANE)] * BF(0.125)
            k = qkv_s[tok, pl.ds(pl.multiple_of(D + at, LANE), LANE)]
            v = qkv_s[tok, pl.ds(pl.multiple_of(2 * D + at, LANE), LANE)]
            ctx = []
            lse = lacc[...]
            lane = lax.broadcasted_iota(jnp.int32, lse.shape, 1)
            for half_of in range(2):
                qm = jnp.where(lane_half(q.shape, half_of), q, BF(0))
                s = dot_nt(qm, k)
                m = jnp.max(s, -1, keepdims=True)
                e = jnp.exp(s - m)
                t = jnp.sum(e, -1, keepdims=True)
                pr = (e * (1.0 / t)).astype(BF)
                ctx.append(dot_nn(pr, v))
                lse = jnp.where(lane == 2 * p + half_of, m + jnp.log(t), lse)
            lacc[...] = lse
            ctx_s[tok, pl.ds(at, LANE)] = jnp.where(lane_half(ctx[0].shape, 0), ctx[0], ctx[1]).astype(BF)

        lacc[...] = jnp.zeros_like(lacc)
        def some(i, carry):
            for n in range(TOGETHER):
                pair(TOGETHER * i + n)
            return carry

        ends = (0, 4 // TOGETHER, NH // (2 * TOGETHER))
        for part in range(2):
            lax.fori_loop(ends[part], ends[part + 1], some, 0)
            if r == 0 and part == 0:
                for n in range(len(near)):
                    cot(n).start()
            if 2 * r + part in early_counts:
                act_counts(2 * r + part)
        lt = lacc[...].T
        for h in range(NH):
            lse_s[r * NH + h] = lt[h : h + 1, :]
        mid_s[tok] = x_s[r].astype(F32) + (dot_nn(ctx_s[tok], wout_s[...]) + ob_ref[...])

    step = 256
    pieces = tokens // step

    def piece(n):
        at = pl.ds(pl.multiple_of(n * step, step), step)
        return at, (n * step // length, pl.ds(pl.multiple_of((n * step) % length, step), step))

    cot_own.wait()
    for n in range(len(near)):
        cot(n).wait()

    def open_piece(n, carry):
        at, row_at = piece(n)
        mid = mid_s[at]
        xhat, _ = norm_parts(mid)
        a2 = (xhat * g2_ref[...] + b2_ref[...]).astype(BF)
        a2_s[at] = a2
        a2t_s[:, at] = a2.T
        dyt_s[:, at] = dy_s[row_at].T
        acc_s[at] = mid + db_ref[...]
        da2_s[at] = jnp.zeros((step, D), F32)
        return carry

    lax.fori_loop(0, pieces, open_piece, 0)

    def ff(i, carry):
        slot = i % 2

        @pl.when(i + 1 < NFF)
        def _():
            for copy in weights(i + 1, 1 - slot):
                copy.start()

        for copy in weights(i, slot):
            copy.wait()
        cols = pl.ds(pl.multiple_of(i * fc, fc), fc)
        u = dot_nn(a2_s[...], wup_s[slot]) + ub_ref[:, cols]
        dh = dot_nt(dy_s[...].reshape(tokens, D), wdn_s[slot])
        cdf = 0.5 + 0.5 * lax.erf(u * (2.0 ** -0.5))
        pdf = jnp.exp(u * u * -0.5) * 0.3989422804014327
        hid = (u * cdf).astype(BF)
        du = (dh * (cdf + u * pdf)).astype(BF)
        gub_s[:, cols] = jnp.sum(du.astype(F32), 0, keepdims=True)
        tick(SPLIT * i, 0, MID - 1)
        acc_s[...] += dot_nn(hid, wdn_s[slot])
        da2_s[...] += dot_nt(du, wup_s[slot])
        gd = dot_nn(dyt_s[...], hid).astype(BF)
        gu = dot_nn(a2t_s[...], du).astype(BF)
        for b in range(NB):
            stage_s[slot, 0, b] = gd[:, b * LANE : (b + 1) * LANE]
            stage_s[slot, 1, b] = gu[:, b * LANE : (b + 1) * LANE]
        tick(SPLIT * i + SPLIT - 1, 0, MID - 1)
        return carry

    lax.fori_loop(0, NFF, ff, 0)

    part_s[...] = jnp.zeros_like(part_s)

    def turn_piece(n, carry):
        at, row_at = piece(n)
        lo_s[row_at] = acc_s[at].astype(BF)
        dy = dy_s[row_at].astype(F32)
        xhat, rstd = norm_parts(mid_s[at])
        da2 = da2_s[at]
        dx2 = dy + norm_back(xhat, rstd, g2_ref[...], da2)
        da2_s[at] = dx2
        do = dx2.astype(BF)
        a2_s[at] = do
        part_s[0:1] += jnp.sum(dy, 0, keepdims=True)
        part_s[1:2] += jnp.sum(da2 * xhat, 0, keepdims=True)
        part_s[2:3] += jnp.sum(da2, 0, keepdims=True)
        part_s[3:4] += jnp.sum(do.astype(F32), 0, keepdims=True)
        dy_s[row_at] = dot_nt(do, wout_s[...]).astype(BF)
        return carry

    lax.fori_loop(0, pieces, turn_piece, 0)
    dctx_s, do_s, dx2_s, da1_s, a1t_s = dy_s, a2_s, da2_s, acc_s, a2t_s
    give_self(0, lo_out).start()
    for r in range(rows):
        give_back(0, lo_out, r, len(near) - 1).start()
    tick(MID, MID, MID)
    gout_s = dyt_s
    gout_s[:, 0:D] = dot_tn(ctx_s[...], do_s[...]).astype(BF)

    def first_norm(n, carry):
        at, row_at = piece(n)
        xhat, _ = norm_parts(x_s[row_at].astype(F32))
        a1t_s[:, at] = (xhat * g1_ref[...] + b1_ref[...]).astype(BF).T
        da1_s[at] = jnp.zeros((step, D), F32)
        return carry

    lax.fori_loop(0, pieces, first_norm, 0)
    tick(MID + 1, MID + 1, MID + 1)

    def group(g, carry):
        def unit(r, h):
            p = 2 * g + h
            tok = pl.ds(pl.multiple_of(r * length, length), length)
            cq = pl.ds(pl.multiple_of(p * LANE, LANE), LANE)
            q = qkv_s[tok, cq] * BF(0.125)
            k = qkv_s[tok, pl.ds(pl.multiple_of(p * LANE + D, LANE), LANE)]
            v = qkv_s[tok, pl.ds(pl.multiple_of(p * LANE + 2 * D, LANE), LANE)]
            dc = dctx_s[r, :, cq]
            dqs, dks, dvs = [], [], []
            for half in range(2):
                keep = lane_half(k.shape, half)
                km = jnp.where(keep, k, BF(0))
                vm = jnp.where(keep, v, BF(0))
                lse = lse_s[r * NH + 2 * p + half]
                st = dot_nt(km, q)
                pt = jnp.exp(st - lse)
                dpt = dot_nt(vm, dc)
                inner = jnp.sum(pt * dpt, 0, keepdims=True)
                dst = (pt * (dpt - inner)).astype(BF)
                dvs.append(dot_nn(pt.astype(BF), dc))
                dks.append(dot_nn(dst, q))
                dqs.append(dot_tn(dst, k))
            sel = lane_half(dqs[0].shape, 0)
            dqkv_s[tok, pl.ds(pl.multiple_of(h * LANE, LANE), LANE)] = (jnp.where(sel, dqs[0], dqs[1]) * 0.125).astype(BF)
            dqkv_s[tok, pl.ds(pl.multiple_of(h * LANE + 2 * LANE, LANE), LANE)] = jnp.where(sel, dks[0], dks[1]).astype(BF)
            dqkv_s[tok, pl.ds(pl.multiple_of(h * LANE + 4 * LANE, LANE), LANE)] = jnp.where(sel, dvs[0], dvs[1]).astype(BF)

        def both_halves(n, inner_carry):
            unit(n, 0)
            unit(n, 1)
            tick(MID + 2 + 5 * g + 2 * n, MID + 2, DRAIN - 1)
            tick(MID + 3 + 5 * g + 2 * n, MID + 2, DRAIN - 1)
            return inner_carry

        lax.fori_loop(0, rows, both_halves, 0)
        slot = (NFF + g) % 2
        grads = dot_nn(a1t_s[...], dqkv_s[...]).astype(BF)
        for b in range(6):
            stage_s[slot, b // NB, b % NB] = grads[:, b * LANE : (b + 1) * LANE]
        for b in range(2):
            stage_s[slot, 1, 2 + b] = gout_s[:, pl.ds(pl.multiple_of((2 * g + b) * LANE, LANE), LANE)]
        two = 2 * LANE
        for c in range(3):
            at = pl.ds(pl.multiple_of(c * D + g * two, two), two)
            da1_s[...] += dot_nt(dqkv_s[:, c * two : (c + 1) * two], wqkv_s[:, at])
        here = pl.ds(pl.multiple_of(g * two, two), two)
        part_s[6:7, here] = jnp.sum(dqkv_s[:, 0:two].astype(F32), 0, keepdims=True)
        part_s[7:8, here] = jnp.sum(dqkv_s[:, 2 * two : 3 * two].astype(F32), 0, keepdims=True)
        tick(MID + 6 + 5 * g, MID + 2, DRAIN - 1)
        return carry

    lax.fori_loop(0, 3, group, 0)

    give_wait(0, lo_out)

    def last_piece(n, carry):
        at, row_at = piece(n)
        xhat, rstd = norm_parts(x_s[row_at].astype(F32))
        da1 = da1_s[at]
        part_s[4:5] += jnp.sum(da1 * xhat, 0, keepdims=True)
        part_s[5:6] += jnp.sum(da1, 0, keepdims=True)
        gm = dx2_s[at] + norm_back(xhat, rstd, g1_ref[...], da1)
        lo_s[row_at] = gm.astype(BF)
        return carry

    lax.fori_loop(0, pieces, last_piece, 0)
    give_self(1, gm_out).start()
    for r in range(rows):
        for n in range(len(near)):
            give_back(1, gm_out, r, n).start()
    vacc_s[0, 0:8] = part_s[...]
    for b in range(FF // (2 * LANE)):
        vacc_s[0, 8 + b // 3 : 9 + b // 3, (b % 3) * 2 * LANE : (b % 3 + 1) * 2 * LANE] = gub_s[:, b * 2 * LANE : (b + 1) * 2 * LANE]
    vacc_s[0, 12:16] = jnp.zeros((4, D), F32)

    def swap(i):
        return pltpu.make_async_remote_copy(src_ref=vacc_s.at[i], dst_ref=vland_s.at[i], send_sem=v_send.at[i], recv_sem=v_recv.at[i],
                                            device_id=across(ways["X"][i]), device_id_type=MESH)

    for kind, j, o, k in late:
        if kind < 2:
            act(kind, j, o, k, WAYS[j][o])
        elif kind == 2:
            act_counts(k)
        else:
            if k > 0:
                swap(k - 1).wait()
                vacc_s[k] = vacc_s[k - 1] + vland_s[k - 1]
            if k < nd:
                swap(k).start()
    vec_out[...] = vacc_s[nd]
    give_wait(1, gm_out)


def layer(shape, mol, cot, wup, wdn, wqkv, wout, ids, g1, b1, qb, ob, g2, b2, ub, db):
    nseq = shape["seq"]
    local = mol.shape[1]
    rows, length = mol.shape[0] // nseq, local * nseq
    tokens = rows * length
    nd = len(orders(shape)["X"])
    vm, hb = pl.BlockSpec(memory_space=pltpu.VMEM), pl.BlockSpec(memory_space=pl.ANY)
    dma = pltpu.SemaphoreType.DMA
    V = pltpu.VMEM
    sds = jax.ShapeDtypeStruct
    fc = NB * LANE
    cnt = (BUCKETS // LANE, ids.shape[0], LANE)
    scratch = [
        V((tokens, D), F32), V((rows, length, D), BF), V((tokens, D), BF), V((D, tokens), BF), V((D, tokens), BF), V((tokens, D), F32),
        V((tokens, D), F32), V((2, D, fc), BF), V((2, fc, D), BF), V((tokens, 3 * D), BF), V((tokens, D), BF), V((rows, length, D), BF),
        V((D, 3 * D), BF), V((D, D), BF), V((tokens, D), BF), V((rows, length, D), BF),
        V((1, FF), F32), V((8, D), F32), dma((6,)), V((2, 2, NB, D, LANE), BF), V((nd, 16, D), F32), V((nd + 1, 16, D), F32),
        V((8, D), F32), V((1, FF), F32), V((length, LANE), F32), V((rows * NH, 1, length), F32), V(cnt, jnp.int32),
        dma((NPAIR, 2, nd)), dma((NPAIR, 2, nd)), dma((NPAIR, 2, nd)), dma((NPAIR, 2, nd)), dma((NPAIR, 2)),
        dma((nd,)), dma((nd,)), dma((nd,)), dma((nd,)), dma, dma((nd,)), dma((nd,)), dma((2, rows, nseq)), dma((2, rows, nseq)), dma((2,)),
        dma((rows, nseq)), dma((rows, nseq)), dma((rows,)), dma((nseq,)), dma((nseq,)), dma,
    ]
    scratch += land_shapes((NPAIR, 2), NB, D, 16, nd, BF)
    scratch += land_shapes((), cnt[0], cnt[1], 8, nd, jnp.int32)
    return pl.pallas_call(
        functools.partial(layer_kernel, shape),
        in_specs=[hb] * 6 + [vm] * 9,
        out_specs=[hb, hb, hb, hb, vm],
        out_shape=[sds((rows * nseq, local, D), BF), sds((rows * nseq, local, D), BF), sds((NPAIR, 2, NB, D, LANE), BF),
                   sds(cnt, jnp.int32), sds((16, D), F32)],
        scratch_shapes=scratch,
        compiler_params=pltpu.CompilerParams(vmem_limit_bytes=63 * MIB, collective_id=0, has_side_effects=True),
        name="layer",
    )(mol, cot, wup, wdn, wqkv, wout, ids, g1, b1, qb, ob, g2, b2, ub, db)


def widen_kernel(src_ref, gm_ref, lo_ref, vec_ref, cnt_ref, gmol_ref, lout_ref, counts_ref, g1_ref, b1_ref, qb_ref, ob_ref, g2_ref,
                 b2_ref, ub_ref, db_ref, qkv_out, out_out, up_out, down_out, wide_s, tall_s, sem):
    j = pl.program_id(0)
    slot = j % 2
    fc = NB * LANE
    two = 2 * LANE

    def first(i, s):
        at = pl.ds(pl.multiple_of(i * fc, fc), fc)
        return [pltpu.make_async_copy(tall_s.at[s], down_out.at[at], sem.at[s, 0]),
                pltpu.make_async_copy(wide_s.at[s, 0], up_out.at[:, at], sem.at[s, 1])]

    def later(i, s):
        g = i - NFF
        to = lambda c: pl.ds(pl.multiple_of(c * D + g * two, two), two)
        return [pltpu.make_async_copy(wide_s.at[s, 0, :, 0:two], qkv_out.at[:, to(0)], sem.at[s, 0]),
                pltpu.make_async_copy(wide_s.at[s, 0, :, two : 2 * two], qkv_out.at[:, to(1)], sem.at[s, 1]),
                pltpu.make_async_copy(wide_s.at[s, 1, :, 0:two], qkv_out.at[:, to(2)], sem.at[s, 2]),
                pltpu.make_async_copy(wide_s.at[s, 1, :, two : 2 * two], out_out.at[:, to(0)], sem.at[s, 3])]

    def finish(i, s):
        @pl.when(i < NFF)
        def _():
            for copy in first(i, s):
                copy.wait()

        @pl.when(i >= NFF)
        def _():
            for copy in later(i, s):
                copy.wait()

    @pl.when(j >= 2)
    def _():
        finish(j - 2, slot)

    gmol_ref[...] = gm_ref[...].astype(F32)
    lout_ref[...] = lo_ref[...]

    @pl.when(j == 0)
    def _():
        for n, ref in ((0, db_ref), (1, g2_ref), (2, b2_ref), (3, ob_ref), (4, g1_ref), (5, b1_ref)):
            ref[...] = vec_ref[n : n + 1].reshape(D)
        qb_ref[...] = vec_ref[6:8]
        ub_ref[...] = jnp.concatenate([vec_ref[n : n + 1] for n in range(8, 12)], 1).reshape(FF)
        for n in range(cnt_ref.shape[0]):
            counts_ref[:, n * LANE : (n + 1) * LANE] = cnt_ref[n]

    @pl.when(j < NFF)
    def _():
        for b in range(NB):
            at = slice(b * LANE, (b + 1) * LANE)
            tall_s[slot, at, :] = src_ref[0, 0, b].astype(F32).T
            wide_s[slot, 0, :, at] = src_ref[0, 1, b].astype(F32)
        for copy in first(j, slot):
            copy.start()

    @pl.when(j >= NFF)
    def _():
        for o in range(2):
            for b in range(NB):
                wide_s[slot, o, :, b * LANE : (b + 1) * LANE] = src_ref[0, o, b].astype(F32)
        for copy in later(j, slot):
            copy.start()

    @pl.when(j == NPAIR - 1)
    def _():
        finish(j - 1, 1 - slot)
        finish(j, slot)


def widen(sums, gm, lo, vec, cnt):
    hb = pl.BlockSpec(memory_space=pl.ANY)
    vm = pl.BlockSpec(memory_space=pltpu.VMEM)
    sds = jax.ShapeDtypeStruct
    one = sds((D,), F32)
    rows = gm.shape[0]
    some = pl.BlockSpec((1,) + gm.shape[1:], lambda j: (jnp.minimum(j, rows - 1), 0, 0))
    return pl.pallas_call(
        widen_kernel,
        grid=(NPAIR,),
        in_specs=[pl.BlockSpec((1, 2, NB, D, LANE), lambda j: (j, 0, 0, 0, 0)), some, some, vm, vm],
        out_specs=[some, some] + [vm] * 9 + [hb] * 4,
        out_shape=[sds(gm.shape, F32), sds(lo.shape, BF), sds((cnt.shape[1], BUCKETS), jnp.int32), one, one, sds((2, D), F32), one, one,
                   one, sds((FF,), F32), one, sds((D, 3 * D), F32), sds((D, D), F32), sds((D, FF), F32), sds((FF, D), F32)],
        scratch_shapes=[pltpu.VMEM((2, 2, D, NB * LANE), F32), pltpu.VMEM((2, NB * LANE, D), F32), pltpu.SemaphoreType.DMA((2, 4))],
        compiler_params=pltpu.CompilerParams(vmem_limit_bytes=60 * MIB),
        name="widen",
    )(sums, gm, lo, vec, cnt)


def on_device(shape, molecules, ln1_gain, ln1_bias, w_qkv, qkv_bias, w_out, out_bias, ln2_gain, ln2_bias, w_up, up_bias,
              w_down, down_bias, out_cotangent, bucket_ids):
    layer_out, gm, sums, counts, vec = layer(shape, molecules, out_cotangent, w_up, w_down, w_qkv, w_out, bucket_ids, ln1_gain, ln1_bias,
                                             qkv_bias, out_bias, ln2_gain, ln2_bias, up_bias, down_bias)
    (g_mol, layer_out, counts, g_g1, g_b1, g_qb, g_ob, g_g2, g_b2, g_ub, g_db, g_qkv, g_out, g_up,
     g_down) = widen(sums, gm, layer_out, vec, counts)
    return (layer_out, g_mol, g_g1, g_b1, g_qkv, g_qb, g_out, g_ob, g_g2, g_b2, g_up, g_ub, g_down, g_db, counts)


def solution(mesh):
    tok = P("rows", "seq", None)
    return jax.shard_map(
        functools.partial(on_device, dict(mesh.shape)),
        mesh=mesh,
        in_specs=(tok,) + (P(),) * 12 + (tok, P(None, "rows", "seq")),
        out_specs=(tok, tok) + (P(),) * 13,
        check_vma=False,
    )
```

```python
import functools
import jax
import jax.numpy as jnp
from jax import lax
from jax.experimental import pallas as pl
from jax.experimental.pallas import tpu as pltpu
from jax.sharding import PartitionSpec as P

MESH = pl.DeviceIdType.MESH
BF = jnp.bfloat16
F32 = jnp.float32
EPS = 1e-5
D = 768
HD = 64
NH = 12
FF = 3072
BUCKETS = 16384
LANE = 128
MIB = 1 << 20


def dot_nn(a, b):
    return lax.dot_general(a, b, (((1,), (0,)), ((), ())), preferred_element_type=F32)


def dot_nt(a, b):
    return lax.dot_general(a, b, (((1,), (1,)), ((), ())), preferred_element_type=F32)


def dot_tn(a, b):
    return lax.dot_general(a, b, (((0,), (0,)), ((), ())), preferred_element_type=F32)


def norm_parts(x):
    mean = jnp.mean(x, -1, keepdims=True)
    cen = x - mean
    var = jnp.mean(cen * cen, -1, keepdims=True)
    rstd = lax.rsqrt(var + EPS)
    return cen * rstd, rstd


def norm_back(xhat, rstd, gain, dy):
    dxh = dy * gain
    m1 = jnp.mean(dxh, -1, keepdims=True)
    m2 = jnp.mean(dxh * xhat, -1, keepdims=True)
    return rstd * (dxh - m1 - xhat * m2)


def lane_half(shape, half):
    lane = lax.broadcasted_iota(jnp.int32, shape, 1)
    return (lane < HD) if half == 0 else (lane >= HD)


NB = 4
NFF = FF // (NB * LANE)
NPAIR = NFF + 3


def spots():
    return lax.axis_index("rows"), lax.axis_index("seq")


def bit_of(step):
    axis, mask = step
    return (lax.axis_index(axis) // mask) % 2


def across(step):
    axis, mask = step
    rows, seq = spots()
    move = mask - 2 * mask * bit_of(step)
    return (rows + move, seq) if axis == "rows" else (rows, seq + move)


def orders(shape):
    seq = [("seq", 1 << b) for b in range(shape["seq"].bit_length() - 1)]
    row = [("rows", 1 << b) for b in range(shape["rows"].bit_length() - 1)]
    first, rest, near, far = seq[:1], seq[1:], row[:1], row[1:]
    named = {"W": near + far + rest, "X": rest + near + far, "Y": near + rest + far, "Z": far + near + rest,
             "V": rest + far + near, "U": far + rest + near}
    return {name: first + then for name, then in named.items()}


class Halving:
    def __init__(self, order, lead, rows, tile):
        self.order, self.tile = order, tile
        self.size, self.split, self.lead_at, self.row_at, self.own = [], [], [], [], []
        lead_at, row_at = 0, 0
        for i, step in enumerate(order):
            bit = bit_of(step)
            if lead > 1:
                lead //= 2
                how = 0
                if i == 0:
                    self.first = bit * lead
                else:
                    lead_at = lead_at + bit * lead
            elif rows % (2 * tile) == 0:
                rows //= 2
                how = 1
                row_at = row_at + bit * rows
            else:
                how = None
            self.own.append(bit)
            self.split.append(how)
            self.size.append((lead, rows))
            self.lead_at.append(lead_at)
            self.row_at.append(row_at)
        self.gathers = [i for i in reversed(range(len(order))) if self.split[i] is not None]

    def partner(self, i):
        return across(self.order[i])

    def rows_of(self, at, size):
        return pl.ds(pl.multiple_of(at, self.tile), size)

    def send(self, i, mine, land, sems):
        lead, rows = self.size[i]
        if i == 0:
            src = mine.at[pl.ds(lead - self.first, lead)]
        else:
            la, ra = self.lead_at[i - 1], self.row_at[i - 1]
            if self.split[i] == 0:
                la = la + (1 - self.own[i]) * lead
            elif self.split[i] == 1:
                ra = ra + (1 - self.own[i]) * rows
            src = land[0].at[pl.ds(la, lead), self.rows_of(ra, rows)]
        return pltpu.make_async_remote_copy(src_ref=src, dst_ref=land[i], send_sem=sems[0].at[i], recv_sem=sems[1].at[i],
                                            device_id=self.partner(i), device_id_type=MESH)

    def add(self, i, mine, land):
        lead, rows = self.size[i]
        part = rows if rows <= LANE else 96
        wide = F32 if land[0].dtype == BF else land[0].dtype

        def some(t, carry):
            at = t * part
            if i == 0:
                here = (slice(None), self.rows_of(at, part))
                left, right = land[0][here], mine[pl.ds(self.first, lead), self.rows_of(at, part)]
            else:
                here = (pl.ds(self.lead_at[i], lead), self.rows_of(self.row_at[i] + at, part))
                left, right = land[0][here], land[i][:, self.rows_of(at, part)]
            land[0][here] = (left.astype(wide) + right.astype(wide)).astype(land[0].dtype)
            return carry

        lax.fori_loop(0, rows // part, some, 0)

    def at_level(self, i):
        lead, rows = self.size[i]
        return pl.ds(self.lead_at[i], lead), self.rows_of(self.row_at[i], rows)

    def out_level(self, i):
        lead, rows = self.size[i]
        return pl.ds(self.first + self.lead_at[i], lead), self.rows_of(self.row_at[i], rows)

    def keep(self, land, out, sem):
        last = len(self.order) - 1
        return pltpu.make_async_copy(land[0].at[self.at_level(last)], out.at[self.out_level(last)], sem)

    def gather(self, m, land, out, sems):
        i = self.gathers[m]
        here = out.at[self.out_level(i)]
        src = land[0].at[self.at_level(len(self.order) - 1)] if m == 0 else here
        return pltpu.make_async_remote_copy(src_ref=src, dst_ref=here, send_sem=sems[0].at[m], recv_sem=sems[1].at[m],
                                            device_id=self.partner(i), device_id_type=MESH)

    def reduce_step(self, k, mine, land, sems):
        n = len(self.order)
        if k > 0:
            self.send(k - 1, mine, land, sems).wait()
            self.add(k - 1, mine, land)
        if k < n:
            self.send(k, mine, land, sems).start()

    def gather_step(self, m, land, out, sems, sem):
        if m == 0:
            self.keep(land, out, sem).start()
        else:
            if m == 1:
                self.keep(land, out, sem).wait()
            self.gather(m - 1, land, out, sems).wait()
        if m < len(self.gathers):
            self.gather(m, land, out, sems).start()


def land_shapes(count, lead, rows, tile, steps, dtype):
    shapes = []
    for _ in range(steps):
        if lead > 1:
            lead //= 2
        elif rows % (2 * tile) == 0:
            rows //= 2
        shapes.append(pltpu.VMEM(count + (lead, rows, LANE), dtype))
    return shapes


def peers(nseq):
    me = lax.axis_index("seq")
    found = []
    for m in sorted(range(1, nseq), key=lambda m: -(m >> 1)):
        to = 0
        for b in range(nseq.bit_length() - 1):
            bit = (me // (1 << b)) % 2
            to = to + (bit + ((m >> b) & 1) * (1 - 2 * bit)) * (1 << b)
        found.append((m, to))
    return found


SPLIT = 2
TOGETHER = 2
MID = SPLIT * NFF
DRAIN = MID + 17
IN_AT = tuple(SPLIT * (j + 1) - 1 for j in range(NFF)) + (MID + 6, MID + 11, MID + 16)
COUNT_WAY = 'U'
WAYS = (
    ('Y', 'Y'), ('Y', 'X'), ('Z', 'W'), ('W', 'Y'), ('X', 'Y'), ('W', 'Y'), ('W', 'W'), ('Y', 'V'), ('Z', 'X'),
)
REDUCE_AT = (
    ((1, 2, 4, 6, 7, 9), (1, 2, 6, 8, 9, 11)),
    ((3, 4, 7, 9, 11, 13), (3, 4, 7, 9, 11, 13)),
    ((5, 6, 8, 10, 12, 13), (5, 6, 8, 10, 12, 13)),
    ((7, 8, 10, 12, 14, 18), (7, 8, 11, 13, 15, 18)),
    ((9, 10, 12, 13, 16, 18), (9, 10, 13, 17, 19, 21)),
    ((11, 12, 15, 18, 21, 26), (11, 12, 17, 21, 25, 28)),
    ((18, 19, 24, 28, 99, 99), (18, 19, 26, 99, 99, 99)),
    ((23, 24, 99, 99, 99, 99), (23, 24, 99, 99, 99, 99)),
    ((28, 99, 99, 99, 99, 99), (28, 99, 99, 99, 99, 99)),
)
GATHER_AT = (
    ((9, 10, 12, 14, 19, 21), (11, 12, 14, 18, 21, 23)),
    ((13, 14, 16, 19, 28, 99), (13, 14, 16, 19, 24, 26)),
    ((13, 16, 19, 23, 28, 99), (13, 16, 19, 23, 28, 99)),
    ((18, 21, 26, 99, 99, 99), (18, 19, 24, 99, 99, 99)),
    ((18, 19, 24, 99, 99, 99), (21, 24, 28, 99, 99, 99)),
    ((26, 99, 99, 99, 99, 99), (28, 99, 99, 99, 99, 99)),
    ((99, 99, 99, 99, 99, 99), (99, 99, 99, 99, 99, 99)),
    ((99, 99, 99, 99, 99, 99), (99, 99, 99, 99, 99, 99)),
    ((99, 99, 99, 99, 99, 99), (99, 99, 99, 99, 99, 99)),
)
COUNT_AT = (-1, -1, -1, -1, 0, 1, 1, 2, 3, 5, 7, 8)
BACK_AT = (21, 13, 17, 22)
LATE = (
    (3, 0, 0, 0), (0, 7, 1, 2), (0, 6, 1, 3), (0, 8, 0, 1), (0, 8, 1, 1), (1, 3, 1, 3), (1, 3, 0, 3), (4, 0, 0, 0), (1, 5, 0, 1),
    (1, 1, 0, 5), (1, 5, 1, 1), (1, 2, 0, 5), (0, 7, 0, 2), (1, 2, 1, 5), (3, 0, 0, 1), (1, 4, 1, 3), (4, 0, 0, 1), (0, 6, 0, 4),
    (1, 4, 0, 3), (0, 7, 1, 3), (0, 6, 1, 4), (0, 8, 1, 2), (1, 3, 1, 4), (1, 3, 1, 5), (0, 8, 0, 2), (1, 5, 1, 2), (1, 5, 0, 2),
    (1, 3, 0, 4), (0, 7, 0, 3), (1, 3, 0, 5), (0, 7, 1, 4), (3, 0, 0, 2), (1, 4, 1, 4), (1, 4, 1, 5), (0, 8, 0, 3), (1, 5, 0, 3),
    (0, 8, 1, 3), (0, 7, 1, 5), (0, 6, 0, 5), (1, 6, 0, 0), (1, 7, 1, 0), (0, 7, 0, 4), (3, 0, 0, 3), (0, 8, 0, 4), (0, 8, 1, 4),
    (0, 7, 0, 5), (1, 7, 0, 0), (3, 0, 0, 4), (1, 4, 0, 4), (4, 0, 0, 2), (0, 6, 1, 5), (1, 6, 1, 0), (0, 8, 1, 5), (1, 8, 1, 0),
    (1, 4, 0, 5), (1, 7, 0, 1), (1, 5, 0, 4), (1, 7, 1, 1), (1, 5, 1, 3), (1, 6, 0, 1), (0, 8, 0, 5), (1, 8, 0, 0), (1, 5, 0, 5),
    (3, 0, 0, 5), (1, 8, 1, 1), (1, 7, 0, 2), (1, 7, 1, 2), (4, 0, 0, 3), (1, 6, 1, 1), (1, 5, 1, 4), (1, 8, 0, 1), (1, 6, 0, 2),
    (1, 8, 1, 2), (1, 5, 1, 5), (1, 7, 0, 3), (1, 8, 0, 2), (1, 7, 1, 3), (1, 8, 1, 3), (1, 6, 1, 2), (1, 6, 0, 3), (1, 7, 0, 4),
    (1, 6, 1, 3), (1, 8, 0, 3), (1, 7, 1, 4), (1, 7, 0, 5), (1, 7, 1, 5), (1, 6, 0, 4), (1, 8, 1, 4), (1, 6, 0, 5), (1, 8, 0, 4),
    (1, 8, 1, 5), (1, 6, 1, 4), (1, 8, 0, 5), (1, 6, 1, 5),
)


def timetable(nd, gathers, tally_gathers):
    if nd == len(REDUCE_AT[0][0]) - 1:
        ticks = {}
        for j in range(NPAIR):
            for o in range(2):
                ticks |= {(0, j, o, k): t for k, t in enumerate(REDUCE_AT[j][o])}
                ticks |= {(1, j, o, m): t for m, t in enumerate(GATHER_AT[j][o])}
        ticks |= {(2, 0, 0, k): t for k, t in enumerate(COUNT_AT)}
        return {key: t for key, t in ticks.items() if t < DRAIN}, BACK_AT, list(LATE)
    ticks = {}
    for j, t in enumerate(IN_AT):
        for o in range(2):
            ticks |= {(0, j, o, k): t + 3 * k for k in range(nd + 1)}
            ticks |= {(1, j, o, m): max(t + 3 * nd, 20 + 2 * j) + 3 * m for m in range(gathers + 1)}
    ticks |= {(2, 0, 0, k): 2 * k for k in range(nd + 2 + tally_gathers)}
    late = sorted((t, key) for key, t in ticks.items() if t >= DRAIN)
    return {key: t for key, t in ticks.items() if t < DRAIN}, (MID + 1,) * 4, [(4, 0, 0, k) for k in range(4)] + [(3, 0, 0, k) for k in range(nd + 1)] + [key for _, key in late]


def layer_kernel(shape, mol_h, cot_h, wup_h, wdn_h, wqkv_h, wout_h, ids_ref,
                 g1_in, b1_in, qb_ref, ob_in, g2_in, b2_in, ub_in, db_in,
                 lo_out, gm_out, sum_out, cnt_out, vec_out,
                 mid_s, dy_s, a2_s, a2t_s, dyt_s, acc_s, da2_s, wup_s, wdn_s, qkv_s, ctx_s, x_s, wqkv_s, wout_s,
                 dqkv_s, lo_s, gub_s, part_s, fetch_sem, stage_s, vland_s, vacc_s, six_s, ub_s, lacc, lse_s, cnt_s,
                 rs_send, rs_recv, ag_send, ag_recv, keep_sem, crs_send, crs_recv, cag_send, cag_recv, ckeep_sem,
                 v_send, v_recv, t_send, t_recv, t_own, m_send, m_recv, m_own, c_send, c_recv, c_own, *lands):
    ways = orders(shape)
    nd = len(ways["X"])
    nseq = shape["seq"]
    land = lands[:nd]
    cland = lands[nd:]
    rows_idx, me = spots()
    rows, length = x_s.shape[0], x_s.shape[1]
    tokens = rows * length
    local = length // nseq
    near = peers(nseq)
    fc = NB * LANE

    barrier = pltpu.get_barrier_semaphore()
    others = [across(step) for step in ways["X"]]
    others += [(rows_idx, to) for m, to in near if m & (m - 1)]
    for other in others:
        pl.semaphore_signal(barrier, inc=1, device_id=other, device_id_type=MESH)

    here = pl.ds(pl.multiple_of(me * local, local), local)

    def weights(i, slot):
        return (pltpu.make_async_copy(wup_h.at[:, pl.ds(pl.multiple_of(i * fc, fc), fc)], wup_s.at[slot], fetch_sem.at[slot]),
                pltpu.make_async_copy(wdn_h.at[pl.ds(pl.multiple_of(i * fc, fc), fc)], wdn_s.at[slot], fetch_sem.at[2 + slot]))

    fetch = [pltpu.make_async_copy(wqkv_h, wqkv_s, fetch_sem.at[4]), pltpu.make_async_copy(wout_h, wout_s, fetch_sem.at[5])]

    def own(r):
        return pltpu.make_async_copy(mol_h.at[me * rows + r], x_s.at[r, here], m_own.at[r])

    def mol(r, n):
        m, to = near[n]
        return pltpu.make_async_remote_copy(src_ref=mol_h.at[to * rows + r], dst_ref=x_s.at[r, here], send_sem=m_send.at[r, m],
                                            recv_sem=m_recv.at[r, m], device_id=(rows_idx, to), device_id_type=MESH)

    def cot(n):
        m, to = near[n]
        return pltpu.make_async_remote_copy(src_ref=cot_h.at[pl.ds(to * rows, rows)], dst_ref=dy_s.at[:, here],
                                            send_sem=c_send.at[m], recv_sem=c_recv.at[m], device_id=(rows_idx, to),
                                            device_id_type=MESH)

    cot_own = pltpu.make_async_copy(cot_h.at[pl.ds(me * rows, rows)], dy_s.at[:, here], c_own)
    for r in range(rows):
        own(r).start()
    fetch[0].start()
    for n, ref in enumerate((g1_in, b1_in, g2_in, b2_in, db_in, ob_in)):
        six_s[n : n + 1] = ref[...].reshape(1, D)
    ub_s[...] = ub_in[...].reshape(1, FF)
    g1_ref, b1_ref, g2_ref, b2_ref, db_ref, ob_ref = (six_s.at[n : n + 1] for n in range(6))
    ub_ref = ub_s
    pl.semaphore_wait(barrier, len(others))
    for r in range(rows):
        for n in range(len(near)):
            mol(r, n).start()
    for n in range(len(near)):
        cot(n).start()
    fetch[1].start()
    cot_own.start()
    for copy in weights(0, 0):
        copy.start()


    def give_back(which, out, r, n):
        m, to = near[n]
        return pltpu.make_async_remote_copy(
            src_ref=lo_s.at[r, pl.ds(pl.multiple_of(to * local, local), local)], dst_ref=out.at[me * rows + r],
            send_sem=t_send.at[which, r, m], recv_sem=t_recv.at[which, r, m], device_id=(rows_idx, to), device_id_type=MESH)

    def give_self(which, out):
        return pltpu.make_async_copy(lo_s.at[:, pl.ds(pl.multiple_of(me * local, local), local)],
                                     out.at[pl.ds(me * rows, rows)], t_own.at[which])

    def give_wait(which, out):
        give_self(which, out).wait()
        for r in range(rows):
            for n in range(len(near)):
                give_back(which, out, r, n).wait()

    back = [(r, n) for r in range(rows) for n in range(len(near) - 1)]

    tally = Halving(ways[COUNT_WAY], cnt_s.shape[0], cnt_s.shape[1], 8)
    gathers = len(Halving(ways["X"], NB, D, 16).gathers)
    ticks, back_at, late = timetable(nd, gathers, len(tally.gathers))

    def act(kind, j, o, k, which):
        plan = Halving(ways[which], NB, D, 16)
        here = [r.at[j, o] for r in land]
        if kind == 0:
            plan.reduce_step(k, stage_s.at[j % 2, o], here, (rs_send.at[j, o], rs_recv.at[j, o]))
        else:
            plan.gather_step(k, here, sum_out.at[j, o], (ag_send.at[j, o], ag_recv.at[j, o]), keep_sem.at[j, o])

    def act_counts(k):
        if k <= nd:
            tally.reduce_step(k, cnt_s, cland, (crs_send, crs_recv))
        else:
            tally.gather_step(k - nd - 1, cland, cnt_out, (cag_send, cag_recv), ckeep_sem)

    def tick(t, met):
        for kind, most in ((0, nd), (1, gathers)):
            for k in reversed(range(most + 1)):
                for o in range(2):
                    for named in sorted(set(way[o] for way in WAYS)):
                        found = [(ticks.get((kind, j, o, k), -1), j) for j in range(NPAIR) if WAYS[j][o] == named]
                        found = [(at, j) for at, j in found if at in met]
                        assert len({at for at, _ in found}) == len(found)
                        if not found:
                            continue
                        hit = sum(jnp.where(t == at, 1, 0) for at, _ in found)
                        j = sum(jnp.where(t == at, j, 0) for at, j in found)

                        @pl.when(hit == 1)
                        def _():
                            act(kind, j, o, k, named)

        for k in range(nd + 2 + len(tally.gathers)):
            at = ticks.get((2, 0, 0, k), -1)
            if at in met:

                @pl.when(t == at)
                def _():
                    act_counts(k)

        for n, at in enumerate(back_at):
            if at in met:

                @pl.when(t == at)
                def _():
                    give_back(0, lo_out, *back[n]).start()

    half = 2 * local

    def project(r, at):
        src = pl.ds(pl.multiple_of(at, half), half)
        dst = pl.ds(pl.multiple_of(r * length + at, half), half)
        xhat, _ = norm_parts(x_s[r, src].astype(F32))
        a1 = (xhat * g1_ref[...] + b1_ref[...]).astype(BF)
        for c in range(3):
            cols = slice(c * D, (c + 1) * D)
            part = dot_nn(a1, wqkv_s[:, cols])
            qkv_s[dst, cols] = (part if c == 1 else part + qb_ref[c // 2 : c // 2 + 1]).astype(BF)

    for r in range(rows):
        own(r).wait()
        mol(r, len(near) - 1).wait()
    fetch[0].wait()
    mine = (me // 2) * half

    def early(r, carry):
        project(r, mine)
        return carry

    lax.fori_loop(0, rows, early, 0)

    hashes, id_rows, chars = ids_ref.shape
    high = BUCKETS // LANE

    def bucket(h, carry):
        total = jnp.zeros((high, LANE), F32)
        for r in range(id_rows):
            ids = ids_ref[h, r : r + 1, :]
            row = lax.broadcasted_iota(jnp.int32, (high, chars), 0)
            hi = jnp.where(row == (ids >> 7), 1.0, 0.0).astype(BF)
            lo = jnp.where(row == (ids & (LANE - 1)), 1.0, 0.0).astype(BF)
            total = total + dot_nt(hi, lo)
        cnt_s[:, pl.ds(h, 1), :] = total.astype(jnp.int32).reshape(high, 1, LANE)
        return carry

    lax.fori_loop(0, hashes, bucket, 0)
    fetch[1].wait()
    early_counts = [k for k, t in enumerate(COUNT_AT) if t < 0] if nd == len(COUNT_AT) // 2 - 1 else []

    for r in range(rows):
        for n in range(len(near) - 1):
            mol(r, n).wait()
        for other in range(1, nseq // 2):
            project(r, ((me // 2 + other) % (nseq // 2)) * half)
        tok = slice(r * length, (r + 1) * length)

        def pair(p):
            at = pl.multiple_of(p * LANE, LANE)
            q = qkv_s[tok, pl.ds(at, LANE)] * BF(0.125)
            k = qkv_s[tok, pl.ds(pl.multiple_of(D + at, LANE), LANE)]
            v = qkv_s[tok, pl.ds(pl.multiple_of(2 * D + at, LANE), LANE)]
            ctx = []
            lse = lacc[...]
            lane = lax.broadcasted_iota(jnp.int32, lse.shape, 1)
            for half_of in range(2):
                qm = jnp.where(lane_half(q.shape, half_of), q, BF(0))
                s = dot_nt(qm, k)
                m = jnp.max(s, -1, keepdims=True)
                e = jnp.exp(s - m)
                t = jnp.sum(e, -1, keepdims=True)
                pr = (e * (1.0 / t)).astype(BF)
                ctx.append(dot_nn(pr, v))
                lse = jnp.where(lane == 2 * p + half_of, m + jnp.log(t), lse)
            lacc[...] = lse
            ctx_s[tok, pl.ds(at, LANE)] = jnp.where(lane_half(ctx[0].shape, 0), ctx[0], ctx[1]).astype(BF)

        lacc[...] = jnp.zeros_like(lacc)
        def some(i, carry):
            for n in range(TOGETHER):
                pair(TOGETHER * i + n)
            return carry

        ends = (0, 4 // TOGETHER, NH // (2 * TOGETHER))
        for part in range(2):
            lax.fori_loop(ends[part], ends[part + 1], some, 0)
            if 2 * r + part in early_counts:
                act_counts(2 * r + part)
        lt = lacc[...].T
        for h in range(NH):
            lse_s[r * NH + h] = lt[h : h + 1, :]
        mid_s[tok] = x_s[r].astype(F32) + (dot_nn(ctx_s[tok], wout_s[...]) + ob_ref[...])

    step = 256
    pieces = tokens // step

    def piece(n):
        at = pl.ds(pl.multiple_of(n * step, step), step)
        return at, (n * step // length, pl.ds(pl.multiple_of((n * step) % length, step), step))

    def open_piece(n, carry):
        at, _ = piece(n)
        mid = mid_s[at]
        xhat, _ = norm_parts(mid)
        a2 = (xhat * g2_ref[...] + b2_ref[...]).astype(BF)
        a2_s[at] = a2
        a2t_s[:, at] = a2.T
        acc_s[at] = mid + db_ref[...]
        da2_s[at] = jnp.zeros((step, D), F32)
        return carry

    lax.fori_loop(0, pieces, open_piece, 0)
    cot_own.wait()
    for n in range(len(near)):
        cot(n).wait()

    def turn_cotangent(n, carry):
        at, row_at = piece(n)
        dyt_s[:, at] = dy_s[row_at].T
        return carry

    lax.fori_loop(0, pieces, turn_cotangent, 0)

    def ff(i, carry):
        slot = i % 2

        @pl.when(i + 1 < NFF)
        def _():
            for copy in weights(i + 1, 1 - slot):
                copy.start()

        for copy in weights(i, slot):
            copy.wait()
        cols = pl.ds(pl.multiple_of(i * fc, fc), fc)
        u = dot_nn(a2_s[...], wup_s[slot]) + ub_ref[:, cols]
        dh = dot_nt(dy_s[...].reshape(tokens, D), wdn_s[slot])
        cdf = 0.5 + 0.5 * lax.erf(u * (2.0 ** -0.5))
        pdf = jnp.exp(u * u * -0.5) * 0.3989422804014327
        hid = (u * cdf).astype(BF)
        du = (dh * (cdf + u * pdf)).astype(BF)
        gub_s[:, cols] = jnp.sum(du.astype(F32), 0, keepdims=True)
        tick(SPLIT * i, range(0, MID, SPLIT))
        acc_s[...] += dot_nn(hid, wdn_s[slot])
        da2_s[...] += dot_nt(du, wup_s[slot])
        gd = dot_nn(dyt_s[...], hid).astype(BF)
        gu = dot_nn(a2t_s[...], du).astype(BF)
        for b in range(NB):
            stage_s[slot, 0, b] = gd[:, b * LANE : (b + 1) * LANE]
            stage_s[slot, 1, b] = gu[:, b * LANE : (b + 1) * LANE]
        tick(SPLIT * i + SPLIT - 1, range(SPLIT - 1, MID, SPLIT))
        return carry

    lax.fori_loop(0, NFF, ff, 0)

    part_s[...] = jnp.zeros_like(part_s)

    def turn_piece(n, carry):
        at, row_at = piece(n)
        lo_s[row_at] = acc_s[at].astype(BF)
        dy = dy_s[row_at].astype(F32)
        xhat, rstd = norm_parts(mid_s[at])
        da2 = da2_s[at]
        dx2 = dy + norm_back(xhat, rstd, g2_ref[...], da2)
        da2_s[at] = dx2
        do = dx2.astype(BF)
        a2_s[at] = do
        part_s[0:1] += jnp.sum(dy, 0, keepdims=True)
        part_s[1:2] += jnp.sum(da2 * xhat, 0, keepdims=True)
        part_s[2:3] += jnp.sum(da2, 0, keepdims=True)
        part_s[3:4] += jnp.sum(do.astype(F32), 0, keepdims=True)
        dy_s[row_at] = dot_nt(do, wout_s[...]).astype(BF)
        return carry

    lax.fori_loop(0, pieces, turn_piece, 0)
    dctx_s, do_s, dx2_s, da1_s, a1t_s = dy_s, a2_s, da2_s, acc_s, a2t_s
    give_self(0, lo_out).start()
    for r in range(rows):
        give_back(0, lo_out, r, len(near) - 1).start()
    tick(MID, (MID,))
    gout_s = dyt_s
    gout_s[:, 0:D] = dot_tn(ctx_s[...], do_s[...]).astype(BF)

    def first_norm(n, carry):
        at, row_at = piece(n)
        xhat, _ = norm_parts(x_s[row_at].astype(F32))
        a1t_s[:, at] = (xhat * g1_ref[...] + b1_ref[...]).astype(BF).T
        da1_s[at] = jnp.zeros((step, D), F32)
        return carry

    lax.fori_loop(0, pieces, first_norm, 0)
    tick(MID + 1, (MID + 1,))

    def group(g, carry):
        def unit(r, h):
            p = 2 * g + h
            tok = pl.ds(pl.multiple_of(r * length, length), length)
            cq = pl.ds(pl.multiple_of(p * LANE, LANE), LANE)
            q = qkv_s[tok, cq] * BF(0.125)
            k = qkv_s[tok, pl.ds(pl.multiple_of(p * LANE + D, LANE), LANE)]
            v = qkv_s[tok, pl.ds(pl.multiple_of(p * LANE + 2 * D, LANE), LANE)]
            dc = dctx_s[r, :, cq]
            dqs, dks, dvs = [], [], []
            for half in range(2):
                keep = lane_half(k.shape, half)
                km = jnp.where(keep, k, BF(0))
                vm = jnp.where(keep, v, BF(0))
                lse = lse_s[r * NH + 2 * p + half]
                st = dot_nt(km, q)
                pt = jnp.exp(st - lse)
                dpt = dot_nt(vm, dc)
                inner = jnp.sum(pt * dpt, 0, keepdims=True)
                dst = (pt * (dpt - inner)).astype(BF)
                dvs.append(dot_nn(pt.astype(BF), dc))
                dks.append(dot_nn(dst, q))
                dqs.append(dot_tn(dst, k))
            sel = lane_half(dqs[0].shape, 0)
            dqkv_s[tok, pl.ds(pl.multiple_of(h * LANE, LANE), LANE)] = (jnp.where(sel, dqs[0], dqs[1]) * 0.125).astype(BF)
            dqkv_s[tok, pl.ds(pl.multiple_of(h * LANE + 2 * LANE, LANE), LANE)] = jnp.where(sel, dks[0], dks[1]).astype(BF)
            dqkv_s[tok, pl.ds(pl.multiple_of(h * LANE + 4 * LANE, LANE), LANE)] = jnp.where(sel, dvs[0], dvs[1]).astype(BF)

        def both_halves(n, inner_carry):
            unit(n, 0)
            unit(n, 1)
            for late_tick in range(2):
                first = MID + 2 + late_tick
                tick(first + 5 * g + 2 * n, [first + 5 * a + 2 * b for a in range(3) for b in range(2)])
            return inner_carry

        lax.fori_loop(0, rows, both_halves, 0)
        slot = (NFF + g) % 2
        grads = dot_nn(a1t_s[...], dqkv_s[...]).astype(BF)
        for b in range(6):
            stage_s[slot, b // NB, b % NB] = grads[:, b * LANE : (b + 1) * LANE]
        for b in range(2):
            stage_s[slot, 1, 2 + b] = gout_s[:, pl.ds(pl.multiple_of((2 * g + b) * LANE, LANE), LANE)]
        two = 2 * LANE
        for c in range(3):
            at = pl.ds(pl.multiple_of(c * D + g * two, two), two)
            da1_s[...] += dot_nt(dqkv_s[:, c * two : (c + 1) * two], wqkv_s[:, at])
        here = pl.ds(pl.multiple_of(g * two, two), two)
        part_s[6:7, here] = jnp.sum(dqkv_s[:, 0:two].astype(F32), 0, keepdims=True)
        part_s[7:8, here] = jnp.sum(dqkv_s[:, 2 * two : 3 * two].astype(F32), 0, keepdims=True)
        tick(MID + 6 + 5 * g, range(MID + 6, DRAIN, 5))
        return carry

    lax.fori_loop(0, 3, group, 0)

    give_wait(0, lo_out)

    def last_piece(n, carry):
        at, row_at = piece(n)
        xhat, rstd = norm_parts(x_s[row_at].astype(F32))
        da1 = da1_s[at]
        part_s[4:5] += jnp.sum(da1 * xhat, 0, keepdims=True)
        part_s[5:6] += jnp.sum(da1, 0, keepdims=True)
        gm = dx2_s[at] + norm_back(xhat, rstd, g1_ref[...], da1)
        lo_s[row_at] = gm.astype(BF)
        return carry

    lax.fori_loop(0, pieces, last_piece, 0)
    give_self(1, gm_out).start()
    for r in range(rows):
        give_back(1, gm_out, r, len(near) - 1).start()
    vacc_s[0, 0:8] = part_s[...]
    for b in range(FF // (2 * LANE)):
        vacc_s[0, 8 + b // 3 : 9 + b // 3, (b % 3) * 2 * LANE : (b % 3 + 1) * 2 * LANE] = gub_s[:, b * 2 * LANE : (b + 1) * 2 * LANE]
    vacc_s[0, 12:16] = jnp.zeros((4, D), F32)

    def swap(i):
        return pltpu.make_async_remote_copy(src_ref=vacc_s.at[i], dst_ref=vland_s.at[i], send_sem=v_send.at[i], recv_sem=v_recv.at[i],
                                            device_id=across(ways["X"][i]), device_id_type=MESH)

    for kind, j, o, k in late:
        if kind < 2:
            act(kind, j, o, k, WAYS[j][o])
        elif kind == 2:
            act_counts(k)
        elif kind == 4:
            give_back(1, gm_out, *back[k]).start()
        else:
            if k > 0:
                swap(k - 1).wait()
                vacc_s[k] = vacc_s[k - 1] + vland_s[k - 1]
            if k < nd:
                swap(k).start()
    vec_out[...] = vacc_s[nd]
    give_wait(1, gm_out)


def layer(shape, mol, cot, wup, wdn, wqkv, wout, ids, g1, b1, qb, ob, g2, b2, ub, db):
    nseq = shape["seq"]
    local = mol.shape[1]
    rows, length = mol.shape[0] // nseq, local * nseq
    tokens = rows * length
    nd = len(orders(shape)["X"])
    vm, hb = pl.BlockSpec(memory_space=pltpu.VMEM), pl.BlockSpec(memory_space=pl.ANY)
    dma = pltpu.SemaphoreType.DMA
    V = pltpu.VMEM
    sds = jax.ShapeDtypeStruct
    fc = NB * LANE
    cnt = (BUCKETS // LANE, ids.shape[0], LANE)
    scratch = [
        V((tokens, D), F32), V((rows, length, D), BF), V((tokens, D), BF), V((D, tokens), BF), V((D, tokens), BF), V((tokens, D), F32),
        V((tokens, D), F32), V((2, D, fc), BF), V((2, fc, D), BF), V((tokens, 3 * D), BF), V((tokens, D), BF), V((rows, length, D), BF),
        V((D, 3 * D), BF), V((D, D), BF), V((tokens, D), BF), V((rows, length, D), BF),
        V((1, FF), F32), V((8, D), F32), dma((6,)), V((2, 2, NB, D, LANE), BF), V((nd, 16, D), F32), V((nd + 1, 16, D), F32),
        V((8, D), F32), V((1, FF), F32), V((length, LANE), F32), V((rows * NH, 1, length), F32), V(cnt, jnp.int32),
        dma((NPAIR, 2, nd)), dma((NPAIR, 2, nd)), dma((NPAIR, 2, nd)), dma((NPAIR, 2, nd)), dma((NPAIR, 2)),
        dma((nd,)), dma((nd,)), dma((nd,)), dma((nd,)), dma, dma((nd,)), dma((nd,)), dma((2, rows, nseq)), dma((2, rows, nseq)), dma((2,)),
        dma((rows, nseq)), dma((rows, nseq)), dma((rows,)), dma((nseq,)), dma((nseq,)), dma,
    ]
    scratch += land_shapes((NPAIR, 2), NB, D, 16, nd, BF)
    scratch += land_shapes((), cnt[0], cnt[1], 8, nd, jnp.int32)
    return pl.pallas_call(
        functools.partial(layer_kernel, shape),
        in_specs=[hb] * 6 + [vm] * 9,
        out_specs=[hb, hb, hb, hb, vm],
        out_shape=[sds((rows * nseq, local, D), BF), sds((rows * nseq, local, D), BF), sds((NPAIR, 2, NB, D, LANE), BF),
                   sds(cnt, jnp.int32), sds((16, D), F32)],
        scratch_shapes=scratch,
        compiler_params=pltpu.CompilerParams(vmem_limit_bytes=63 * MIB, collective_id=0, has_side_effects=True),
        name="layer",
    )(mol, cot, wup, wdn, wqkv, wout, ids, g1, b1, qb, ob, g2, b2, ub, db)


def widen_kernel(src_ref, gm_ref, lo_ref, vec_ref, cnt_ref, gmol_ref, lout_ref, counts_ref, g1_ref, b1_ref, qb_ref, ob_ref, g2_ref,
                 b2_ref, ub_ref, db_ref, qkv_out, out_out, up_out, down_out, wide_s, tall_s, sem):
    j = pl.program_id(0)
    slot = j % 2
    fc = NB * LANE
    two = 2 * LANE

    def first(i, s):
        at = pl.ds(pl.multiple_of(i * fc, fc), fc)
        return [pltpu.make_async_copy(tall_s.at[s], down_out.at[at], sem.at[s, 0]),
                pltpu.make_async_copy(wide_s.at[s, 0], up_out.at[:, at], sem.at[s, 1])]

    def later(i, s):
        g = i - NFF
        to = lambda c: pl.ds(pl.multiple_of(c * D + g * two, two), two)
        return [pltpu.make_async_copy(wide_s.at[s, 0, :, 0:two], qkv_out.at[:, to(0)], sem.at[s, 0]),
                pltpu.make_async_copy(wide_s.at[s, 0, :, two : 2 * two], qkv_out.at[:, to(1)], sem.at[s, 1]),
                pltpu.make_async_copy(wide_s.at[s, 1, :, 0:two], qkv_out.at[:, to(2)], sem.at[s, 2]),
                pltpu.make_async_copy(wide_s.at[s, 1, :, two : 2 * two], out_out.at[:, to(0)], sem.at[s, 3])]

    def finish(i, s):
        @pl.when(i < NFF)
        def _():
            for copy in first(i, s):
                copy.wait()

        @pl.when(i >= NFF)
        def _():
            for copy in later(i, s):
                copy.wait()

    @pl.when(j >= 2)
    def _():
        finish(j - 2, slot)

    gmol_ref[...] = gm_ref[...].astype(F32)
    lout_ref[...] = lo_ref[...]

    @pl.when(j == 0)
    def _():
        for n, ref in ((0, db_ref), (1, g2_ref), (2, b2_ref), (3, ob_ref), (4, g1_ref), (5, b1_ref)):
            ref[...] = vec_ref[n : n + 1].reshape(D)
        qb_ref[...] = vec_ref[6:8]
        ub_ref[...] = jnp.concatenate([vec_ref[n : n + 1] for n in range(8, 12)], 1).reshape(FF)
        for n in range(cnt_ref.shape[0]):
            counts_ref[:, n * LANE : (n + 1) * LANE] = cnt_ref[n]

    @pl.when(j < NFF)
    def _():
        for b in range(NB):
            at = slice(b * LANE, (b + 1) * LANE)
            tall_s[slot, at, :] = src_ref[0, 0, b].astype(F32).T
            wide_s[slot, 0, :, at] = src_ref[0, 1, b].astype(F32)
        for copy in first(j, slot):
            copy.start()

    @pl.when(j >= NFF)
    def _():
        for o in range(2):
            for b in range(NB):
                wide_s[slot, o, :, b * LANE : (b + 1) * LANE] = src_ref[0, o, b].astype(F32)
        for copy in later(j, slot):
            copy.start()

    @pl.when(j == NPAIR - 1)
    def _():
        finish(j - 1, 1 - slot)
        finish(j, slot)


def widen(sums, gm, lo, vec, cnt):
    hb = pl.BlockSpec(memory_space=pl.ANY)
    vm = pl.BlockSpec(memory_space=pltpu.VMEM)
    sds = jax.ShapeDtypeStruct
    one = sds((D,), F32)
    rows = gm.shape[0]
    some = pl.BlockSpec((1,) + gm.shape[1:], lambda j: (jnp.minimum(j, rows - 1), 0, 0))
    return pl.pallas_call(
        widen_kernel,
        grid=(NPAIR,),
        in_specs=[pl.BlockSpec((1, 2, NB, D, LANE), lambda j: (j, 0, 0, 0, 0)), some, some, vm, vm],
        out_specs=[some, some] + [vm] * 9 + [hb] * 4,
        out_shape=[sds(gm.shape, F32), sds(lo.shape, BF), sds((cnt.shape[1], BUCKETS), jnp.int32), one, one, sds((2, D), F32), one, one,
                   one, sds((FF,), F32), one, sds((D, 3 * D), F32), sds((D, D), F32), sds((D, FF), F32), sds((FF, D), F32)],
        scratch_shapes=[pltpu.VMEM((2, 2, D, NB * LANE), F32), pltpu.VMEM((2, NB * LANE, D), F32), pltpu.SemaphoreType.DMA((2, 4))],
        compiler_params=pltpu.CompilerParams(vmem_limit_bytes=60 * MIB),
        name="widen",
    )(sums, gm, lo, vec, cnt)


def on_device(shape, molecules, ln1_gain, ln1_bias, w_qkv, qkv_bias, w_out, out_bias, ln2_gain, ln2_bias, w_up, up_bias,
              w_down, down_bias, out_cotangent, bucket_ids):
    layer_out, gm, sums, counts, vec = layer(shape, molecules, out_cotangent, w_up, w_down, w_qkv, w_out, bucket_ids, ln1_gain, ln1_bias,
                                             qkv_bias, out_bias, ln2_gain, ln2_bias, up_bias, down_bias)
    (g_mol, layer_out, counts, g_g1, g_b1, g_qb, g_ob, g_g2, g_b2, g_ub, g_db, g_qkv, g_out, g_up,
     g_down) = widen(sums, gm, layer_out, vec, counts)
    return (layer_out, g_mol, g_g1, g_b1, g_qkv, g_qb, g_out, g_ob, g_g2, g_b2, g_up, g_ub, g_down, g_db, counts)


def solution(mesh):
    tok = P("rows", "seq", None)
    return jax.shard_map(
        functools.partial(on_device, dict(mesh.shape)),
        mesh=mesh,
        in_specs=(tok,) + (P(),) * 12 + (tok, P(None, "rows", "seq")),
        out_specs=(tok, tok) + (P(),) * 13,
        check_vma=False,
    )
```
